128 devices in a mesh: section: 16 (over x, z), tp: 8 (over y, core).
Axes of the slice: x: 4, y: 4, z: 4, core: 2. Of those that a mesh axis runs over, the one named last changes fastest.
Arguments:
- tokens: bfloat16 [8192, 8192], P('section'), may hold values from -6 to 6
- gain: float32 [8192], replicated, may hold values from 0.5 to 1.5
- q_weight: bfloat16 [8192, 4096], P(None, 'tp'), may hold values from -0.0625 to 0.0625
- q_bias: float32 [4096], P('tp'), may hold values from -14 to 14
- kv_weight: bfloat16 [8192, 2048], P(None, 'tp'), may hold values from -0.0625 to 0.0625
- kv_bias: float32 [2048], P('tp'), may hold values from -14 to 14
- out_weight: bfloat16 [4096, 8192], P('tp'), may hold values from -0.09375 to 0.09375
- placement: int32 [512, 1], replicated, may hold values from 0 to 15; in each aligned block of 32 rows (0 to 31, 32 to 63, ...) at most 4 rows name the same one
Outputs:
- mixed: bfloat16 [8192, 8192], P('section', 'tp')
- decode_cache: bfloat16 [1024, 16, 2048], P('section', None, 'tp')
The draws below stay inside these ranges and needn't reach their ends.
Inputs may be any that keep to these rules, and one draw needn't show every extreme that they name: `placement`: within the 32 blocks of one stretch no owner is named more than 4 times.
All inputs are finite; a program needn't handle non-finite values.
Results may differ from the reference program's by a relative error of at most 0.014.
The reference program's roundings to bfloat16 on the way (of `normed`, `queries`, `cache_rows` and `attended`) count: a program that leaves them out, or rounds other values in their place, can miss the bound.
Values may be sent and summed in bfloat16 or wider, within the bound.
No kernel may reach another device: no remote copies, remote signals or barrier semaphores. Data moves between devices by JAX's collectives and lax.ppermute only.
A program may use at most 256 MiB of HBM per device.

```python
import math
import jax
import jax.numpy as jnp
import numpy as np
from jax import lax

D = 8192
HEADS = 32
KVH = 8
HD = 128
BLOCK = 16
TOKENS = 8192
BLK_DEV = 32
NBLK = 512
PAIR = 4
SLOTS = 64
N_SECTION = 16
N_TP = 8


def draw_q_bias(key, part):
    key = jax.random.fold_in(key, 11)
    first = jax.random.fold_in(key, 0)
    base = jnp.clip(jax.random.normal(first, (HEADS, HD), jnp.float32) * 0.5, -3.0, 3.0)
    return base.reshape(HEADS * HD)


def draw_kv_bias(key, part):
    key = jax.random.fold_in(key, 12)
    base = jnp.clip(jax.random.normal(key, (KVH, 2, HD), jnp.float32) * 0.5, -3.0, 3.0)
    return base.reshape(2 * KVH * HD)


def block_scale(rng, shape, cuts, low, high):
    factor_of, own = 1.0, jax.random.fold_in(rng, 6)
    for dim, shards_of in cuts:
        draws = jnp.exp(jax.random.uniform(jax.random.fold_in(own, dim), (shards_of,), jnp.float32, low / len(cuts), high / len(cuts)))
        factor_of = factor_of * jnp.repeat(draws, shape[dim] // shards_of).reshape([-1 if axis == dim else 1 for axis in range(len(shape))])
    return factor_of


def routed_block(key, own, number, rows, count, top, bound, lean):
    ranking = jax.random.permutation(key, count)
    crowded, usual = portions_of(count, rows * top, bound, lean, True), portions_of(count, rows * top, bound, lean, False)
    places = jnp.arange(count)

    def named(sizes, offset_by):
        used = int((sizes > 0).sum())
        fixed = max(1, used // 4)
        passed = fixed + (places - fixed + offset_by * (used - fixed)) % max(1, count - fixed)
        return jnp.zeros((count,), jnp.int32).at[ranking[jnp.where(places < fixed, places, passed)]].set(jnp.asarray(sizes, jnp.int32))

    sizes = jnp.where(number % 4 == 0, named(crowded, number // 4), named(usual, number - number // 4 - 1))
    mixed = jax.random.permutation(jax.random.fold_in(own, 3), count)
    giver, sink = mixed[0:count // 2 * 2:2], mixed[1:count // 2 * 2:2]
    slack = jnp.minimum(sizes[giver] - 1, bound - sizes[sink]) // 2
    slack = jnp.where((giver == ranking[0]) | (sink == ranking[0]) | (sizes[sink] == 0), 0, jnp.maximum(slack, 0))
    passed = jax.random.randint(jax.random.fold_in(own, 4), (count // 2,), 0, 1 << 20) % (slack + 1)
    sizes = sizes.at[giver].add(-passed).at[sink].add(passed)
    labels = jnp.searchsorted(jnp.cumsum(sizes), jnp.arange(rows * top), side="right").astype(jnp.int32)
    listing = labels.reshape(top, rows).T
    listing = listing[jax.random.permutation(jax.random.fold_in(own, 1), rows)]
    offset_by = jax.random.randint(jax.random.fold_in(own, 2), (rows, 1), 0, top)
    return jnp.take_along_axis(listing, (jnp.arange(top)[None, :] + offset_by) % top, axis=1)


def portions_of(number_of, total, reach, skew, full):
    portions = [(1 << 20) // math.isqrt(rank ** skew) + 1 for rank in range(1, number_of + 1)]
    largest = reach if full else min(reach, max(-(-total // number_of), total * portions[0] // sum(portions)))
    least = 1 if total - largest >= number_of - 1 else 0
    counts, surplus = [largest] + [least] * (number_of - 1), total - largest - least * (number_of - 1)
    while surplus > 0:
        candidates = [i for i in range(1, number_of) if counts[i] < largest] or [i for i in range(1, number_of) if counts[i] < reach]
        mass, left = sum([portions[i] for i in candidates]), surplus
        for i in candidates:
            extra = min(reach - counts[i], max(1, left * portions[i] // mass), surplus)
            counts[i] = counts[i] + extra
            surplus = surplus - extra
    return np.array(counts)


def bell_draw(own_key, shape, scale, limit, pieces=(), kind=jnp.bfloat16):
    entries = scale * jax.random.normal(own_key, shape, jnp.float32)
    if pieces:
        entries = entries * block_scale(own_key, shape, pieces, -0.22, 0.18)
    return jnp.clip(entries, -limit, limit).astype(kind)


def setup_inputs(seed: int = 0) -> dict:
    splits = jax.random.split(jax.random.key(seed), 9)
    tokens = bell_draw(splits[0], (TOKENS, D), 1.0, 6.0, ((0, 16),))
    gain = jnp.clip(1.0 + 0.1 * jax.random.normal(splits[1], (D,), jnp.float32), 0.5, 1.5)
    q_weight = bell_draw(splits[2], (D, HEADS * HD), D ** -0.5, 0.0625, ((1, 8),))
    q_bias = draw_q_bias(jax.random.fold_in(splits[8], 71), 0)
    kv_weight = bell_draw(splits[4], (D, 2 * KVH * HD), D ** -0.5, 0.0625, ((1, 8),))
    kv_bias = draw_kv_bias(jax.random.fold_in(splits[8], 71), 0)
    out_weight = bell_draw(splits[6], (HEADS * HD, D), (HEADS * HD) ** -0.5, 0.09375, ((0, 8),))
    placement_keys = jax.random.split(jax.random.fold_in(splits[7], 1), NBLK // BLK_DEV)
    placement_turns = jax.random.permutation(jax.random.fold_in(splits[7], 3), NBLK // BLK_DEV)
    placement = jax.vmap(lambda own, number: routed_block(jax.random.fold_in(splits[7], 2), own, number, BLK_DEV, N_SECTION, 1, PAIR, 2))(placement_keys, placement_turns).reshape((NBLK, 1))
    return dict(tokens=tokens, gain=gain, q_weight=q_weight, q_bias=q_bias, kv_weight=kv_weight, kv_bias=kv_bias, out_weight=out_weight, placement=placement)


ROPE_BASE = 1000000.0

def rotate(values, positions):
    half = values.shape[-1] // 2
    freq = ROPE_BASE ** (-(jnp.arange(half, dtype=jnp.float32) * 2.0 / values.shape[-1]))
    angle = positions[:, None] * freq[None, :]
    cosine = jnp.cos(angle)[:, None, :]
    sine = jnp.sin(angle)[:, None, :]
    first = values[..., :half]
    second = values[..., half:]
    return jnp.concatenate([first * cosine - second * sine, second * cosine + first * sine], -1)

def reround(values):
    return lax.optimization_barrier(values.astype(jnp.bfloat16)).astype(jnp.float32)

def reference(tokens, gain, q_weight, q_bias, kv_weight, kv_bias, out_weight, placement):
    wide = tokens.astype(jnp.float32)
    meansq = lax.optimization_barrier(jnp.mean(wide * wide, axis=-1, keepdims=True))
    normed = (wide * lax.rsqrt(meansq + 1e-06) * gain).astype(jnp.bfloat16)
    positions = jnp.arange(TOKENS).astype(jnp.float32)
    queries = (jnp.dot(normed, q_weight, preferred_element_type=jnp.float32) + q_bias).reshape(TOKENS, HEADS, HD)
    queries = rotate(queries, positions).astype(jnp.bfloat16)
    pairs = (jnp.dot(normed, kv_weight, preferred_element_type=jnp.float32) + kv_bias).reshape(TOKENS, KVH, 2, HD)
    keys = rotate(pairs[:, :, 0], positions)
    cache_rows = jnp.stack([keys, pairs[:, :, 1]], 2).astype(jnp.bfloat16)
    group = HEADS // KVH
    grouped = jnp.transpose(queries.reshape(TOKENS, KVH, group, HD), (1, 0, 2, 3))
    key_heads = jnp.transpose(cache_rows[:, :, 0], (1, 0, 2))
    value_heads = jnp.transpose(cache_rows[:, :, 1], (1, 0, 2))
    causal = jnp.arange(TOKENS)[:, None] >= jnp.arange(TOKENS)[None, :]
    scale = HD ** (-0.5)

    def one_head(inputs):
        query_g, key_g, value_g = inputs
        scores = jnp.einsum('qhd,kd->hqk', query_g.astype(jnp.float32), key_g.astype(jnp.float32)) * scale
        scores = jnp.where(causal[None], scores, -1e+30)
        highest = lax.optimization_barrier(jnp.max(scores, axis=-1, keepdims=True))
        weights = jnp.where(causal[None], jnp.exp(scores - highest), 0.0)
        totals = lax.optimization_barrier(jnp.sum(weights, axis=-1))
        summed = jnp.einsum('hqk,kd->qhd', reround(weights), value_g.astype(jnp.float32))
        return summed / jnp.transpose(totals)[:, :, None]
    attended = lax.map(one_head, (grouped, key_heads, value_heads))
    attended = jnp.transpose(attended, (1, 0, 2, 3)).reshape(TOKENS, HEADS * HD).astype(jnp.bfloat16)
    width = HEADS * HD // N_TP
    total = jnp.zeros((TOKENS, D), jnp.float32)
    for shard in range(N_TP):
        term = jnp.dot(attended[:, shard * width:(shard + 1) * width], out_weight[shard * width:(shard + 1) * width], preferred_element_type=jnp.float32)
        total = total + reround(term)
    mixed = (wide + total).astype(jnp.bfloat16)
    blocks = cache_rows.reshape(NBLK, BLOCK, 2 * KVH * HD)
    owners = placement[:, 0].astype(jnp.int32)
    grid = owners.reshape(N_SECTION, BLK_DEV)
    same = grid[:, :, None] == grid[:, None, :]
    before = jnp.arange(BLK_DEV)[:, None] < jnp.arange(BLK_DEV)[None, :]
    ranks = lax.optimization_barrier(jnp.sum((same & before[None]).astype(jnp.int32), axis=1)).reshape(NBLK)
    stretches = (jnp.arange(NBLK) // BLK_DEV).astype(jnp.int32)
    slots = (owners * SLOTS + stretches * PAIR + ranks).astype(jnp.int32)
    decode_cache = jnp.zeros((N_SECTION * SLOTS, BLOCK, 2 * KVH * HD), jnp.bfloat16).at[slots].set(blocks)
    return (mixed, decode_cache)
```

```python
import functools
import math

import jax
import jax.numpy as jnp
import numpy as np
from jax import lax
from jax.experimental import pallas as pl
from jax.experimental.pallas import tpu as pltpu
from jax.sharding import PartitionSpec as P

HD = 128
BLOCK = 16
SIDE = 4
HALF = 256
ROWS = 512
D = 8192
HEADS = 4
PAIR = 4
ROPE_BASE = 1000000.0
LOG2_SCALE = math.log2(math.e) / math.sqrt(HD)
VMEM = pltpu.CompilerParams(vmem_limit_bytes=56 * 1024 * 1024)
BF = jnp.bfloat16
F32 = jnp.float32
ANY = pl.BlockSpec(memory_space=pl.ANY)
WHOLE = pl.BlockSpec(memory_space=pltpu.VMEM)


def tables():
    freq = ROPE_BASE ** (-(np.arange(HD // 2, dtype=np.float64) * 2.0 / HD))
    inner = np.arange(ROWS, dtype=np.float64)[:, None] * freq
    outer = ROWS * np.arange(SIDE * SIDE, dtype=np.float64)[:, None] * freq
    twice = lambda a: np.concatenate([a, a], -1)
    signed = lambda a: np.concatenate([-a, a], -1)
    small = np.concatenate([twice(np.cos(inner)), twice(np.sin(inner))], -1)
    large = np.concatenate(
        [twice(np.cos(outer)), twice(np.sin(outer)), signed(np.cos(outer)), signed(np.sin(outer))], -1
    )
    return small.astype(np.float32), large.astype(np.float32)


def angles(small, large):
    cos_r, sin_r = small[:, :HD], small[:, HD:]
    cos_s, sin_s = large[:, :HD], large[:, HD : 2 * HD]
    cos_g, sin_g = large[:, 2 * HD : 3 * HD], large[:, 3 * HD :]
    return cos_s * cos_r - sin_s * sin_r, sin_g * cos_r + cos_g * sin_r


def turn(value, cosine, sine):
    return value * cosine + pltpu.roll(value, HD // 2, 1) * sine


NORM_ROWS = 128


def norm_kv_kernel(tokens, gain, weight, bias, small, large, normed, first, second):
    step = pl.program_id(0)

    def rows_of(i, _):
        rows = pl.ds(pl.multiple_of(i * 32, 32), 32)
        total = jnp.zeros((32, 128), F32)
        for c in range(0, D, 1024):
            wide = tokens[rows, c : c + 1024].astype(F32)
            square = wide * wide
            for k in range(0, 1024, 128):
                total = total + square[:, k : k + 128]
        meansq = jnp.sum(total, axis=1, keepdims=True) * (1.0 / D)
        factor = lax.rsqrt(meansq + 1e-06)
        for c in range(0, D, 1024):
            wide = tokens[rows, c : c + 1024].astype(F32)
            normed[rows, c : c + 1024] = (wide * factor * gain[:, c : c + 1024]).astype(BF)
        return 0

    lax.fori_loop(0, NORM_ROWS // 32, rows_of, 0)
    product = jnp.dot(normed[...], weight[...], preferred_element_type=F32) + bias[...]
    section = lax.axis_index("section")
    cosine, sine = angles(small[...], large[pl.ds(section, 1), :])
    keys = turn(product[:, :HD], cosine, sine).astype(BF)
    values = product[:, HD:].astype(BF)

    @pl.when(step < 2)
    def _():
        first[:, :HD] = keys
        first[:, HD:] = values

    @pl.when(step >= 2)
    def _():
        second[:, :HD] = keys
        second[:, HD:] = values


def norm_kv(tokens, gain, weight, bias, small, large):
    half = jax.ShapeDtypeStruct((HALF, 2 * HD), BF)
    return pl.pallas_call(
        norm_kv_kernel,
        grid=(ROWS // NORM_ROWS,),
        in_specs=[
            pl.BlockSpec((NORM_ROWS, D), lambda i: (i, 0)),
            pl.BlockSpec((1, D), lambda i: (0, 0)),
            pl.BlockSpec((D, 2 * HD), lambda i: (0, 0)),
            pl.BlockSpec((1, 2 * HD), lambda i: (0, 0)),
            pl.BlockSpec((NORM_ROWS, 2 * HD), lambda i: (i, 0)),
            pl.BlockSpec((SIDE * SIDE, 4 * HD), lambda i: (0, 0)),
        ],
        out_specs=[
            pl.BlockSpec((NORM_ROWS, D), lambda i: (i, 0)),
            pl.BlockSpec((NORM_ROWS, 2 * HD), lambda i: (jnp.minimum(i, 1), 0)),
            pl.BlockSpec((NORM_ROWS, 2 * HD), lambda i: (jnp.maximum(i - 2, 0), 0)),
        ],
        out_shape=[jax.ShapeDtypeStruct((ROWS, D), BF), half, half],
        compiler_params=VMEM,
        cost_estimate=pl.CostEstimate(flops=2 * ROWS * D * 256, bytes_accessed=20 << 20, transcendentals=0),
        name="norm_kv",
    )(tokens, gain, weight, bias, small, large)


Q_DEPTH = 1024


def query_kernel(normed, weight, bias, small, large, out, total):
    step = pl.program_id(0)
    product = jnp.dot(normed[...], weight[...], preferred_element_type=F32)

    @pl.when(step == 0)
    def _():
        total[...] = product

    @pl.when(step > 0)
    def _():
        total[...] += product

    @pl.when(step == pl.num_programs(0) - 1)
    def _():
        cosine, sine = angles(small[...], large[pl.ds(lax.axis_index("section"), 1), :])
        for h in range(HEADS):
            columns = slice(h * HD, (h + 1) * HD)
            value = total[:, columns] + bias[:, columns]
            out[h * ROWS : (h + 1) * ROWS, :] = turn(value, cosine, sine).astype(BF)


def query(normed, weight, bias, small, large):
    width = HEADS * HD
    return pl.pallas_call(
        query_kernel,
        grid=(D // Q_DEPTH,),
        in_specs=[
            pl.BlockSpec((ROWS, Q_DEPTH), lambda i: (0, i)),
            pl.BlockSpec((Q_DEPTH, width), lambda i: (i, 0)),
            pl.BlockSpec((1, width), lambda i: (0, 0)),
            pl.BlockSpec((ROWS, 2 * HD), lambda i: (0, 0)),
            pl.BlockSpec((SIDE * SIDE, 4 * HD), lambda i: (0, 0)),
        ],
        out_specs=pl.BlockSpec((HEADS * ROWS, HD), lambda i: (0, 0)),
        out_shape=jax.ShapeDtypeStruct((HEADS * ROWS, HD), BF),
        scratch_shapes=[pltpu.VMEM((ROWS, width), F32)],
        compiler_params=VMEM,
        cost_estimate=pl.CostEstimate(flops=2 * ROWS * D * 512, bytes_accessed=16 << 20, transcendentals=0),
        name="query",
    )(normed, weight, bias, small, large)


TILE = 128
QROWS = HEADS * ROWS


def attend(queries, keys, values, acc, maxima, rows, mask=None, first=False):
    scores = lax.dot_general(queries, keys, (((1,), (1,)), ((), ())), preferred_element_type=F32)
    if mask is not None:
        scores = jnp.where(mask, scores, -1e30)
    highest = jnp.max(scores, axis=1, keepdims=True)
    if first:
        newest = jnp.broadcast_to(highest, (rows.size, HD))
    else:
        old = maxima[rows, :]
        newest = jnp.maximum(old, highest)
        rescale = jnp.exp2((old - newest) * LOG2_SCALE)
    maxima[rows, :] = newest
    weights = jnp.exp2(scores * LOG2_SCALE - newest[:, :1] * LOG2_SCALE).astype(BF)
    added = jnp.dot(weights, values, preferred_element_type=F32)
    if first:
        acc[rows, :] = added
    else:
        acc[rows, :HD] = acc[rows, :HD] * rescale + added[:, :HD]
        acc[rows, HD:] = acc[rows, HD:] * rescale + added[:, HD:]


def attend_kernel(plan, diagonal, final, *refs):
    refs = list(refs)
    take = lambda n: [refs.pop(0) for _ in range(n)]
    (queries,) = take(1)
    own = take(2) if diagonal else []
    old = [] if diagonal else take(2)
    pieces = take(len(plan))
    outs = take(1 if final else 2)
    keys, values, *rest = refs
    if final:
        acc, maxima, sems = rest
    else:
        (sems,) = rest
        acc, maxima = outs
    section = lax.axis_index("section")
    x, z = section // SIDE, section % SIDE
    count = jnp.int32(0)
    jobs = []
    for piece, offsets in zip(pieces, plan):
        for j, (dx, dz) in enumerate(offsets):
            source = lax.rem(x + dx, SIDE) * SIDE + lax.rem(z + dz, SIDE)
            needed = source < section
            here = pl.ds(j * HALF, HALF)
            there = pl.ds(pl.multiple_of(count * HALF, HALF), HALF)
            n = len(jobs)
            copies = (
                pltpu.make_async_copy(piece.at[here, :HD], keys.at[there, :], sems.at[n, 0]),
                pltpu.make_async_copy(piece.at[here, HD:], values.at[there, :HD], sems.at[n, 1]),
            )

            @pl.when(needed)
            def _():
                copies[0].start()
                copies[1].start()

            jobs.append((needed, copies))
            count = count + needed.astype(jnp.int32)
    values[:, HD:] = jnp.ones((values.shape[0], HD), BF)
    if diagonal:
        def head(h, _):
            for start in range(0, ROWS, TILE):
                rows = pl.ds(pl.multiple_of(h * ROWS + start, TILE), TILE)
                stop = start + TILE
                low, high = min(stop, HALF), max(stop - HALF, 0)
                ones = jnp.ones((stop, HD), BF)
                kd, vd = own[0][:low, :HD], own[0][:low, HD:]
                if high:
                    kd = jnp.concatenate([kd, own[1][:high, :HD]], 0)
                    vd = jnp.concatenate([vd, own[1][:high, HD:]], 0)
                vd = jnp.concatenate([vd, ones], 1)
                shape = (TILE, stop)
                mask = lax.broadcasted_iota(jnp.int32, shape, 1) <= start + lax.broadcasted_iota(
                    jnp.int32, shape, 0
                )
                attend(queries[rows, :], kd, vd, acc, maxima, rows, mask, True)
            return 0

        lax.fori_loop(0, HEADS, head, 0)
    else:
        acc[...] = old[0][...]
        maxima[...] = old[1][...]
    for needed, copies in jobs:
        @pl.when(needed)
        def _():
            copies[0].wait()
            copies[1].wait()

    def part(base, size):
        at = pl.ds(pl.multiple_of(base, HALF), size)
        kd, vd = keys[at, :], values[at, :]
        for start in range(0, QROWS, TILE):
            rows = pl.ds(start, TILE)
            attend(queries[rows, :], kd, vd, acc, maxima, rows)

    def whole(i, _):
        part(i * 4 * HALF, 4 * HALF)
        return 0

    lax.fori_loop(0, count // 4, whole, 0)
    left = lax.rem(count, 4)

    @pl.when(left >= 2)
    def _():
        part((count // 4) * 4 * HALF, 2 * HALF)

    @pl.when(lax.rem(left, 2) == 1)
    def _():
        part((count - 1) * HALF, HALF)

    if final:
        for h in range(HEADS):
            rows = slice(h * ROWS, (h + 1) * ROWS)
            outs[0][:, h * HD : (h + 1) * HD] = (acc[rows, :HD] / acc[rows, HD:]).astype(BF)


def attention(queries, own, state, pieces, plan, final, name):
    subs = sum(len(p) for p in plan)
    diagonal = state is None
    state_shape = [jax.ShapeDtypeStruct((QROWS, 2 * HD), F32), jax.ShapeDtypeStruct((QROWS, HD), F32)]
    scratch = [pltpu.VMEM((subs * HALF, HD), BF), pltpu.VMEM((subs * HALF, 2 * HD), BF)]
    if final:
        scratch += [pltpu.VMEM(s.shape, s.dtype) for s in state_shape]
        out_shape = [jax.ShapeDtypeStruct((ROWS, HEADS * HD), BF)]
    else:
        out_shape = state_shape
    scratch.append(pltpu.SemaphoreType.DMA((subs, 2)))
    start = list(own) if diagonal else list(state)
    return pl.pallas_call(
        functools.partial(attend_kernel, plan, diagonal, final),
        in_specs=[WHOLE] * (1 + len(start)) + [ANY] * len(pieces),
        out_specs=[WHOLE] * len(out_shape),
        out_shape=out_shape,
        scratch_shapes=scratch,
        compiler_params=VMEM,
        cost_estimate=pl.CostEstimate(
            flops=4 * QROWS * HALF * (subs + diagonal) * HD,
            bytes_accessed=8 << 20,
            transcendentals=QROWS * HALF * subs,
        ),
        name=name,
    )(queries, *start, *pieces)


def cache_kernel(places, table, *refs):
    pieces, (out, zeros, sem) = refs[:-3], refs[-3:]
    zeros[...] = jnp.zeros_like(zeros)
    section = lax.axis_index("section")
    x, z = section // SIDE, section % SIDE
    for dx in range(SIDE):
        for dz in range(SIDE):
            source = lax.rem(x + dx, SIDE) * SIDE + lax.rem(z + dz, SIDE)
            for rank in range(PAIR):
                slot = source * PAIR + rank
                block = table[slot]

                @pl.when(block < 0)
                def _():
                    pltpu.make_async_copy(zeros, out.at[slot], sem).start()

                for half in range(2):
                    piece, row = places[half][(dx, dz)]
                    inside = block - half * (HALF // BLOCK)

                    @pl.when((inside >= 0) & (inside < HALF // BLOCK))
                    def _():
                        at = pl.ds(pl.multiple_of(row + inside * BLOCK, BLOCK), BLOCK)
                        pltpu.make_async_copy(pieces[piece].at[at, :], out.at[slot], sem).start()

    pltpu.make_async_copy(out, out, sem).wait()


def cache_table(placement, section):
    owners = placement.reshape(SIDE * SIDE, ROWS // BLOCK)
    mine = owners == section
    before = jnp.arange(ROWS // BLOCK)[:, None] < jnp.arange(ROWS // BLOCK)[None, :]
    ranks = jnp.sum((mine[:, :, None] & before[None]).astype(jnp.int32), axis=1)
    hit = mine[:, None, :] & (ranks[:, None, :] == jnp.arange(PAIR)[None, :, None])
    number = jnp.arange(ROWS // BLOCK, dtype=jnp.int32) + 1
    return (jnp.sum(jnp.where(hit, number[None, None, :], 0), axis=-1) - 1).reshape(-1)


def decode(places, table, pieces):
    slots = SIDE * SIDE * PAIR
    return pl.pallas_call(
        functools.partial(cache_kernel, places),
        in_specs=[pl.BlockSpec(memory_space=pltpu.SMEM)] + [ANY] * len(pieces),
        out_specs=ANY,
        out_shape=jax.ShapeDtypeStruct((slots, BLOCK, 2 * HD), BF),
        scratch_shapes=[pltpu.VMEM((BLOCK, 2 * HD), BF), pltpu.SemaphoreType.DMA],
        compiler_params=VMEM,
        cost_estimate=pl.CostEstimate(flops=0, bytes_accessed=4 << 20, transcendentals=0),
        name="decode_cache",
    )(table, *pieces)


COLS = 1024
PART = 512


def project_kernel(targets, index, own, other, w_own, w_other, *refs):
    product = jnp.dot(own[...], w_own[...], preferred_element_type=F32)
    product += jnp.dot(other[...], w_other[...], preferred_element_type=F32)
    if targets == (2,):
        refs[0][...] = product[:HALF].astype(BF)
        refs[1][...] = product[HALF:].astype(BF)
    elif targets == (1, 3):
        from_below, from_above, up, down = refs
        step = pl.program_id(0)

        @pl.when(step < COLS // PART)
        def _():
            up[:HALF] = (product[:HALF] + from_below[...].astype(F32)).astype(BF)
            up[HALF:] = product[HALF:].astype(BF)

        @pl.when(step >= COLS // PART)
        def _():
            down[:HALF] = product[:HALF].astype(BF)
            down[HALF:] = (product[HALF:] + from_above[...].astype(F32)).astype(BF)
    else:
        from_below, from_above, tokens, mixed = refs
        total = product + from_below[...].astype(F32) + from_above[...].astype(F32)
        mixed[...] = (tokens[...].astype(F32) + total).astype(BF)


def project(targets, index, own, other, w_own, w_other, extra):
    per = COLS // PART
    ring = lambda i, t: lax.rem(t[0] // 2 + (targets[0] if len(targets) == 1 else 1 + 2 * (i // per)), SIDE)
    own_col = lambda i, t: (0, (ring(i, t) * 2 + lax.rem(t[0], 2)) * per + lax.rem(i, per))
    other_col = lambda i, t: (0, ring(i, t) * per + lax.rem(i, per))
    here = lambda i, t: (0, lax.rem(i, per))
    low = lambda i, t: (0, jnp.minimum(i, per - 1))
    high = lambda i, t: (0, jnp.maximum(i - per, 0))
    full = lambda i, t: (0, 0)
    share = jax.ShapeDtypeStruct((ROWS, COLS), BF)
    if targets == (2,):
        extra_specs = []
        out_specs = [pl.BlockSpec((HALF, PART), here)] * 2
        out_shape = [jax.ShapeDtypeStruct((HALF, COLS), BF)] * 2
    elif targets == (1, 3):
        extra_specs = [pl.BlockSpec((HALF, PART), low), pl.BlockSpec((HALF, PART), high)]
        out_specs = [pl.BlockSpec((ROWS, PART), low), pl.BlockSpec((ROWS, PART), high)]
        out_shape = [share] * 2
    else:
        extra_specs = [pl.BlockSpec((ROWS, PART), here)] * 2
        extra_specs.append(pl.BlockSpec((ROWS, PART), lambda i, t: (0, t[0] * per + i)))
        out_specs = [pl.BlockSpec((ROWS, PART), here)]
        out_shape = [share]
    return pl.pallas_call(
        functools.partial(project_kernel, targets),
        grid_spec=pltpu.PrefetchScalarGridSpec(
            num_scalar_prefetch=1,
            grid=(per * len(targets),),
            in_specs=[
                pl.BlockSpec((ROWS, HEADS * HD), full),
                pl.BlockSpec((ROWS, HEADS * HD), full),
                pl.BlockSpec((HEADS * HD, PART), own_col),
                pl.BlockSpec((HEADS * HD, PART), other_col),
                *extra_specs,
            ],
            out_specs=out_specs,
        ),
        out_shape=out_shape,
        compiler_params=VMEM,
        cost_estimate=pl.CostEstimate(
            flops=4 * ROWS * 512 * COLS * len(targets), bytes_accessed=6 << 20, transcendentals=0
        ),
        name="project_" + "".join(map(str, targets)),
    )(index, own, other, w_own, w_other, *extra)


def from_section(value, dx, dz):
    pairs = []
    for x in range(SIDE):
        for z in range(SIDE):
            pairs.append((((x + dx) % SIDE) * SIDE + (z + dz) % SIDE, x * SIDE + z))
    return lax.ppermute(value, "section", pairs)


def from_tp(value, dy, dc):
    pairs = []
    for y in range(SIDE):
        for c in range(2):
            pairs.append((((y + dy) % SIDE) * 2 + (c ^ dc), y * 2 + c))
    return lax.ppermute(value, "tp", pairs)


RING = (1, 3, 2)
ORDER = (0,) + RING


def per_device(tokens, gain, q_weight, q_bias, kv_weight, kv_bias, out_weight, placement):
    section = lax.axis_index("section")
    tp = lax.axis_index("tp")
    small, large = tables()
    normed, first, second = norm_kv(tokens, gain[None, :], kv_weight, kv_bias[None, :], small, large)
    row_first = [from_section(first, 0, k) for k in RING]
    row_second = [from_section(second, k, 0) for k in RING]
    queries = query(normed, q_weight, q_bias[None, :], small, large)
    split = out_weight.reshape(HEADS * HD, SIDE, 2, COLS)
    other = lax.dynamic_index_in_dim(split, 1 - lax.rem(tp, 2), 2, keepdims=False)
    w_other = from_tp(other.reshape(HEADS * HD, SIDE * COLS), 0, 1)
    all_first = jnp.concatenate([first, *row_first], 0)
    all_second = jnp.concatenate([second, *row_second], 0)
    far_first = [from_section(all_first, k, 0) for k in RING]
    far_second = [from_section(all_second, 0, k) for k in RING]
    near = [[(0, k)] for k in RING] + [[(k, 0)] for k in RING]
    state = attention(
        queries, (first, second), None, row_first + row_second, near, False, "attention_near"
    )
    far = [[(k, j) for j in ORDER] for k in RING], [[(j, k) for j in ORDER] for k in RING]
    state = attention(
        queries, None, state, far_first[:2] + far_second[:2], far[0][:2] + far[1][:2], False, "attention_far"
    )
    (attended,) = attention(
        queries, None, state, far_first[2:] + far_second[2:], far[0][2:] + far[1][2:], True, "attention_last"
    )
    attended_other = from_tp(attended, 0, 1)
    index = jnp.reshape(tp, (1,)).astype(jnp.int32)
    call = lambda targets, extra: project(
        targets, index, attended, attended_other, out_weight, w_other, extra
    )
    top, bottom = call((2,), [])
    from_below, from_above = from_tp(top, 3, 0), from_tp(bottom, 1, 0)
    up, down = call((1, 3), [from_below, from_above])
    from_below, from_above = from_tp(up, 3, 0), from_tp(down, 1, 0)
    (mixed,) = call((0,), [from_below, from_above, tokens])
    pieces = [first, second] + row_first + row_second + far_first + far_second
    places = [{(0, 0): (0, 0)}, {(0, 0): (1, 0)}]
    for i, k in enumerate(RING):
        places[0][(0, k)] = (2 + i, 0)
        places[1][(k, 0)] = (5 + i, 0)
        for n, j in enumerate(ORDER):
            places[0][(k, j)] = (8 + i, n * HALF)
            places[1][(j, k)] = (11 + i, n * HALF)
    decode_cache = decode(places, cache_table(placement, section), pieces)
    return mixed, decode_cache


def solution(mesh):
    placed = (
        P("section", None),
        P(),
        P(None, "tp"),
        P("tp"),
        P(None, "tp"),
        P("tp"),
        P("tp", None),
        P(),
    )
    return jax.shard_map(
        per_device,
        mesh=mesh,
        in_specs=placed,
        out_specs=(P("section", "tp"), P("section", None, "tp")),
        check_vma=False,
    )
```

```python
import functools
import math

import jax
import jax.numpy as jnp
import numpy as np
from jax import lax
from jax.experimental import pallas as pl
from jax.experimental.pallas import tpu as pltpu
from jax.sharding import PartitionSpec as P

HD = 128
BLOCK = 16
SIDE = 4
HALF = 256
ROWS = 512
D = 8192
HEADS = 4
PAIR = 4
ROPE_BASE = 1000000.0
LOG2_SCALE = math.log2(math.e) / math.sqrt(HD)
SHARE = 256
COLS = 1024
limit = lambda mib: pltpu.CompilerParams(vmem_limit_bytes=mib * 1024 * 1024)
BF = jnp.bfloat16
F32 = jnp.float32
ANY = pl.BlockSpec(memory_space=pl.ANY)
WHOLE = pl.BlockSpec(memory_space=pltpu.VMEM)
FAR = pl.BlockSpec(memory_space=pltpu.HBM)


def tables():
    freq = ROPE_BASE ** (-(np.arange(HD // 2, dtype=np.float64) * 2.0 / HD))
    inner = np.arange(ROWS, dtype=np.float64)[:, None] * freq
    outer = ROWS * np.arange(SIDE * SIDE, dtype=np.float64)[:, None] * freq
    twice = lambda a: np.concatenate([a, a], -1)
    signed = lambda a: np.concatenate([-a, a], -1)
    small = np.concatenate([twice(np.cos(inner)), twice(np.sin(inner))], -1)
    large = np.concatenate(
        [twice(np.cos(outer)), twice(np.sin(outer)), signed(np.cos(outer)), signed(np.sin(outer))], -1
    )
    return small.astype(np.float32), large.astype(np.float32)


def angles(small, large):
    cos_r, sin_r = small[:, :HD], small[:, HD:]
    cos_s, sin_s = large[:, :HD], large[:, HD : 2 * HD]
    cos_g, sin_g = large[:, 2 * HD : 3 * HD], large[:, 3 * HD :]
    return cos_s * cos_r - sin_s * sin_r, sin_g * cos_r + cos_g * sin_r


def turn(value, cosine, sine):
    return value * cosine + pltpu.roll(value, HD // 2, 1) * sine


CHUNK = 64
GROUP = 32
DEPTH = 2048
AHEAD = 3


def norm_kv_kernel(
    tokens, gain, weight, bias, small, large, w_out, factors, first, second, w_send, tv, nv, wv, sv, total, st, sw, sn, ss
):
    chunks = ROWS // CHUNK
    rows_at = lambda i: pl.ds(pl.multiple_of(i * CHUNK, CHUNK), CHUNK)
    load = lambda i: pltpu.make_async_copy(tokens.at[rows_at(i), :], tv.at[rows_at(i), :], st.at[i])
    weights = [
        pltpu.make_async_copy(weight.at[k : k + DEPTH, :], wv.at[k : k + DEPTH, :], sw.at[k // DEPTH])
        for k in range(0, D, DEPTH)
    ]
    sibling = 1 - lax.rem(lax.axis_index("tp"), 2)
    fetches, sends = [], []
    for y in range(SIDE):
        here = pl.ds(pl.multiple_of((2 * y + sibling) * COLS, COLS), COLS)
        fetches.append(pltpu.make_async_copy(w_out.at[:, here], sv.at[y], sn.at[y]))
        sends.append(pltpu.make_async_copy(sv.at[y], w_send.at[:, y * COLS : (y + 1) * COLS], ss.at[y]))
    for i in range(AHEAD):
        load(i).start()

    def chunk(i, _):
        load(i).wait()

        @pl.when(i < chunks - AHEAD)
        def _():
            load(i + AHEAD).start()

        for n in range(AHEAD):
            @pl.when(i == chunks - AHEAD + n)
            def _():
                weights[n].start()

        for g in range(0, CHUNK, GROUP):
            rows = pl.ds(pl.multiple_of(i * CHUNK + g, GROUP), GROUP)
            squares = jnp.zeros((GROUP, 128), F32)
            for c in range(0, D, 1024):
                wide = tv[rows, c : c + 1024].astype(F32)
                square = wide * wide
                for k in range(0, 1024, 128):
                    squares = squares + square[:, k : k + 128]
            meansq = jnp.sum(squares, axis=1, keepdims=True) * (1.0 / D)
            factor = lax.rsqrt(meansq + 1e-06)
            factors[rows, :] = jnp.broadcast_to(factor, (GROUP, 128))
            for c in range(0, D, 1024):
                wide = tv[rows, c : c + 1024].astype(F32)
                nv[rows, c : c + 1024] = (wide * factor * gain[:, c : c + 1024]).astype(BF)
        return 0

    lax.fori_loop(0, chunks, chunk, 0)
    for n in range(AHEAD, D // DEPTH):
        weights[n].start()
    for copy in fetches:
        copy.start()
    total[...] = jnp.broadcast_to(bias[...], total.shape)
    for n, k in enumerate(range(0, D, DEPTH)):
        weights[n].wait()
        total[...] += jnp.dot(nv[:, k : k + DEPTH], wv[k : k + DEPTH, :], preferred_element_type=F32)
        if n >= 2:
            for y in range(2 * n - 4, 2 * n - 2):
                fetches[y].wait()
                sends[y].start()
    cosine, sine = angles(small[...], large[pl.ds(lax.axis_index("section"), 1), :])
    keys = turn(total[:, :HD], cosine, sine).astype(BF)
    values = total[:, HD:].astype(BF)
    for half, out in enumerate((first, second)):
        rows = slice(half * HALF, (half + 1) * HALF)
        out[:, :HD] = keys[rows]
        out[:, HD:] = values[rows]
    for copy in sends:
        copy.wait()


def norm_kv(tokens, gain, weight, bias, small, large, w_out):
    half = jax.ShapeDtypeStruct((HALF, 2 * HD), BF)
    return pl.pallas_call(
        norm_kv_kernel,
        in_specs=[ANY, WHOLE, ANY, WHOLE, WHOLE, WHOLE, ANY],
        out_specs=[WHOLE, WHOLE, WHOLE, ANY],
        out_shape=[
            jax.ShapeDtypeStruct((ROWS, 128), F32),
            half,
            half,
            jax.ShapeDtypeStruct((HEADS * HD, SIDE * COLS), BF),
        ],
        scratch_shapes=[
            pltpu.VMEM((ROWS, D), BF),
            pltpu.VMEM((ROWS, D), BF),
            pltpu.VMEM((D, 2 * HD), BF),
            pltpu.VMEM((SIDE, HEADS * HD, COLS), BF),
            pltpu.VMEM((ROWS, 2 * HD), F32),
            pltpu.SemaphoreType.DMA((ROWS // CHUNK,)),
            pltpu.SemaphoreType.DMA((D // DEPTH,)),
            pltpu.SemaphoreType.DMA((SIDE,)),
            pltpu.SemaphoreType.DMA((SIDE,)),
        ],
        compiler_params=limit(56),
        cost_estimate=pl.CostEstimate(flops=2 * ROWS * D * 256, bytes_accessed=20 << 20, transcendentals=0),
        name="norm_kv",
    )(tokens, gain, weight, bias, small, large, w_out)


Q_DEPTH = 1024
Q_AHEAD = 2


def query_kernel(tokens, factors, gain, weight, bias, small, large, out, tv, nv, wv, total, sems):
    steps = D // Q_DEPTH
    copies = []
    for n in range(steps):
        at = slice(n * Q_DEPTH, (n + 1) * Q_DEPTH)
        copies.append(
            (
                pltpu.make_async_copy(tokens.at[:, at], tv.at[n], sems.at[n, 0]),
                pltpu.make_async_copy(weight.at[at, :], wv.at[n], sems.at[n, 1]),
            )
        )
    begin = lambda n: [copy.start() for copy in copies[n]]
    for n in range(Q_AHEAD):
        begin(n)
    total[...] = jnp.broadcast_to(bias[...], total.shape)

    def scale(n):
        for copy in copies[n]:
            copy.wait()
        if n + Q_AHEAD < steps:
            begin(n + Q_AHEAD)
        for r in range(0, ROWS, 128):
            factor = factors[r : r + 128, :1]
            at = slice(n * Q_DEPTH, (n + 1) * Q_DEPTH)
            nv[n, r : r + 128, :] = (tv[n, r : r + 128, :].astype(F32) * factor * gain[:, at]).astype(BF)

    scale(0)
    for n in range(steps):
        if n + 1 < steps:
            scale(n + 1)
        total[...] += jnp.dot(nv[n], wv[n], preferred_element_type=F32)
    cosine, sine = angles(small[...], large[pl.ds(lax.axis_index("section"), 1), :])
    for h in range(HEADS):
        value = turn(total[:, h * HD : (h + 1) * HD], cosine, sine).astype(BF)
        for n in range(ROWS // SHARE):
            start = (n * HEADS + h) * SHARE
            out[start : start + SHARE, :] = value[n * SHARE : (n + 1) * SHARE]


def query(tokens, factors, gain, weight, bias, small, large):
    width = HEADS * HD
    steps = D // Q_DEPTH
    return pl.pallas_call(
        query_kernel,
        in_specs=[ANY, WHOLE, WHOLE, ANY, WHOLE, WHOLE, WHOLE],
        out_specs=WHOLE,
        out_shape=jax.ShapeDtypeStruct((HEADS * ROWS, HD), BF),
        scratch_shapes=[
            pltpu.VMEM((steps, ROWS, Q_DEPTH), BF),
            pltpu.VMEM((steps, ROWS, Q_DEPTH), BF),
            pltpu.VMEM((steps, Q_DEPTH, width), BF),
            pltpu.VMEM((ROWS, width), F32),
            pltpu.SemaphoreType.DMA((steps, 2)),
        ],
        compiler_params=limit(56),
        cost_estimate=pl.CostEstimate(flops=2 * ROWS * D * 512, bytes_accessed=16 << 20, transcendentals=0),
        name="query",
    )(tokens, factors, gain, weight, bias, small, large)


TILE = 128
QROWS = HEADS * ROWS


def attend(queries, keys, values, acc, maxima, rows, mask=None, first=False):
    scores = lax.dot_general(queries, keys, (((1,), (1,)), ((), ())), preferred_element_type=F32)
    if mask is not None:
        scores = jnp.where(mask, scores, -1e30)
    highest = jnp.max(scores, axis=1, keepdims=True)
    if first:
        newest = jnp.broadcast_to(highest, (rows.size, HD))
    else:
        old = maxima[rows, :]
        newest = jnp.maximum(old, highest)
        rescale = jnp.exp2((old - newest) * LOG2_SCALE)
    maxima[rows, :] = newest
    weights = jnp.exp2(scores * LOG2_SCALE - newest[:, :1] * LOG2_SCALE).astype(BF)
    added = jnp.dot(weights, values, preferred_element_type=F32)
    if first:
        acc[rows, :] = added
    else:
        acc[rows, :HD] = acc[rows, :HD] * rescale + added[:, :HD]
        acc[rows, HD:] = acc[rows, HD:] * rescale + added[:, HD:]


def attend_kernel(plan, diagonal, final, *refs):
    refs = list(refs)
    take = lambda n: [refs.pop(0) for _ in range(n)]
    (queries,) = take(1)
    begin = take(2)
    pieces = take(len(plan))
    outs = take(1 if final else 2)
    if final:
        keys, values, acc, maxima, sems = refs
    else:
        keys, values, sems = refs
        acc, maxima = outs
    count_rows = queries.shape[0]
    section = lax.axis_index("section")
    x, z = section // SIDE, section % SIDE
    count = jnp.int32(0)
    jobs = []
    for piece, offsets in zip(pieces, plan):
        for j, (dx, dz) in enumerate(offsets):
            source = lax.rem(x + dx, SIDE) * SIDE + lax.rem(z + dz, SIDE)
            needed = source < section
            here = pl.ds(j * HALF, HALF)
            there = pl.ds(pl.multiple_of(count * HALF, HALF), HALF)
            n = len(jobs)
            copies = (
                pltpu.make_async_copy(piece.at[here, :HD], keys.at[there, :], sems.at[n, 0]),
                pltpu.make_async_copy(piece.at[here, HD:], values.at[there, :HD], sems.at[n, 1]),
            )

            @pl.when(needed)
            def _():
                copies[0].start()
                copies[1].start()

            jobs.append((needed, copies))
            count = count + needed.astype(jnp.int32)
    values[:, HD:] = jnp.ones((values.shape[0], HD), BF)
    if diagonal:
        last = len(jobs) * HALF
        for half in range(2):
            rows = slice(last + half * HALF, last + (half + 1) * HALF)
            keys[rows, :] = begin[half][:, :HD]
            values[rows, :HD] = begin[half][:, HD:]
        for start in range(0, ROWS, TILE):
            shape = (TILE, start + TILE)
            mask = lax.broadcasted_iota(jnp.int32, shape, 1) <= start + lax.broadcasted_iota(jnp.int32, shape, 0)
            kd, vd = keys[last : last + start + TILE, :], values[last : last + start + TILE, :]
            for h in range(HEADS):
                rows = pl.ds((start // SHARE * HEADS + h) * SHARE + start % SHARE, TILE)
                attend(queries[rows, :], kd, vd, acc, maxima, rows, mask, True)
    else:
        acc[...] = begin[0][...]
        maxima[...] = begin[1][...]
    for needed, copies in jobs:
        @pl.when(needed)
        def _():
            copies[0].wait()
            copies[1].wait()

    def part(base, size):
        at = pl.ds(pl.multiple_of(base, HALF), size)
        kd, vd = keys[at, :], values[at, :]
        for start in range(0, count_rows, TILE):
            rows = pl.ds(start, TILE)
            attend(queries[rows, :], kd, vd, acc, maxima, rows)

    def whole(i, _):
        part(i * 4 * HALF, 4 * HALF)
        return 0

    lax.fori_loop(0, count // 4, whole, 0)
    left = lax.rem(count, 4)

    @pl.when(left >= 2)
    def _():
        part((count // 4) * 4 * HALF, 2 * HALF)

    @pl.when(lax.rem(left, 2) == 1)
    def _():
        part((count - 1) * HALF, HALF)

    if final:
        for h in range(HEADS):
            rows = slice(h * SHARE, (h + 1) * SHARE)
            outs[0][:, h * HD : (h + 1) * HD] = (acc[rows, :HD] / acc[rows, HD:]).astype(BF)


def attention(queries, begin, pieces, plan, name, diagonal=False, share=None):
    subs = sum(len(p) for p in plan)
    final = share is not None
    rows = HEADS * SHARE if final else QROWS
    size = subs * HALF + (ROWS if diagonal else 0)
    state_shape = [jax.ShapeDtypeStruct((rows, 2 * HD), F32), jax.ShapeDtypeStruct((rows, HD), F32)]
    scratch = [pltpu.VMEM((size, HD), BF), pltpu.VMEM((size, 2 * HD), BF)]
    if final:
        scratch += [pltpu.VMEM(s.shape, s.dtype) for s in state_shape]
        out_shape = [jax.ShapeDtypeStruct((SHARE, HEADS * HD), BF)]
        at = lambda i: (share, 0)
        first_specs = [pl.BlockSpec((rows, HD), at), pl.BlockSpec((rows, 2 * HD), at), pl.BlockSpec((rows, HD), at)]
        grid = (1,)
        out_specs = [pl.BlockSpec((SHARE, HEADS * HD), lambda i: (0, 0))]
    else:
        out_shape = state_shape
        first_specs = [WHOLE] * 3
        grid = ()
        out_specs = [WHOLE] * 2
    scratch.append(pltpu.SemaphoreType.DMA((subs, 2)))
    return pl.pallas_call(
        functools.partial(attend_kernel, plan, diagonal, final),
        grid=grid,
        in_specs=first_specs + [ANY] * len(pieces),
        out_specs=out_specs,
        out_shape=out_shape,
        scratch_shapes=scratch,
        compiler_params=limit(20),
        cost_estimate=pl.CostEstimate(
            flops=8 * rows * size * HD, bytes_accessed=8 << 20, transcendentals=rows * size
        ),
        name=name,
    )(queries, *begin, *pieces)


def join_kernel(*refs):
    n = (len(refs) - 2) // 2
    for ins, out in ((refs[:n], refs[-2]), (refs[n : 2 * n], refs[-1])):
        for j, piece in enumerate(ins):
            out[j * HALF : (j + 1) * HALF, :] = piece[...]


def join(first, second):
    out = jax.ShapeDtypeStruct((len(first) * HALF, 2 * HD), BF)
    return pl.pallas_call(
        join_kernel,
        in_specs=[WHOLE] * (len(first) + len(second)),
        out_specs=[WHOLE] * 2,
        out_shape=[out] * 2,
        compiler_params=limit(8),
        cost_estimate=pl.CostEstimate(flops=0, bytes_accessed=2 << 20, transcendentals=0),
        name="join",
    )(*first, *second)


def cache_kernel(places, table, *refs):
    pieces, (out, zeros, sem) = refs[:-3], refs[-3:]
    zeros[...] = jnp.zeros_like(zeros)
    section = lax.axis_index("section")
    x, z = section // SIDE, section % SIDE
    for dx in range(SIDE):
        for dz in range(SIDE):
            source = lax.rem(x + dx, SIDE) * SIDE + lax.rem(z + dz, SIDE)
            for rank in range(PAIR):
                slot = source * PAIR + rank
                block = table[slot]

                @pl.when(block < 0)
                def _():
                    pltpu.make_async_copy(zeros, out.at[slot], sem).start()

                for half in range(2):
                    piece, row = places[half][(dx, dz)]
                    inside = block - half * (HALF // BLOCK)

                    @pl.when((inside >= 0) & (inside < HALF // BLOCK))
                    def _():
                        at = pl.ds(pl.multiple_of(row + inside * BLOCK, BLOCK), BLOCK)
                        pltpu.make_async_copy(pieces[piece].at[at, :], out.at[slot], sem).start()

    pltpu.make_async_copy(out, out, sem).wait()


def cache_table(placement, section):
    owners = placement.reshape(SIDE * SIDE, ROWS // BLOCK)
    mine = owners == section
    before = jnp.arange(ROWS // BLOCK)[:, None] < jnp.arange(ROWS // BLOCK)[None, :]
    ranks = jnp.sum((mine[:, :, None] & before[None]).astype(jnp.int32), axis=1)
    hit = mine[:, None, :] & (ranks[:, None, :] == jnp.arange(PAIR)[None, :, None])
    number = jnp.arange(ROWS // BLOCK, dtype=jnp.int32) + 1
    return (jnp.sum(jnp.where(hit, number[None, None, :], 0), axis=-1) - 1).reshape(-1)


def decode(places, table, pieces):
    slots = SIDE * SIDE * PAIR
    return pl.pallas_call(
        functools.partial(cache_kernel, places),
        in_specs=[pl.BlockSpec(memory_space=pltpu.SMEM)] + [ANY] * len(pieces),
        out_specs=WHOLE,
        out_shape=jax.ShapeDtypeStruct((slots, BLOCK, 2 * HD), BF),
        scratch_shapes=[pltpu.VMEM((BLOCK, 2 * HD), BF), pltpu.SemaphoreType.DMA],
        compiler_params=limit(16),
        cost_estimate=pl.CostEstimate(flops=0, bytes_accessed=4 << 20, transcendentals=0),
        name="decode_cache",
    )(table, *pieces)


PART = 512


MID = SHARE // 2


def project_kernel(targets, index, own, other, w_own, w_other, *refs):
    product = jnp.dot(own[...], w_own[...], preferred_element_type=F32)
    product += jnp.dot(other[...], w_other[...], preferred_element_type=F32)
    if targets == (2,):
        refs[0][...] = product[:MID].astype(BF)
        refs[1][...] = product[MID:].astype(BF)
    elif targets == (1, 3):
        from_below, from_above, up, down = refs
        step = pl.program_id(0)

        @pl.when(step < COLS // PART)
        def _():
            up[:MID] = (product[:MID] + from_below[...].astype(F32)).astype(BF)
            up[MID:] = product[MID:].astype(BF)

        @pl.when(step >= COLS // PART)
        def _():
            down[:MID] = product[:MID].astype(BF)
            down[MID:] = (product[MID:] + from_above[...].astype(F32)).astype(BF)
    else:
        from_below, from_above, tokens = refs[:3]
        total = product + from_below[...].astype(F32) + from_above[...].astype(F32)
        refs[-1][...] = (tokens[...].astype(F32) + total).astype(BF)


def project(targets, index, own, other, w_own, w_other, extra, share=0):
    per = COLS // PART
    ring = lambda i, t: lax.rem(t[0] // 2 + (targets[0] if len(targets) == 1 else 1 + 2 * (i // per)), SIDE)
    own_col = lambda i, t: (0, (ring(i, t) * 2 + lax.rem(t[0], 2)) * per + lax.rem(i, per))
    other_col = lambda i, t: (0, ring(i, t) * per + lax.rem(i, per))
    here = lambda i, t: (0, lax.rem(i, per))
    low = lambda i, t: (0, jnp.minimum(i, per - 1))
    high = lambda i, t: (0, jnp.maximum(i - per, 0))
    full = lambda i, t: (0, 0)
    block = jax.ShapeDtypeStruct((SHARE, COLS), BF)
    aliases = {}
    if targets == (2,):
        extra_specs = []
        out_specs = [pl.BlockSpec((MID, PART), here)] * 2
        out_shape = [jax.ShapeDtypeStruct((MID, COLS), BF)] * 2
    elif targets == (1, 3):
        extra_specs = [pl.BlockSpec((MID, PART), low), pl.BlockSpec((MID, PART), high)]
        out_specs = [pl.BlockSpec((SHARE, PART), low), pl.BlockSpec((SHARE, PART), high)]
        out_shape = [block] * 2
    else:
        extra_specs = [pl.BlockSpec((SHARE, PART), here)] * 2
        extra_specs.append(pl.BlockSpec((SHARE, PART), lambda i, t: (share, t[0] * per + i)))
        if len(extra) > 3:
            extra_specs.append(ANY)
            aliases = {8: 0}
        out_specs = [pl.BlockSpec((SHARE, PART), lambda i, t: (share, i))]
        out_shape = [jax.ShapeDtypeStruct((ROWS, COLS), BF)]
    return pl.pallas_call(
        functools.partial(project_kernel, targets),
        grid_spec=pltpu.PrefetchScalarGridSpec(
            num_scalar_prefetch=1,
            grid=(per * len(targets),),
            in_specs=[
                pl.BlockSpec((SHARE, HEADS * HD), full),
                pl.BlockSpec((SHARE, HEADS * HD), full),
                pl.BlockSpec((HEADS * HD, PART), own_col),
                pl.BlockSpec((HEADS * HD, PART), other_col),
                *extra_specs,
            ],
            out_specs=out_specs,
        ),
        out_shape=out_shape,
        input_output_aliases=aliases,
        compiler_params=limit(16),
        cost_estimate=pl.CostEstimate(
            flops=4 * SHARE * 512 * COLS * len(targets), bytes_accessed=6 << 20, transcendentals=0
        ),
        name="project_" + "".join(map(str, targets)),
    )(index, own, other, w_own, w_other, *extra)


def from_section(value, dx, dz):
    pairs = []
    for x in range(SIDE):
        for z in range(SIDE):
            pairs.append((((x + dx) % SIDE) * SIDE + (z + dz) % SIDE, x * SIDE + z))
    return lax.ppermute(value, "section", pairs)


def from_tp(value, dy, dc):
    pairs = []
    for y in range(SIDE):
        for c in range(2):
            pairs.append((((y + dy) % SIDE) * 2 + (c ^ dc), y * 2 + c))
    return lax.ppermute(value, "tp", pairs)


RING = (1, 3, 2)
ORDER = (0,) + RING


def per_device(tokens, gain, q_weight, q_bias, kv_weight, kv_bias, out_weight, placement):
    section = lax.axis_index("section")
    tp = lax.axis_index("tp")
    small, large = tables()
    factors, first, second, w_send = norm_kv(
        tokens, gain[None, :], kv_weight, kv_bias[None, :], small, large, out_weight
    )
    row_first = [from_section(first, 0, k) for k in RING]
    row_second = [from_section(second, k, 0) for k in RING]
    w_other = from_tp(w_send, 0, 1)
    queries = query(tokens, factors, gain[None, :], q_weight, q_bias[None, :], small, large)
    all_first, all_second = join([first, *row_first], [second, *row_second])
    far_first = [from_section(all_first, k, 0) for k in RING]
    far_second = [from_section(all_second, 0, k) for k in RING]
    near = [[(0, k)] for k in RING] + [[(k, 0)] for k in RING]
    state = attention(queries, (first, second), row_first + row_second, near, "attention_near", diagonal=True)
    far = [[(k, j) for j in ORDER] for k in RING], [[(j, k) for j in ORDER] for k in RING]
    state = attention(
        queries, state, far_first[:2] + far_second[:2], far[0][:2] + far[1][:2], "attention_far"
    )
    index = jnp.reshape(tp, (1,)).astype(jnp.int32)
    mixed = []
    for share in range(ROWS // SHARE):
        (own,) = attention(
            queries, state, far_first[2:] + far_second[2:], far[0][2:] + far[1][2:], "attention_last", share=share
        )
        other = from_tp(own, 0, 1)
        call = lambda targets, extra: project(targets, index, own, other, out_weight, w_other, extra, share)
        top, bottom = call((2,), [])
        from_below, from_above = from_tp(top, 3, 0), from_tp(bottom, 1, 0)
        up, down = call((1, 3), [from_below, from_above])
        from_below, from_above = from_tp(up, 3, 0), from_tp(down, 1, 0)
        mixed = call((0,), [from_below, from_above, tokens, *mixed])
    pieces = [first, second] + row_first + row_second + far_first + far_second
    places = [{(0, 0): (0, 0)}, {(0, 0): (1, 0)}]
    for i, k in enumerate(RING):
        places[0][(0, k)] = (2 + i, 0)
        places[1][(k, 0)] = (5 + i, 0)
        for n, j in enumerate(ORDER):
            places[0][(k, j)] = (8 + i, n * HALF)
            places[1][(j, k)] = (11 + i, n * HALF)
    decode_cache = decode(places, cache_table(placement, section), pieces)
    return mixed[0], decode_cache


def solution(mesh):
    placed = (
        P("section", None),
        P(),
        P(None, "tp"),
        P("tp"),
        P(None, "tp"),
        P("tp"),
        P("tp", None),
        P(),
    )
    return jax.shard_map(
        per_device,
        mesh=mesh,
        in_specs=placed,
        out_specs=(P("section", "tp"), P("section", None, "tp")),
        check_vma=False,
    )
```

```python
import functools
import math

import jax
import jax.numpy as jnp
import numpy as np
from jax import lax
from jax.experimental import pallas as pl
from jax.experimental.pallas import tpu as pltpu
from jax.sharding import PartitionSpec as P

HD = 128
BLOCK = 16
SIDE = 4
HALF = 256
ROWS = 512
D = 8192
HEADS = 4
PAIR = 4
ROPE_BASE = 1000000.0
LOG2_SCALE = math.log2(math.e) / math.sqrt(HD)
SHARE = 256
COLS = 1024
limit = lambda mib: pltpu.CompilerParams(vmem_limit_bytes=mib * 1024 * 1024)
BF = jnp.bfloat16
F32 = jnp.float32
ANY = pl.BlockSpec(memory_space=pl.ANY)
WHOLE = pl.BlockSpec(memory_space=pltpu.VMEM)
FAR = pl.BlockSpec(memory_space=pltpu.HBM)


def tables():
    freq = ROPE_BASE ** (-(np.arange(HD // 2, dtype=np.float64) * 2.0 / HD))
    inner = np.arange(ROWS, dtype=np.float64)[:, None] * freq
    outer = ROWS * np.arange(SIDE * SIDE, dtype=np.float64)[:, None] * freq
    twice = lambda a: np.concatenate([a, a], -1)
    signed = lambda a: np.concatenate([-a, a], -1)
    small = np.concatenate([twice(np.cos(inner)), twice(np.sin(inner))], -1)
    large = np.concatenate(
        [twice(np.cos(outer)), twice(np.sin(outer)), signed(np.cos(outer)), signed(np.sin(outer))], -1
    )
    return small.astype(np.float32), large.astype(np.float32)


def angles(small, large):
    cos_r, sin_r = small[:, :HD], small[:, HD:]
    cos_s, sin_s = large[:, :HD], large[:, HD : 2 * HD]
    cos_g, sin_g = large[:, 2 * HD : 3 * HD], large[:, 3 * HD :]
    return cos_s * cos_r - sin_s * sin_r, sin_g * cos_r + cos_g * sin_r


def turn(value, cosine, sine):
    return value * cosine + pltpu.roll(value, HD // 2, 1) * sine


CHUNK = 64
GROUP = 32
DEPTH = 2048
AHEAD = 4
NORM_LIMIT = 56


def norm_kv_kernel(
    tokens, gain, weight, bias, small, large, normed, first, second, residual, tv, nv, wv, total, st, sw, sn
):
    chunks = ROWS // CHUNK
    rows_at = lambda i: pl.ds(pl.multiple_of(i * CHUNK, CHUNK), CHUNK)
    load = lambda i: pltpu.make_async_copy(tokens.at[rows_at(i), :], tv.at[rows_at(i), :], st.at[i])
    store = lambda i: pltpu.make_async_copy(nv.at[rows_at(i), :], normed.at[rows_at(i), :], sn.at[i])
    weights = [
        pltpu.make_async_copy(weight.at[k : k + DEPTH, :], wv.at[k : k + DEPTH, :], sw.at[k // DEPTH])
        for k in range(0, D, DEPTH)
    ]
    for i in range(AHEAD):
        load(i).start()

    def chunk(i, _):
        load(i).wait()

        @pl.when(i < chunks - AHEAD)
        def _():
            load(i + AHEAD).start()

        for n in range(AHEAD):
            @pl.when(i == chunks - AHEAD + n)
            def _():
                weights[n].start()

        for g in range(0, CHUNK, GROUP):
            rows = pl.ds(pl.multiple_of(i * CHUNK + g, GROUP), GROUP)
            squares = jnp.zeros((GROUP, 128), F32)
            for c in range(0, D, 1024):
                wide = tv[rows, c : c + 1024].astype(F32)
                square = wide * wide
                for k in range(0, 1024, 128):
                    squares = squares + square[:, k : k + 128]
            meansq = jnp.sum(squares, axis=1, keepdims=True) * (1.0 / D)
            factor = lax.rsqrt(meansq + 1e-06)
            for c in range(0, D, 1024):
                wide = tv[rows, c : c + 1024].astype(F32)
                nv[rows, c : c + 1024] = (wide * factor * gain[:, c : c + 1024]).astype(BF)
        return 0

    def keep(i, _):
        store(i).start()
        return 0

    lax.fori_loop(0, chunks, chunk, 0)
    for n in range(AHEAD, D // DEPTH):
        weights[n].start()
    lax.fori_loop(0, chunks, keep, 0)
    residual[...] = tv[:, pl.ds(pl.multiple_of(lax.axis_index("tp") * COLS, COLS), COLS)]
    total[...] = jnp.broadcast_to(bias[...], total.shape)
    for n, k in enumerate(range(0, D, DEPTH)):
        weights[n].wait()
        total[...] += jnp.dot(nv[:, k : k + DEPTH], wv[k : k + DEPTH, :], preferred_element_type=F32)
    cosine, sine = angles(small[...], large[pl.ds(lax.axis_index("section"), 1), :])
    keys = turn(total[:, :HD], cosine, sine).astype(BF)
    values = total[:, HD:].astype(BF)
    for half, out in enumerate((first, second)):
        rows = slice(half * HALF, (half + 1) * HALF)
        out[:, :HD] = keys[rows]
        out[:, HD:] = values[rows]
    for i in range(chunks):
        store(i).wait()


def norm_kv(tokens, gain, weight, bias, small, large):
    half = jax.ShapeDtypeStruct((HALF, 2 * HD), BF)
    return pl.pallas_call(
        norm_kv_kernel,
        in_specs=[ANY, WHOLE, ANY, WHOLE, WHOLE, WHOLE],
        out_specs=[ANY] + [WHOLE] * 3,
        out_shape=[jax.ShapeDtypeStruct((ROWS, D), BF), half, half, jax.ShapeDtypeStruct((ROWS, COLS), BF)],
        scratch_shapes=[
            pltpu.VMEM((ROWS, D), BF),
            pltpu.VMEM((ROWS, D), BF),
            pltpu.VMEM((D, 2 * HD), BF),
            pltpu.VMEM((ROWS, 2 * HD), F32),
            pltpu.SemaphoreType.DMA((ROWS // CHUNK,)),
            pltpu.SemaphoreType.DMA((D // DEPTH,)),
            pltpu.SemaphoreType.DMA((ROWS // CHUNK,)),
        ],
        compiler_params=limit(NORM_LIMIT),
        cost_estimate=pl.CostEstimate(flops=2 * ROWS * D * 256, bytes_accessed=20 << 20, transcendentals=0),
        name="norm_kv",
    )(tokens, gain, weight, bias, small, large)


Q_DEPTH = 1024
Q_AHEAD = 2


def query_kernel(normed, weight, bias, small, large, out, nv, wv, total, sems):
    steps = D // Q_DEPTH
    at = lambda n: slice(n * Q_DEPTH, (n + 1) * Q_DEPTH)
    copies = []
    for n in range(steps):
        copies.append(
            (
                pltpu.make_async_copy(normed.at[:, at(n)], nv.at[n], sems.at[n, 0]),
                pltpu.make_async_copy(weight.at[at(n), :], wv.at[n], sems.at[n, 1]),
            )
        )
    begin = lambda n: [copy.start() for copy in copies[n]]
    for n in range(Q_AHEAD):
        begin(n)
    for n in range(steps):
        for copy in copies[n]:
            copy.wait()
        if n + Q_AHEAD < steps:
            begin(n + Q_AHEAD)
        product = jnp.dot(nv[n], wv[n], preferred_element_type=F32)
        if n == 0:
            total[...] = product + bias[...]
        else:
            total[...] += product
    cosine, sine = angles(small[...], large[pl.ds(lax.axis_index("section"), 1), :])
    for h in range(HEADS):
        value = turn(total[:, h * HD : (h + 1) * HD], cosine, sine).astype(BF)
        for n in range(ROWS // SHARE):
            start = (n * HEADS + h) * SHARE
            out[start : start + SHARE, :] = value[n * SHARE : (n + 1) * SHARE]


def query(normed, weight, bias, small, large):
    width = HEADS * HD
    steps = D // Q_DEPTH
    return pl.pallas_call(
        query_kernel,
        in_specs=[ANY, ANY, WHOLE, WHOLE, WHOLE],
        out_specs=WHOLE,
        out_shape=jax.ShapeDtypeStruct((HEADS * ROWS, HD), BF),
        scratch_shapes=[
            pltpu.VMEM((steps, ROWS, Q_DEPTH), BF),
            pltpu.VMEM((steps, Q_DEPTH, width), BF),
            pltpu.VMEM((ROWS, width), F32),
            pltpu.SemaphoreType.DMA((steps, 2)),
        ],
        compiler_params=limit(NORM_LIMIT),
        cost_estimate=pl.CostEstimate(flops=2 * ROWS * D * 512, bytes_accessed=16 << 20, transcendentals=0),
        name="query",
    )(normed, weight, bias, small, large)


def columns_kernel(w_out, mine, send, sems):
    core = lax.rem(lax.axis_index("tp"), 2)
    copies = []
    for n, (out, c) in enumerate(((send, 1 - core), (mine, core))):
        for y in range(SIDE):
            here = pl.ds(pl.multiple_of((2 * y + c) * COLS, COLS), COLS)
            copies.append(pltpu.make_async_copy(w_out.at[:, here], out.at[y], sems.at[n, y]))
    for copy in copies:
        copy.start()
    for copy in copies:
        copy.wait()


def columns(w_out):
    out = jax.ShapeDtypeStruct((SIDE, HEADS * HD, COLS), BF)
    return pl.pallas_call(
        columns_kernel,
        in_specs=[ANY],
        out_specs=[WHOLE] * 2,
        out_shape=[out] * 2,
        scratch_shapes=[pltpu.SemaphoreType.DMA((2, SIDE))],
        compiler_params=limit(40),
        cost_estimate=pl.CostEstimate(flops=0, bytes_accessed=16 << 20, transcendentals=0),
        name="columns",
    )(w_out)


TILE = 128
QROWS = HEADS * ROWS


def attend(queries, keys, values, acc, maxima, rows, mask=None, first=False):
    scores = lax.dot_general(queries, keys, (((1,), (1,)), ((), ())), preferred_element_type=F32)
    if mask is not None:
        scores = jnp.where(mask, scores, -1e30)
    highest = jnp.max(scores, axis=1, keepdims=True)
    if first:
        newest = jnp.broadcast_to(highest, (rows.size, HD))
    else:
        old = maxima[rows, :]
        newest = jnp.maximum(old, highest)
        rescale = jnp.exp2((old - newest) * LOG2_SCALE)
    maxima[rows, :] = newest
    weights = jnp.exp2(scores * LOG2_SCALE - newest[:, :1] * LOG2_SCALE).astype(BF)
    added = jnp.dot(weights, values, preferred_element_type=F32)
    if first:
        acc[rows, :] = added
    else:
        acc[rows, :HD] = acc[rows, :HD] * rescale + added[:, :HD]
        acc[rows, HD:] = acc[rows, HD:] * rescale + added[:, HD:]


def attend_kernel(plan, halves, diagonal, final, *refs):
    refs = list(refs)
    take = lambda n: [refs.pop(0) for _ in range(n)]
    (queries,) = take(1)
    begin = take(2)
    pieces = take(len(plan))
    placing = halves is not None
    if placing:
        (table,) = take(1)
        before = [] if diagonal else take(1)
    outs = take(1 if final else 2)
    if placing:
        (cache,) = take(1)
        block_sem = refs.pop()
    if final:
        keys, values, acc, maxima, sems = refs
    else:
        keys, values, sems = refs
        acc, maxima = outs
    count_rows = queries.shape[0]
    section = lax.axis_index("section")
    x, z = section // SIDE, section % SIDE
    count = jnp.int32(0)
    jobs = []
    for piece, offsets in zip(pieces, plan):
        for j, (dx, dz) in enumerate(offsets):
            source = lax.rem(x + dx, SIDE) * SIDE + lax.rem(z + dz, SIDE)
            needed = source < section
            here = pl.ds(j * HALF, HALF)
            there = pl.ds(pl.multiple_of(count * HALF, HALF), HALF)
            n = len(jobs)
            copies = (
                pltpu.make_async_copy(piece.at[here, :HD], keys.at[there, :], sems.at[n, 0]),
                pltpu.make_async_copy(piece.at[here, HD:], values.at[there, :HD], sems.at[n, 1]),
            )

            @pl.when(needed)
            def _():
                copies[0].start()
                copies[1].start()

            jobs.append((needed, copies))
            count = count + needed.astype(jnp.int32)
    if placing:
        cache[...] = jnp.zeros_like(cache) if diagonal else before[0][...]
        placed = jnp.int32(0)
        sources = [(piece, j * HALF, dx, dz, half)
                   for piece, offsets, half in zip(pieces, plan, halves)
                   for j, (dx, dz) in enumerate(offsets)]
        if diagonal:
            sources += [(begin[0], 0, 0, 0, 0), (begin[1], 0, 0, 0, 1)]
        for piece, row, dx, dz, half in sources:
            source = lax.rem(x + dx, SIDE) * SIDE + lax.rem(z + dz, SIDE)
            for rank in range(PAIR):
                slot = source * PAIR + rank
                inside = table[slot] - half * (HALF // BLOCK)
                found = (inside >= 0) & (inside < HALF // BLOCK)

                @pl.when(found)
                def _():
                    at = pl.ds(pl.multiple_of(row + inside * BLOCK, BLOCK), BLOCK)
                    pltpu.make_async_copy(piece.at[at, :], cache.at[slot], block_sem).start()

                placed = placed + found.astype(jnp.int32)
    values[:, HD:] = jnp.ones((values.shape[0], HD), BF)
    if diagonal:
        last = len(jobs) * HALF
        for half in range(2):
            rows = slice(last + half * HALF, last + (half + 1) * HALF)
            keys[rows, :] = begin[half][:, :HD]
            values[rows, :HD] = begin[half][:, HD:]
        for start in range(0, ROWS, TILE):
            shape = (TILE, start + TILE)
            mask = lax.broadcasted_iota(jnp.int32, shape, 1) <= start + lax.broadcasted_iota(jnp.int32, shape, 0)
            kd, vd = keys[last : last + start + TILE, :], values[last : last + start + TILE, :]
            for h in range(HEADS):
                rows = pl.ds((start // SHARE * HEADS + h) * SHARE + start % SHARE, TILE)
                attend(queries[rows, :], kd, vd, acc, maxima, rows, mask, True)
    else:
        acc[...] = begin[0][...]
        maxima[...] = begin[1][...]
    for needed, copies in jobs:
        @pl.when(needed)
        def _():
            copies[0].wait()
            copies[1].wait()

    def part(base, size):
        at = pl.ds(pl.multiple_of(base, HALF), size)
        kd, vd = keys[at, :], values[at, :]
        for start in range(0, count_rows, TILE):
            rows = pl.ds(start, TILE)
            attend(queries[rows, :], kd, vd, acc, maxima, rows)

    def whole(i, _):
        part(i * 4 * HALF, 4 * HALF)
        return 0

    lax.fori_loop(0, count // 4, whole, 0)
    left = lax.rem(count, 4)

    @pl.when(left >= 2)
    def _():
        part((count // 4) * 4 * HALF, 2 * HALF)

    @pl.when(lax.rem(left, 2) == 1)
    def _():
        part((count - 1) * HALF, HALF)

    if final:
        for h in range(HEADS):
            rows = slice(h * SHARE, (h + 1) * SHARE)
            outs[0][:, h * HD : (h + 1) * HD] = (acc[rows, :HD] / acc[rows, HD:]).astype(BF)
    if placing:
        def block(i, _):
            pltpu.make_async_copy(cache.at[0], cache.at[0], block_sem).wait()
            return 0

        lax.fori_loop(0, placed, block, 0)


def attention(queries, begin, pieces, plan, name, diagonal=False, share=None, table=None, cache=None, halves=None):
    subs = sum(len(p) for p in plan)
    final = share is not None
    rows = HEADS * SHARE if final else QROWS
    size = subs * HALF + (ROWS if diagonal else 0)
    state_shape = [jax.ShapeDtypeStruct((rows, 2 * HD), F32), jax.ShapeDtypeStruct((rows, HD), F32)]
    scratch = [pltpu.VMEM((size, HD), BF), pltpu.VMEM((size, 2 * HD), BF)]
    if final:
        scratch += [pltpu.VMEM(s.shape, s.dtype) for s in state_shape]
        out_shape = [jax.ShapeDtypeStruct((SHARE, HEADS * HD), BF)]
        at = lambda i: (share, 0)
        in_specs = [pl.BlockSpec((rows, HD), at), pl.BlockSpec((rows, 2 * HD), at), pl.BlockSpec((rows, HD), at)]
        grid = (1,)
        out_specs = [pl.BlockSpec((SHARE, HEADS * HD), lambda i: (0, 0))]
    else:
        out_shape = state_shape
        in_specs = [WHOLE] * 3
        grid = ()
        out_specs = [WHOLE] * 2
    in_specs = in_specs + [ANY] * len(pieces)
    args = [queries, *begin, *pieces]
    scratch.append(pltpu.SemaphoreType.DMA((subs, 2)))
    if table is not None:
        in_specs.append(pl.BlockSpec(memory_space=pltpu.SMEM))
        args.append(table)
        if cache is not None:
            in_specs.append(WHOLE)
            args.append(cache)
        out_shape = out_shape + [jax.ShapeDtypeStruct((SIDE * SIDE * PAIR, BLOCK, 2 * HD), BF)]
        out_specs = out_specs + [WHOLE]
        scratch.append(pltpu.SemaphoreType.DMA)
    return pl.pallas_call(
        functools.partial(attend_kernel, plan, halves, diagonal, final),
        grid=grid,
        in_specs=in_specs,
        out_specs=out_specs,
        out_shape=out_shape,
        scratch_shapes=scratch,
        compiler_params=limit(20),
        cost_estimate=pl.CostEstimate(
            flops=8 * rows * size * HD, bytes_accessed=8 << 20, transcendentals=rows * size
        ),
        name=name,
    )(*args)


def join_kernel(*refs):
    n = (len(refs) - 2) // 2
    for ins, out in ((refs[:n], refs[-2]), (refs[n : 2 * n], refs[-1])):
        for j, piece in enumerate(ins):
            out[j * HALF : (j + 1) * HALF, :] = piece[...]


def join(first, second):
    out = jax.ShapeDtypeStruct((len(first) * HALF, 2 * HD), BF)
    return pl.pallas_call(
        join_kernel,
        in_specs=[WHOLE] * (len(first) + len(second)),
        out_specs=[WHOLE] * 2,
        out_shape=[out] * 2,
        compiler_params=limit(8),
        cost_estimate=pl.CostEstimate(flops=0, bytes_accessed=2 << 20, transcendentals=0),
        name="join",
    )(*first, *second)


def cache_table(placement, section):
    owners = placement.reshape(SIDE * SIDE, ROWS // BLOCK)
    mine = owners == section
    before = jnp.arange(ROWS // BLOCK)[:, None] < jnp.arange(ROWS // BLOCK)[None, :]
    ranks = jnp.sum((mine[:, :, None] & before[None]).astype(jnp.int32), axis=1)
    hit = mine[:, None, :] & (ranks[:, None, :] == jnp.arange(PAIR)[None, :, None])
    number = jnp.arange(ROWS // BLOCK, dtype=jnp.int32) + 1
    return (jnp.sum(jnp.where(hit, number[None, None, :], 0), axis=-1) - 1).reshape(-1)


MID = SHARE // 2


def term(offset, own, other, w_own, w_other):
    y = lax.rem(lax.axis_index("tp") // 2 + offset, SIDE)
    product = jnp.dot(own[...], w_own[y], preferred_element_type=F32)
    return product + jnp.dot(other[...], w_other[y], preferred_element_type=F32)


def opposite_kernel(own, other, w_own, w_other, top, bottom):
    product = term(2, own, other, w_own, w_other)
    top[...] = product[:MID].astype(BF)
    bottom[...] = product[MID:].astype(BF)


def neighbour_kernel(own, other, w_own, w_other, from_below, from_above, up, down):
    product = term(1, own, other, w_own, w_other)
    up[:MID] = (product[:MID] + from_below[...].astype(F32)).astype(BF)
    up[MID:] = product[MID:].astype(BF)
    product = term(3, own, other, w_own, w_other)
    down[:MID] = product[:MID].astype(BF)
    down[MID:] = (product[MID:] + from_above[...].astype(F32)).astype(BF)


def home_kernel(own, other, w_own, w_other, tokens, out):
    out[...] = tokens[...].astype(F32) + term(0, own, other, w_own, w_other)


def finish_kernel(base, from_below, from_above, *refs):
    refs[-1][...] = (base[...] + from_below[...].astype(F32) + from_above[...].astype(F32)).astype(BF)


def project(kernel, args, out, name):
    return pl.pallas_call(
        kernel,
        in_specs=[WHOLE] * len(args),
        out_specs=[WHOLE] * len(out),
        out_shape=[jax.ShapeDtypeStruct(shape, dtype) for shape, dtype in out],
        compiler_params=limit(8),
        cost_estimate=pl.CostEstimate(
            flops=4 * SHARE * 512 * COLS * len(out), bytes_accessed=6 << 20, transcendentals=0
        ),
        name=name,
    )(*args)


def home(own, other, w_own, w_other, residual, share):
    return pl.pallas_call(
        home_kernel,
        grid=(1,),
        in_specs=[WHOLE] * 4 + [pl.BlockSpec((SHARE, COLS), lambda i: (share, 0))],
        out_specs=pl.BlockSpec((SHARE, COLS), lambda i: (0, 0)),
        out_shape=jax.ShapeDtypeStruct((SHARE, COLS), F32),
        compiler_params=limit(8),
        cost_estimate=pl.CostEstimate(flops=4 * SHARE * 512 * COLS, bytes_accessed=6 << 20, transcendentals=0),
        name="project_home",
    )(own, other, w_own, w_other, residual)


def finish(base, from_below, from_above, done, share):
    return pl.pallas_call(
        finish_kernel,
        grid=(1,),
        in_specs=[WHOLE] * 3 + [ANY] * len(done),
        out_specs=pl.BlockSpec((SHARE, COLS), lambda i: (share, 0)),
        out_shape=jax.ShapeDtypeStruct((ROWS, COLS), BF),
        input_output_aliases={3: 0} if done else {},
        compiler_params=limit(8),
        cost_estimate=pl.CostEstimate(flops=4 * SHARE * COLS, bytes_accessed=3 << 20, transcendentals=0),
        name="finish",
    )(base, from_below, from_above, *done)


def from_section(value, dx, dz):
    pairs = []
    for x in range(SIDE):
        for z in range(SIDE):
            pairs.append((((x + dx) % SIDE) * SIDE + (z + dz) % SIDE, x * SIDE + z))
    return lax.ppermute(value, "section", pairs)


def from_tp(value, dy, dc):
    pairs = []
    for y in range(SIDE):
        for c in range(2):
            pairs.append((((y + dy) % SIDE) * 2 + (c ^ dc), y * 2 + c))
    return lax.ppermute(value, "tp", pairs)


RING = (1, 3, 2)
ORDER = (0,) + RING


def per_device(tokens, gain, q_weight, q_bias, kv_weight, kv_bias, out_weight, placement):
    section = lax.axis_index("section")
    small, large = tables()
    table = cache_table(placement, section)
    normed, first, second, residual = norm_kv(tokens, gain[None, :], kv_weight, kv_bias[None, :], small, large)
    row_first = [from_section(first, 0, k) for k in RING]
    row_second = [from_section(second, k, 0) for k in RING]
    all_first, all_second = join([first, *row_first], [second, *row_second])
    normed, all_first, all_second = lax.optimization_barrier((normed, all_first, all_second))
    far_first = [from_section(all_first, k, 0) for k in RING]
    far_second = [from_section(all_second, 0, k) for k in RING]
    queries = query(normed, q_weight, q_bias[None, :], small, large)
    out_weight, queries = lax.optimization_barrier((out_weight, queries))
    w_own, w_send = columns(out_weight)
    w_other = from_tp(w_send, 0, 1)
    near = [[(0, k)] for k in RING] + [[(k, 0)] for k in RING]
    *state, cache = attention(
        queries,
        (first, second),
        row_first + row_second,
        near,
        "attention_near",
        diagonal=True,
        table=table,
        halves=[0] * 3 + [1] * 3,
    )
    far = [[(k, j) for j in ORDER] for k in RING], [[(j, k) for j in ORDER] for k in RING]
    *state, cache = attention(
        queries,
        state,
        far_first[:2] + far_second[:2],
        far[0][:2] + far[1][:2],
        "attention_far",
        table=table,
        cache=cache,
        halves=[0] * 2 + [1] * 2,
    )
    mixed = []
    for share in range(ROWS // SHARE):
        closing = share == ROWS // SHARE - 1
        own, *rest = attention(
            queries,
            state,
            far_first[2:] + far_second[2:],
            far[0][2:] + far[1][2:],
            "attention_last",
            share=share,
            table=table if closing else None,
            cache=cache if closing else None,
            halves=[0, 1] if closing else None,
        )
        terms = (own, from_tp(own, 0, 1), w_own, w_other)
        small_out, wide_out = ((MID, COLS), BF), ((SHARE, COLS), BF)
        top, bottom = project(opposite_kernel, terms, [small_out] * 2, "project_opposite")
        from_below, from_above = from_tp(top, 3, 0), from_tp(bottom, 1, 0)
        base = home(*terms, residual, share)
        up, down = project(
            neighbour_kernel, (*terms, from_below, from_above), [wide_out] * 2, "project_neighbours"
        )
        from_below, from_above = from_tp(up, 3, 0), from_tp(down, 1, 0)
        mixed = [finish(base, from_below, from_above, mixed, share)]
    return mixed[0], rest[0]


def solution(mesh):
    placed = (
        P("section", None),
        P(),
        P(None, "tp"),
        P("tp"),
        P(None, "tp"),
        P("tp"),
        P("tp", None),
        P(),
    )
    return jax.shard_map(
        per_device,
        mesh=mesh,
        in_specs=placed,
        out_specs=(P("section", "tp"), P("section", None, "tp")),
        check_vma=False,
    )
```

```python
import functools
import math

import jax
import jax.numpy as jnp
import numpy as np
from jax import lax
from jax.experimental import pallas as pl
from jax.experimental.pallas import tpu as pltpu
from jax.sharding import PartitionSpec as P

HD = 128
BLOCK = 16
SIDE = 4
HALF = 256
ROWS = 512
D = 8192
HEADS = 4
PAIR = 4
ROPE_BASE = 1000000.0
LOG2_SCALE = math.log2(math.e) / math.sqrt(HD)
SHARE = 256
COLS = 1024
limit = lambda mib: pltpu.CompilerParams(vmem_limit_bytes=mib * 1024 * 1024)
BF = jnp.bfloat16
F32 = jnp.float32
ANY = pl.BlockSpec(memory_space=pl.ANY)
WHOLE = pl.BlockSpec(memory_space=pltpu.VMEM)
FAR = pl.BlockSpec(memory_space=pltpu.HBM)


def tables():
    freq = ROPE_BASE ** (-(np.arange(HD // 2, dtype=np.float64) * 2.0 / HD))
    inner = np.arange(ROWS, dtype=np.float64)[:, None] * freq
    outer = ROWS * np.arange(SIDE * SIDE, dtype=np.float64)[:, None] * freq
    twice = lambda a: np.concatenate([a, a], -1)
    signed = lambda a: np.concatenate([-a, a], -1)
    small = np.concatenate([twice(np.cos(inner)), twice(np.sin(inner))], -1)
    large = np.concatenate(
        [twice(np.cos(outer)), twice(np.sin(outer)), signed(np.cos(outer)), signed(np.sin(outer))], -1
    )
    return small.astype(np.float32), large.astype(np.float32)


def angles(small, large):
    cos_r, sin_r = small[:, :HD], small[:, HD:]
    cos_s, sin_s = large[:, :HD], large[:, HD : 2 * HD]
    cos_g, sin_g = large[:, 2 * HD : 3 * HD], large[:, 3 * HD :]
    return cos_s * cos_r - sin_s * sin_r, sin_g * cos_r + cos_g * sin_r


def turn(value, cosine, sine):
    return value * cosine + pltpu.roll(value, HD // 2, 1) * sine


CHUNK = 64
GROUP = 32
DEPTH = 2048
AHEAD = 4
NORM_LIMIT = 56


def norm_kv_kernel(
    tokens, gain, weight, bias, small, large, w_out, factors, first, second, residual, w_send,
    tv, nv, wv, sv, total, st, sw, s_in, s_out
):
    chunks = ROWS // CHUNK
    rows_at = lambda i: pl.ds(pl.multiple_of(i * CHUNK, CHUNK), CHUNK)
    load = lambda i: pltpu.make_async_copy(tokens.at[rows_at(i), :], tv.at[rows_at(i), :], st.at[i])
    weights = [
        pltpu.make_async_copy(weight.at[k : k + DEPTH, :], wv.at[k : k + DEPTH, :], sw.at[k // DEPTH])
        for k in range(0, D, DEPTH)
    ]
    sibling = 1 - lax.rem(lax.axis_index("tp"), 2)
    fetches, sends = [], []
    for y in range(SIDE):
        here = pl.ds(pl.multiple_of((2 * y + sibling) * COLS, COLS), COLS)
        fetches.append(pltpu.make_async_copy(w_out.at[:, here], sv.at[y], s_in.at[y]))
        sends.append(pltpu.make_async_copy(sv.at[y], w_send.at[y], s_out.at[y]))
    for i in range(AHEAD):
        load(i).start()

    def chunk(i, _):
        load(i).wait()

        @pl.when(i < chunks - AHEAD)
        def _():
            load(i + AHEAD).start()

        for n in range(AHEAD):
            @pl.when(i == chunks - AHEAD + n)
            def _():
                weights[n].start()

        for g in range(0, CHUNK, GROUP):
            rows = pl.ds(pl.multiple_of(i * CHUNK + g, GROUP), GROUP)
            squares = jnp.zeros((GROUP, 128), F32)
            for c in range(0, D, 1024):
                wide = tv[rows, c : c + 1024].astype(F32)
                square = wide * wide
                for k in range(0, 1024, 128):
                    squares = squares + square[:, k : k + 128]
            meansq = jnp.sum(squares, axis=1, keepdims=True) * (1.0 / D)
            factor = lax.rsqrt(meansq + 1e-06)
            factors[rows, :] = jnp.broadcast_to(factor, (GROUP, 128))
            for c in range(0, D, 1024):
                wide = tv[rows, c : c + 1024].astype(F32)
                nv[rows, c : c + 1024] = (wide * factor * gain[:, c : c + 1024]).astype(BF)
        return 0

    lax.fori_loop(0, chunks, chunk, 0)
    for n in range(AHEAD, D // DEPTH):
        weights[n].start()
    for copy in fetches:
        copy.start()
    residual[...] = tv[:, pl.ds(pl.multiple_of(lax.axis_index("tp") * COLS, COLS), COLS)]
    total[...] = jnp.broadcast_to(bias[...], total.shape)
    for n, k in enumerate(range(0, D, DEPTH)):
        weights[n].wait()
        total[...] += jnp.dot(nv[:, k : k + DEPTH], wv[k : k + DEPTH, :], preferred_element_type=F32)
        fetches[n].wait()
        sends[n].start()
    cosine, sine = angles(small[...], large[pl.ds(lax.axis_index("section"), 1), :])
    keys = turn(total[:, :HD], cosine, sine).astype(BF)
    values = total[:, HD:].astype(BF)
    for half, out in enumerate((first, second)):
        rows = slice(half * HALF, (half + 1) * HALF)
        out[:, :HD] = keys[rows]
        out[:, HD:] = values[rows]
    for copy in sends:
        copy.wait()


def norm_kv(tokens, gain, weight, bias, small, large, w_out):
    half = jax.ShapeDtypeStruct((HALF, 2 * HD), BF)
    return pl.pallas_call(
        norm_kv_kernel,
        in_specs=[ANY, WHOLE, ANY, WHOLE, WHOLE, WHOLE, ANY],
        out_specs=[WHOLE] * 4 + [ANY],
        out_shape=[
            jax.ShapeDtypeStruct((ROWS, 128), F32),
            half,
            half,
            jax.ShapeDtypeStruct((ROWS, COLS), BF),
            jax.ShapeDtypeStruct((SIDE, HEADS * HD, COLS), BF),
        ],
        scratch_shapes=[
            pltpu.VMEM((ROWS, D), BF),
            pltpu.VMEM((ROWS, D), BF),
            pltpu.VMEM((D, 2 * HD), BF),
            pltpu.VMEM((SIDE, HEADS * HD, COLS), BF),
            pltpu.VMEM((ROWS, 2 * HD), F32),
            pltpu.SemaphoreType.DMA((ROWS // CHUNK,)),
            pltpu.SemaphoreType.DMA((D // DEPTH,)),
            pltpu.SemaphoreType.DMA((SIDE,)),
            pltpu.SemaphoreType.DMA((SIDE,)),
        ],
        compiler_params=limit(NORM_LIMIT),
        cost_estimate=pl.CostEstimate(flops=2 * ROWS * D * 256, bytes_accessed=20 << 20, transcendentals=0),
        name="norm_kv",
    )(tokens, gain, weight, bias, small, large, w_out)


Q_DEPTH = 1024
Q_AHEAD = 2


def query_kernel(tokens, factors, gain, weight, bias, small, large, out, tv, nv, wv, total, sems):
    steps = D // Q_DEPTH
    copies = []
    for n in range(steps):
        at = slice(n * Q_DEPTH, (n + 1) * Q_DEPTH)
        copies.append(
            (
                pltpu.make_async_copy(tokens.at[:, at], tv.at[n], sems.at[n, 0]),
                pltpu.make_async_copy(weight.at[at, :], wv.at[n], sems.at[n, 1]),
            )
        )
    begin = lambda n: [copy.start() for copy in copies[n]]
    for n in range(Q_AHEAD):
        begin(n)
    total[...] = jnp.broadcast_to(bias[...], total.shape)

    def scale(n):
        for copy in copies[n]:
            copy.wait()
        if n + Q_AHEAD < steps:
            begin(n + Q_AHEAD)
        for r in range(0, ROWS, 128):
            factor = factors[r : r + 128, :1]
            at = slice(n * Q_DEPTH, (n + 1) * Q_DEPTH)
            nv[n, r : r + 128, :] = (tv[n, r : r + 128, :].astype(F32) * factor * gain[:, at]).astype(BF)

    scale(0)
    for n in range(steps):
        if n + 1 < steps:
            scale(n + 1)
        total[...] += jnp.dot(nv[n], wv[n], preferred_element_type=F32)
    cosine, sine = angles(small[...], large[pl.ds(lax.axis_index("section"), 1), :])
    for h in range(HEADS):
        value = turn(total[:, h * HD : (h + 1) * HD], cosine, sine).astype(BF)
        for n in range(ROWS // SHARE):
            start = (n * HEADS + h) * SHARE
            out[start : start + SHARE, :] = value[n * SHARE : (n + 1) * SHARE]


def query(tokens, factors, gain, weight, bias, small, large):
    width = HEADS * HD
    steps = D // Q_DEPTH
    return pl.pallas_call(
        query_kernel,
        in_specs=[ANY, WHOLE, WHOLE, ANY, WHOLE, WHOLE, WHOLE],
        out_specs=WHOLE,
        out_shape=jax.ShapeDtypeStruct((HEADS * ROWS, HD), BF),
        scratch_shapes=[
            pltpu.VMEM((steps, ROWS, Q_DEPTH), BF),
            pltpu.VMEM((steps, ROWS, Q_DEPTH), BF),
            pltpu.VMEM((steps, Q_DEPTH, width), BF),
            pltpu.VMEM((ROWS, width), F32),
            pltpu.SemaphoreType.DMA((steps, 2)),
        ],
        compiler_params=limit(56),
        cost_estimate=pl.CostEstimate(flops=2 * ROWS * D * 512, bytes_accessed=16 << 20, transcendentals=0),
        name="query",
    )(tokens, factors, gain, weight, bias, small, large)


TILE = 128
QROWS = HEADS * ROWS


def attend(queries, keys, values, acc, maxima, rows, mask=None, first=False):
    scores = lax.dot_general(queries, keys, (((1,), (1,)), ((), ())), preferred_element_type=F32)
    if mask is not None:
        scores = jnp.where(mask, scores, -1e30)
    highest = jnp.max(scores, axis=1, keepdims=True)
    if first:
        newest = jnp.broadcast_to(highest, (rows.size, HD))
    else:
        old = maxima[rows, :]
        newest = jnp.maximum(old, highest)
        rescale = jnp.exp2((old - newest) * LOG2_SCALE)
    maxima[rows, :] = newest
    weights = jnp.exp2(scores * LOG2_SCALE - newest[:, :1] * LOG2_SCALE).astype(BF)
    added = jnp.dot(weights, values, preferred_element_type=F32)
    if first:
        acc[rows, :] = added
    else:
        acc[rows, :HD] = acc[rows, :HD] * rescale + added[:, :HD]
        acc[rows, HD:] = acc[rows, HD:] * rescale + added[:, HD:]


def attend_kernel(plan, halves, diagonal, final, *refs):
    refs = list(refs)
    take = lambda n: [refs.pop(0) for _ in range(n)]
    (queries,) = take(1)
    begin = take(2)
    pieces = take(len(plan))
    placing = halves is not None
    if placing:
        (table,) = take(1)
        before = [] if diagonal else take(1)
    outs = take(1 if final else 2)
    if placing:
        (cache,) = take(1)
        block_sem = refs.pop()
    if final:
        keys, values, acc, maxima, sems = refs
    else:
        keys, values, sems = refs
        acc, maxima = outs
    count_rows = queries.shape[0]
    section = lax.axis_index("section")
    x, z = section // SIDE, section % SIDE
    count = jnp.int32(0)
    jobs = []
    for piece, offsets in zip(pieces, plan):
        for j, (dx, dz) in enumerate(offsets):
            source = lax.rem(x + dx, SIDE) * SIDE + lax.rem(z + dz, SIDE)
            needed = source < section
            here = pl.ds(j * HALF, HALF)
            there = pl.ds(pl.multiple_of(count * HALF, HALF), HALF)
            n = len(jobs)
            copies = (
                pltpu.make_async_copy(piece.at[here, :HD], keys.at[there, :], sems.at[n, 0]),
                pltpu.make_async_copy(piece.at[here, HD:], values.at[there, :HD], sems.at[n, 1]),
            )

            @pl.when(needed)
            def _():
                copies[0].start()
                copies[1].start()

            jobs.append((needed, copies))
            count = count + needed.astype(jnp.int32)
    if placing:
        cache[...] = jnp.zeros_like(cache) if diagonal else before[0][...]
        placed = jnp.int32(0)
        sources = [(piece, j * HALF, dx, dz, half)
                   for piece, offsets, half in zip(pieces, plan, halves)
                   for j, (dx, dz) in enumerate(offsets)]
        if diagonal:
            sources += [(begin[0], 0, 0, 0, 0), (begin[1], 0, 0, 0, 1)]
        for piece, row, dx, dz, half in sources:
            source = lax.rem(x + dx, SIDE) * SIDE + lax.rem(z + dz, SIDE)
            for rank in range(PAIR):
                slot = source * PAIR + rank
                inside = table[slot] - half * (HALF // BLOCK)
                found = (inside >= 0) & (inside < HALF // BLOCK)

                @pl.when(found)
                def _():
                    at = pl.ds(pl.multiple_of(row + inside * BLOCK, BLOCK), BLOCK)
                    pltpu.make_async_copy(piece.at[at, :], cache.at[slot], block_sem).start()

                placed = placed + found.astype(jnp.int32)
    values[:, HD:] = jnp.ones((values.shape[0], HD), BF)
    if diagonal:
        last = len(jobs) * HALF
        for half in range(2):
            rows = slice(last + half * HALF, last + (half + 1) * HALF)
            keys[rows, :] = begin[half][:, :HD]
            values[rows, :HD] = begin[half][:, HD:]
        for start in range(0, ROWS, TILE):
            shape = (TILE, start + TILE)
            mask = lax.broadcasted_iota(jnp.int32, shape, 1) <= start + lax.broadcasted_iota(jnp.int32, shape, 0)
            kd, vd = keys[last : last + start + TILE, :], values[last : last + start + TILE, :]
            for h in range(HEADS):
                rows = pl.ds((start // SHARE * HEADS + h) * SHARE + start % SHARE, TILE)
                attend(queries[rows, :], kd, vd, acc, maxima, rows, mask, True)
    else:
        acc[...] = begin[0][...]
        maxima[...] = begin[1][...]
    for needed, copies in jobs:
        @pl.when(needed)
        def _():
            copies[0].wait()
            copies[1].wait()

    def part(base, size):
        at = pl.ds(pl.multiple_of(base, HALF), size)
        kd, vd = keys[at, :], values[at, :]
        for start in range(0, count_rows, TILE):
            rows = pl.ds(start, TILE)
            attend(queries[rows, :], kd, vd, acc, maxima, rows)

    def whole(i, _):
        part(i * 4 * HALF, 4 * HALF)
        return 0

    lax.fori_loop(0, count // 4, whole, 0)
    left = lax.rem(count, 4)

    @pl.when(left >= 2)
    def _():
        part((count // 4) * 4 * HALF, 2 * HALF)

    @pl.when(lax.rem(left, 2) == 1)
    def _():
        part((count - 1) * HALF, HALF)

    if final:
        for h in range(HEADS):
            rows = slice(h * SHARE, (h + 1) * SHARE)
            outs[0][:, h * HD : (h + 1) * HD] = (acc[rows, :HD] / acc[rows, HD:]).astype(BF)
    if placing:
        def block(i, _):
            pltpu.make_async_copy(cache.at[0], cache.at[0], block_sem).wait()
            return 0

        lax.fori_loop(0, placed, block, 0)


def attention(queries, begin, pieces, plan, name, diagonal=False, share=None, table=None, cache=None, halves=None):
    subs = sum(len(p) for p in plan)
    final = share is not None
    rows = HEADS * SHARE if final else QROWS
    size = subs * HALF + (ROWS if diagonal else 0)
    state_shape = [jax.ShapeDtypeStruct((rows, 2 * HD), F32), jax.ShapeDtypeStruct((rows, HD), F32)]
    scratch = [pltpu.VMEM((size, HD), BF), pltpu.VMEM((size, 2 * HD), BF)]
    if final:
        scratch += [pltpu.VMEM(s.shape, s.dtype) for s in state_shape]
        out_shape = [jax.ShapeDtypeStruct((SHARE, HEADS * HD), BF)]
        at = lambda i: (share, 0)
        in_specs = [pl.BlockSpec((rows, HD), at), pl.BlockSpec((rows, 2 * HD), at), pl.BlockSpec((rows, HD), at)]
        grid = (1,)
        out_specs = [pl.BlockSpec((SHARE, HEADS * HD), lambda i: (0, 0))]
    else:
        out_shape = state_shape
        in_specs = [WHOLE] * 3
        grid = ()
        out_specs = [WHOLE] * 2
    in_specs = in_specs + [ANY] * len(pieces)
    args = [queries, *begin, *pieces]
    scratch.append(pltpu.SemaphoreType.DMA((subs, 2)))
    if table is not None:
        in_specs.append(pl.BlockSpec(memory_space=pltpu.SMEM))
        args.append(table)
        if cache is not None:
            in_specs.append(WHOLE)
            args.append(cache)
        out_shape = out_shape + [jax.ShapeDtypeStruct((SIDE * SIDE * PAIR, BLOCK, 2 * HD), BF)]
        out_specs = out_specs + [WHOLE]
        scratch.append(pltpu.SemaphoreType.DMA)
    return pl.pallas_call(
        functools.partial(attend_kernel, plan, halves, diagonal, final),
        grid=grid,
        in_specs=in_specs,
        out_specs=out_specs,
        out_shape=out_shape,
        scratch_shapes=scratch,
        compiler_params=limit(20),
        cost_estimate=pl.CostEstimate(
            flops=8 * rows * size * HD, bytes_accessed=8 << 20, transcendentals=rows * size
        ),
        name=name,
    )(*args)


def join_kernel(*refs):
    n = (len(refs) - 2) // 2
    for ins, out in ((refs[:n], refs[-2]), (refs[n : 2 * n], refs[-1])):
        for j, piece in enumerate(ins):
            out[j * HALF : (j + 1) * HALF, :] = piece[...]


def join(first, second):
    out = jax.ShapeDtypeStruct((len(first) * HALF, 2 * HD), BF)
    return pl.pallas_call(
        join_kernel,
        in_specs=[WHOLE] * (len(first) + len(second)),
        out_specs=[WHOLE] * 2,
        out_shape=[out] * 2,
        compiler_params=limit(8),
        cost_estimate=pl.CostEstimate(flops=0, bytes_accessed=2 << 20, transcendentals=0),
        name="join",
    )(*first, *second)


def cache_kernel(places, table, *refs):
    pieces, (out, zeros, sem) = refs[:-3], refs[-3:]
    zeros[...] = jnp.zeros_like(zeros)
    section = lax.axis_index("section")
    x, z = section // SIDE, section % SIDE
    for dx in range(SIDE):
        for dz in range(SIDE):
            source = lax.rem(x + dx, SIDE) * SIDE + lax.rem(z + dz, SIDE)
            for rank in range(PAIR):
                slot = source * PAIR + rank
                block = table[slot]

                @pl.when(block < 0)
                def _():
                    pltpu.make_async_copy(zeros, out.at[slot], sem).start()

                for half in range(2):
                    piece, row = places[half][(dx, dz)]
                    inside = block - half * (HALF // BLOCK)

                    @pl.when((inside >= 0) & (inside < HALF // BLOCK))
                    def _():
                        at = pl.ds(pl.multiple_of(row + inside * BLOCK, BLOCK), BLOCK)
                        pltpu.make_async_copy(pieces[piece].at[at, :], out.at[slot], sem).start()

    pltpu.make_async_copy(out, out, sem).wait()


def cache_table(placement, section):
    owners = placement.reshape(SIDE * SIDE, ROWS // BLOCK)
    mine = owners == section
    before = jnp.arange(ROWS // BLOCK)[:, None] < jnp.arange(ROWS // BLOCK)[None, :]
    ranks = jnp.sum((mine[:, :, None] & before[None]).astype(jnp.int32), axis=1)
    hit = mine[:, None, :] & (ranks[:, None, :] == jnp.arange(PAIR)[None, :, None])
    number = jnp.arange(ROWS // BLOCK, dtype=jnp.int32) + 1
    return (jnp.sum(jnp.where(hit, number[None, None, :], 0), axis=-1) - 1).reshape(-1)


def decode(places, table, pieces):
    slots = SIDE * SIDE * PAIR
    return pl.pallas_call(
        functools.partial(cache_kernel, places),
        in_specs=[pl.BlockSpec(memory_space=pltpu.SMEM)] + [ANY] * len(pieces),
        out_specs=WHOLE,
        out_shape=jax.ShapeDtypeStruct((slots, BLOCK, 2 * HD), BF),
        scratch_shapes=[pltpu.VMEM((BLOCK, 2 * HD), BF), pltpu.SemaphoreType.DMA],
        compiler_params=limit(16),
        cost_estimate=pl.CostEstimate(flops=0, bytes_accessed=4 << 20, transcendentals=0),
        name="decode_cache",
    )(table, *pieces)


MID = SHARE // 2
PROJECT_LIMIT = 50


def blocks_of(offsets, w_out, w_other, wv, sems):
    tp = lax.axis_index("tp")
    copies = []
    for n, offset in enumerate(offsets):
        y = lax.rem(tp // 2 + offset, SIDE)
        here = pl.ds(pl.multiple_of((2 * y + lax.rem(tp, 2)) * COLS, COLS), COLS)
        copies.append(pltpu.make_async_copy(w_out.at[:, here], wv.at[n, 0], sems.at[n, 0]))
        copies.append(pltpu.make_async_copy(w_other.at[y], wv.at[n, 1], sems.at[n, 1]))
    for copy in copies:
        copy.start()
    return copies


def term(n, copies, own, other, wv):
    copies[2 * n].wait()
    product = jnp.dot(own[...], wv[n, 0], preferred_element_type=F32)
    copies[2 * n + 1].wait()
    return product + jnp.dot(other[...], wv[n, 1], preferred_element_type=F32)


def opposite_kernel(own, other, w_out, w_other, top, bottom, wv, sems):
    copies = blocks_of((2,), w_out, w_other, wv, sems)
    product = term(0, copies, own, other, wv)
    top[...] = product[:MID].astype(BF)
    bottom[...] = product[MID:].astype(BF)


def neighbour_kernel(own, other, w_out, w_other, from_below, from_above, up, down, wv, sems):
    copies = blocks_of((1, 3), w_out, w_other, wv, sems)
    product = term(0, copies, own, other, wv)
    up[:MID] = (product[:MID] + from_below[...].astype(F32)).astype(BF)
    up[MID:] = product[MID:].astype(BF)
    product = term(1, copies, own, other, wv)
    down[:MID] = product[:MID].astype(BF)
    down[MID:] = (product[MID:] + from_above[...].astype(F32)).astype(BF)


def home_kernel(share, own, other, w_out, w_other, residual, out, wv, sems):
    copies = blocks_of((0,), w_out, w_other, wv, sems)
    rows = slice(share * SHARE, (share + 1) * SHARE)
    out[...] = residual[rows, :].astype(F32) + term(0, copies, own, other, wv)


def project(kernel, targets, terms, extra, out, name):
    return pl.pallas_call(
        kernel,
        in_specs=[WHOLE, WHOLE, ANY, ANY] + [WHOLE] * len(extra),
        out_specs=[WHOLE] * len(out),
        out_shape=[jax.ShapeDtypeStruct(shape, dtype) for shape, dtype in out],
        scratch_shapes=[
            pltpu.VMEM((targets, 2, HEADS * HD, COLS), BF),
            pltpu.SemaphoreType.DMA((targets, 2)),
        ],
        compiler_params=limit(PROJECT_LIMIT),
        cost_estimate=pl.CostEstimate(
            flops=4 * SHARE * 512 * COLS * targets, bytes_accessed=4 << 20, transcendentals=0
        ),
        name=name,
    )(*terms, *extra)


def finish_kernel(base, from_below, from_above, *refs):
    refs[-1][...] = (base[...] + from_below[...].astype(F32) + from_above[...].astype(F32)).astype(BF)


def finish(base, from_below, from_above, done, share):
    return pl.pallas_call(
        finish_kernel,
        grid=(1,),
        in_specs=[WHOLE] * 3 + [ANY] * len(done),
        out_specs=pl.BlockSpec((SHARE, COLS), lambda i: (share, 0)),
        out_shape=jax.ShapeDtypeStruct((ROWS, COLS), BF),
        input_output_aliases={3: 0} if done else {},
        compiler_params=limit(8),
        cost_estimate=pl.CostEstimate(flops=4 * SHARE * COLS, bytes_accessed=3 << 20, transcendentals=0),
        name="finish",
    )(base, from_below, from_above, *done)


def from_section(value, dx, dz):
    pairs = []
    for x in range(SIDE):
        for z in range(SIDE):
            pairs.append((((x + dx) % SIDE) * SIDE + (z + dz) % SIDE, x * SIDE + z))
    return lax.ppermute(value, "section", pairs)


def from_tp(value, dy, dc):
    pairs = []
    for y in range(SIDE):
        for c in range(2):
            pairs.append((((y + dy) % SIDE) * 2 + (c ^ dc), y * 2 + c))
    return lax.ppermute(value, "tp", pairs)


RING = (1, 3, 2)
ORDER = (0,) + RING


def per_device(tokens, gain, q_weight, q_bias, kv_weight, kv_bias, out_weight, placement):
    section = lax.axis_index("section")
    small, large = tables()
    factors, first, second, residual, w_send = norm_kv(
        tokens, gain[None, :], kv_weight, kv_bias[None, :], small, large, out_weight
    )
    w_other = from_tp(w_send, 0, 1)
    row_first = [from_section(first, 0, k) for k in RING]
    row_second = [from_section(second, k, 0) for k in RING]
    factors, row_first[0] = lax.optimization_barrier((factors, row_first[0]))
    queries = query(tokens, factors, gain[None, :], q_weight, q_bias[None, :], small, large)
    row_first[1], w_other, queries = lax.optimization_barrier((row_first[1], w_other, queries))
    all_first, all_second = join([first, *row_first], [second, *row_second])
    far_first = [from_section(all_first, k, 0) for k in RING]
    far_second = [from_section(all_second, 0, k) for k in RING]
    near = [[(0, k)] for k in RING] + [[(k, 0)] for k in RING]
    state = attention(queries, (first, second), row_first + row_second, near, "attention_near", diagonal=True)
    far = [[(k, j) for j in ORDER] for k in RING], [[(j, k) for j in ORDER] for k in RING]
    state = attention(
        queries, state, far_first[:2] + far_second[:2], far[0][:2] + far[1][:2], "attention_far"
    )
    shares = []
    for share in range(ROWS // SHARE):
        shares += attention(
            queries, state, far_first[2:] + far_second[2:], far[0][2:] + far[1][2:], "attention_last", share=share
        )
    mixed = []
    for share, own in enumerate(shares):
        terms = (own, from_tp(own, 0, 1), out_weight, w_other)
        top, bottom = project(opposite_kernel, 1, terms, [], [((MID, COLS), BF)] * 2, "project_opposite")
        from_below, from_above = from_tp(top, 3, 0), from_tp(bottom, 1, 0)
        up, down = project(
            neighbour_kernel, 2, terms, [from_below, from_above], [((SHARE, COLS), BF)] * 2, "project_neighbours"
        )
        from_below, from_above = from_tp(up, 3, 0), from_tp(down, 1, 0)
        (base,) = project(
            functools.partial(home_kernel, share), 1, terms, [residual], [((SHARE, COLS), F32)], "project_home"
        )
        mixed = [finish(base, from_below, from_above, mixed, share)]
    pieces = [first, second] + row_first + row_second + far_first + far_second
    places = [{(0, 0): (0, 0)}, {(0, 0): (1, 0)}]
    for i, k in enumerate(RING):
        places[0][(0, k)] = (2 + i, 0)
        places[1][(k, 0)] = (5 + i, 0)
        for n, j in enumerate(ORDER):
            places[0][(k, j)] = (8 + i, n * HALF)
            places[1][(j, k)] = (11 + i, n * HALF)
    placement, base = lax.optimization_barrier((placement, base))
    decode_cache = decode(places, cache_table(placement, section), pieces)
    return mixed[0], decode_cache


def solution(mesh):
    placed = (
        P("section", None),
        P(),
        P(None, "tp"),
        P("tp"),
        P(None, "tp"),
        P("tp"),
        P("tp", None),
        P(),
    )
    return jax.shard_map(
        per_device,
        mesh=mesh,
        in_specs=placed,
        out_specs=(P("section", "tp"), P("section", None, "tp")),
        check_vma=False,
    )
```

```python
import functools
import math

import jax
import jax.numpy as jnp
import numpy as np
from jax import lax
from jax.experimental import pallas as pl
from jax.experimental.pallas import tpu as pltpu
from jax.sharding import PartitionSpec as P

HD = 128
BLOCK = 16
SIDE = 4
HALF = 256
ROWS = 512
D = 8192
HEADS = 4
PAIR = 4
ROPE_BASE = 1000000.0
LOG2_SCALE = math.log2(math.e) / math.sqrt(HD)
SHARE = 256
COLS = 1024
limit = lambda mib: pltpu.CompilerParams(vmem_limit_bytes=mib * 1024 * 1024)
BF = jnp.bfloat16
F32 = jnp.float32
ANY = pl.BlockSpec(memory_space=pl.ANY)
WHOLE = pl.BlockSpec(memory_space=pltpu.VMEM)
FAR = pl.BlockSpec(memory_space=pltpu.HBM)


def tables():
    freq = ROPE_BASE ** (-(np.arange(HD // 2, dtype=np.float64) * 2.0 / HD))
    inner = np.arange(ROWS, dtype=np.float64)[:, None] * freq
    outer = ROWS * np.arange(SIDE * SIDE, dtype=np.float64)[:, None] * freq
    twice = lambda a: np.concatenate([a, a], -1)
    signed = lambda a: np.concatenate([-a, a], -1)
    small = np.concatenate([twice(np.cos(inner)), twice(np.sin(inner))], -1)
    large = np.concatenate(
        [twice(np.cos(outer)), twice(np.sin(outer)), signed(np.cos(outer)), signed(np.sin(outer))], -1
    )
    return small.astype(np.float32), large.astype(np.float32)


def angles(small, large):
    cos_r, sin_r = small[:, :HD], small[:, HD:]
    cos_s, sin_s = large[:, :HD], large[:, HD : 2 * HD]
    cos_g, sin_g = large[:, 2 * HD : 3 * HD], large[:, 3 * HD :]
    return cos_s * cos_r - sin_s * sin_r, sin_g * cos_r + cos_g * sin_r


def turn(value, cosine, sine):
    return value * cosine + pltpu.roll(value, HD // 2, 1) * sine


CHUNK = 64
GROUP = 32
DEPTH = 2048
AHEAD = 4
NORM_LIMIT = 56


def norm_kv_kernel(
    tokens, gain, weight, bias, small, large, w_out, factors, first, second, residual, w_send,
    tv, nv, wv, sv, total, st, sw, s_in, s_out
):
    chunks = ROWS // CHUNK
    rows_at = lambda i: pl.ds(pl.multiple_of(i * CHUNK, CHUNK), CHUNK)
    load = lambda i: pltpu.make_async_copy(tokens.at[rows_at(i), :], tv.at[rows_at(i), :], st.at[i])
    weights = [
        pltpu.make_async_copy(weight.at[k : k + DEPTH, :], wv.at[k : k + DEPTH, :], sw.at[k // DEPTH])
        for k in range(0, D, DEPTH)
    ]
    sibling = 1 - lax.rem(lax.axis_index("tp"), 2)
    fetches, sends = [], []
    for y in range(SIDE):
        here = pl.ds(pl.multiple_of((2 * y + sibling) * COLS, COLS), COLS)
        fetches.append(pltpu.make_async_copy(w_out.at[:, here], sv.at[y], s_in.at[y]))
        sends.append(pltpu.make_async_copy(sv.at[y], w_send.at[y], s_out.at[y]))
    for i in range(AHEAD):
        load(i).start()

    def chunk(i, _):
        load(i).wait()

        @pl.when(i < chunks - AHEAD)
        def _():
            load(i + AHEAD).start()

        for n in range(AHEAD):
            @pl.when(i == chunks - AHEAD + n)
            def _():
                weights[n].start()

        for g in range(0, CHUNK, GROUP):
            rows = pl.ds(pl.multiple_of(i * CHUNK + g, GROUP), GROUP)
            squares = jnp.zeros((GROUP, 128), F32)
            for c in range(0, D, 1024):
                wide = tv[rows, c : c + 1024].astype(F32)
                square = wide * wide
                for k in range(0, 1024, 128):
                    squares = squares + square[:, k : k + 128]
            meansq = jnp.sum(squares, axis=1, keepdims=True) * (1.0 / D)
            factor = lax.rsqrt(meansq + 1e-06)
            factors[rows, :] = jnp.broadcast_to(factor, (GROUP, 128))
            for c in range(0, D, 1024):
                wide = tv[rows, c : c + 1024].astype(F32)
                nv[rows, c : c + 1024] = (wide * factor * gain[:, c : c + 1024]).astype(BF)
        return 0

    lax.fori_loop(0, chunks, chunk, 0)
    for n in range(AHEAD, D // DEPTH):
        weights[n].start()
    for copy in fetches:
        copy.start()
    residual[...] = tv[:, pl.ds(pl.multiple_of(lax.axis_index("tp") * COLS, COLS), COLS)]
    total[...] = jnp.broadcast_to(bias[...], total.shape)
    for n, k in enumerate(range(0, D, DEPTH)):
        weights[n].wait()
        total[...] += jnp.dot(nv[:, k : k + DEPTH], wv[k : k + DEPTH, :], preferred_element_type=F32)
        fetches[n].wait()
        sends[n].start()
    cosine, sine = angles(small[...], large[pl.ds(lax.axis_index("section"), 1), :])
    keys = turn(total[:, :HD], cosine, sine).astype(BF)
    values = total[:, HD:].astype(BF)
    for half, out in enumerate((first, second)):
        rows = slice(half * HALF, (half + 1) * HALF)
        out[:, :HD] = keys[rows]
        out[:, HD:] = values[rows]
    for copy in sends:
        copy.wait()


def norm_kv(tokens, gain, weight, bias, small, large, w_out):
    half = jax.ShapeDtypeStruct((HALF, 2 * HD), BF)
    return pl.pallas_call(
        norm_kv_kernel,
        in_specs=[ANY, WHOLE, ANY, WHOLE, WHOLE, WHOLE, ANY],
        out_specs=[WHOLE] * 4 + [ANY],
        out_shape=[
            jax.ShapeDtypeStruct((ROWS, 128), F32),
            half,
            half,
            jax.ShapeDtypeStruct((ROWS, COLS), BF),
            jax.ShapeDtypeStruct((SIDE, HEADS * HD, COLS), BF),
        ],
        scratch_shapes=[
            pltpu.VMEM((ROWS, D), BF),
            pltpu.VMEM((ROWS, D), BF),
            pltpu.VMEM((D, 2 * HD), BF),
            pltpu.VMEM((SIDE, HEADS * HD, COLS), BF),
            pltpu.VMEM((ROWS, 2 * HD), F32),
            pltpu.SemaphoreType.DMA((ROWS // CHUNK,)),
            pltpu.SemaphoreType.DMA((D // DEPTH,)),
            pltpu.SemaphoreType.DMA((SIDE,)),
            pltpu.SemaphoreType.DMA((SIDE,)),
        ],
        compiler_params=limit(NORM_LIMIT),
        cost_estimate=pl.CostEstimate(flops=2 * ROWS * D * 256, bytes_accessed=20 << 20, transcendentals=0),
        name="norm_kv",
    )(tokens, gain, weight, bias, small, large, w_out)


Q_DEPTH = 1024
Q_AHEAD = 2


def query_kernel(
    tokens, factors, gain, weight, bias, small, large, w_out, out, w_own, tv, nv, wv, sv, total, sems, s_in, s_out
):
    steps = D // Q_DEPTH
    copies = []
    for n in range(steps):
        at = slice(n * Q_DEPTH, (n + 1) * Q_DEPTH)
        copies.append(
            (
                pltpu.make_async_copy(tokens.at[:, at], tv.at[n], sems.at[n, 0]),
                pltpu.make_async_copy(weight.at[at, :], wv.at[n], sems.at[n, 1]),
            )
        )
    core = lax.rem(lax.axis_index("tp"), 2)
    fetches, keeps = [], []
    for y in range(SIDE):
        here = pl.ds(pl.multiple_of((2 * y + core) * COLS, COLS), COLS)
        fetches.append(pltpu.make_async_copy(w_out.at[:, here], sv.at[y], s_in.at[y]))
        keeps.append(pltpu.make_async_copy(sv.at[y], w_own.at[y], s_out.at[y]))
    begin = lambda n: [copy.start() for copy in copies[n]]
    for n in range(Q_AHEAD):
        begin(n)
    total[...] = jnp.broadcast_to(bias[...], total.shape)

    def scale(n):
        for copy in copies[n]:
            copy.wait()
        if n + Q_AHEAD < steps:
            begin(n + Q_AHEAD)
        for r in range(0, ROWS, 128):
            factor = factors[r : r + 128, :1]
            at = slice(n * Q_DEPTH, (n + 1) * Q_DEPTH)
            nv[n, r : r + 128, :] = (tv[n, r : r + 128, :].astype(F32) * factor * gain[:, at]).astype(BF)

    scale(0)
    for n in range(steps):
        if n + 1 < steps:
            scale(n + 1)
        if n < SIDE:
            fetches[n].start()
        else:
            fetches[n - SIDE].wait()
            keeps[n - SIDE].start()
        total[...] += jnp.dot(nv[n], wv[n], preferred_element_type=F32)
    cosine, sine = angles(small[...], large[pl.ds(lax.axis_index("section"), 1), :])
    for h in range(HEADS):
        value = turn(total[:, h * HD : (h + 1) * HD], cosine, sine).astype(BF)
        for n in range(ROWS // SHARE):
            start = (n * HEADS + h) * SHARE
            out[start : start + SHARE, :] = value[n * SHARE : (n + 1) * SHARE]
    for copy in keeps:
        copy.wait()


def query(tokens, factors, gain, weight, bias, small, large, w_out):
    width = HEADS * HD
    steps = D // Q_DEPTH
    columns = (SIDE, HEADS * HD, COLS)
    return pl.pallas_call(
        query_kernel,
        in_specs=[ANY, WHOLE, WHOLE, ANY, WHOLE, WHOLE, WHOLE, ANY],
        out_specs=[WHOLE, ANY],
        out_shape=[jax.ShapeDtypeStruct((HEADS * ROWS, HD), BF), jax.ShapeDtypeStruct(columns, BF)],
        scratch_shapes=[
            pltpu.VMEM((steps, ROWS, Q_DEPTH), BF),
            pltpu.VMEM((steps, ROWS, Q_DEPTH), BF),
            pltpu.VMEM((steps, Q_DEPTH, width), BF),
            pltpu.VMEM(columns, BF),
            pltpu.VMEM((ROWS, width), F32),
            pltpu.SemaphoreType.DMA((steps, 2)),
            pltpu.SemaphoreType.DMA((SIDE,)),
            pltpu.SemaphoreType.DMA((SIDE,)),
        ],
        compiler_params=limit(56),
        cost_estimate=pl.CostEstimate(flops=2 * ROWS * D * 512, bytes_accessed=16 << 20, transcendentals=0),
        name="query",
    )(tokens, factors, gain, weight, bias, small, large, w_out)


TILE = 128
QROWS = HEADS * ROWS


def attend(queries, keys, values, acc, maxima, rows, mask=None, first=False):
    scores = lax.dot_general(queries, keys, (((1,), (1,)), ((), ())), preferred_element_type=F32)
    if mask is not None:
        scores = jnp.where(mask, scores, -1e30)
    highest = jnp.max(scores, axis=1, keepdims=True)
    if first:
        newest = jnp.broadcast_to(highest, (rows.size, HD))
    else:
        old = maxima[rows, :]
        newest = jnp.maximum(old, highest)
        rescale = jnp.exp2((old - newest) * LOG2_SCALE)
    maxima[rows, :] = newest
    weights = jnp.exp2(scores * LOG2_SCALE - newest[:, :1] * LOG2_SCALE).astype(BF)
    added = jnp.dot(weights, values, preferred_element_type=F32)
    if first:
        acc[rows, :] = added
    else:
        acc[rows, :HD] = acc[rows, :HD] * rescale + added[:, :HD]
        acc[rows, HD:] = acc[rows, HD:] * rescale + added[:, HD:]


def attend_kernel(plan, halves, diagonal, final, *refs):
    refs = list(refs)
    take = lambda n: [refs.pop(0) for _ in range(n)]
    (queries,) = take(1)
    begin = take(2)
    pieces = take(len(plan))
    placing = halves is not None
    if placing:
        (table,) = take(1)
        before = [] if diagonal else take(1)
    outs = take(1 if final else 2)
    if placing:
        (cache,) = take(1)
        block_sem = refs.pop()
    if final:
        keys, values, acc, maxima, sems = refs
    else:
        keys, values, sems = refs
        acc, maxima = outs
    count_rows = queries.shape[0]
    section = lax.axis_index("section")
    x, z = section // SIDE, section % SIDE
    count = jnp.int32(0)
    jobs = []
    for piece, offsets in zip(pieces, plan):
        for j, (dx, dz) in enumerate(offsets):
            source = lax.rem(x + dx, SIDE) * SIDE + lax.rem(z + dz, SIDE)
            needed = source < section
            here = pl.ds(j * HALF, HALF)
            there = pl.ds(pl.multiple_of(count * HALF, HALF), HALF)
            n = len(jobs)
            copies = (
                pltpu.make_async_copy(piece.at[here, :HD], keys.at[there, :], sems.at[n, 0]),
                pltpu.make_async_copy(piece.at[here, HD:], values.at[there, :HD], sems.at[n, 1]),
            )

            @pl.when(needed)
            def _():
                copies[0].start()
                copies[1].start()

            jobs.append((needed, copies))
            count = count + needed.astype(jnp.int32)
    if placing:
        cache[...] = jnp.zeros_like(cache) if diagonal else before[0][...]
        placed = jnp.int32(0)
        sources = [(piece, j * HALF, dx, dz, half)
                   for piece, offsets, half in zip(pieces, plan, halves)
                   for j, (dx, dz) in enumerate(offsets)]
        if diagonal:
            sources += [(begin[0], 0, 0, 0, 0), (begin[1], 0, 0, 0, 1)]
        for piece, row, dx, dz, half in sources:
            source = lax.rem(x + dx, SIDE) * SIDE + lax.rem(z + dz, SIDE)
            for rank in range(PAIR):
                slot = source * PAIR + rank
                inside = table[slot] - half * (HALF // BLOCK)
                found = (inside >= 0) & (inside < HALF // BLOCK)

                @pl.when(found)
                def _():
                    at = pl.ds(pl.multiple_of(row + inside * BLOCK, BLOCK), BLOCK)
                    pltpu.make_async_copy(piece.at[at, :], cache.at[slot], block_sem).start()

                placed = placed + found.astype(jnp.int32)
    values[:, HD:] = jnp.ones((values.shape[0], HD), BF)
    if diagonal:
        last = len(jobs) * HALF
        for half in range(2):
            rows = slice(last + half * HALF, last + (half + 1) * HALF)
            keys[rows, :] = begin[half][:, :HD]
            values[rows, :HD] = begin[half][:, HD:]
        for start in range(0, ROWS, TILE):
            shape = (TILE, start + TILE)
            mask = lax.broadcasted_iota(jnp.int32, shape, 1) <= start + lax.broadcasted_iota(jnp.int32, shape, 0)
            kd, vd = keys[last : last + start + TILE, :], values[last : last + start + TILE, :]
            for h in range(HEADS):
                rows = pl.ds((start // SHARE * HEADS + h) * SHARE + start % SHARE, TILE)
                attend(queries[rows, :], kd, vd, acc, maxima, rows, mask, True)
    else:
        acc[...] = begin[0][...]
        maxima[...] = begin[1][...]
    for needed, copies in jobs:
        @pl.when(needed)
        def _():
            copies[0].wait()
            copies[1].wait()

    def part(base, size):
        at = pl.ds(pl.multiple_of(base, HALF), size)
        kd, vd = keys[at, :], values[at, :]
        for start in range(0, count_rows, TILE):
            rows = pl.ds(start, TILE)
            attend(queries[rows, :], kd, vd, acc, maxima, rows)

    def whole(i, _):
        part(i * 4 * HALF, 4 * HALF)
        return 0

    lax.fori_loop(0, count // 4, whole, 0)
    left = lax.rem(count, 4)

    @pl.when(left >= 2)
    def _():
        part((count // 4) * 4 * HALF, 2 * HALF)

    @pl.when(lax.rem(left, 2) == 1)
    def _():
        part((count - 1) * HALF, HALF)

    if final:
        for h in range(HEADS):
            rows = slice(h * SHARE, (h + 1) * SHARE)
            outs[0][:, h * HD : (h + 1) * HD] = (acc[rows, :HD] / acc[rows, HD:]).astype(BF)
    if placing:
        def block(i, _):
            pltpu.make_async_copy(cache.at[0], cache.at[0], block_sem).wait()
            return 0

        lax.fori_loop(0, placed, block, 0)


def attention(queries, begin, pieces, plan, name, diagonal=False, share=None, table=None, cache=None, halves=None):
    subs = sum(len(p) for p in plan)
    final = share is not None
    rows = HEADS * SHARE if final else QROWS
    size = subs * HALF + (ROWS if diagonal else 0)
    state_shape = [jax.ShapeDtypeStruct((rows, 2 * HD), F32), jax.ShapeDtypeStruct((rows, HD), F32)]
    scratch = [pltpu.VMEM((size, HD), BF), pltpu.VMEM((size, 2 * HD), BF)]
    if final:
        scratch += [pltpu.VMEM(s.shape, s.dtype) for s in state_shape]
        out_shape = [jax.ShapeDtypeStruct((SHARE, HEADS * HD), BF)]
        at = lambda i: (share, 0)
        in_specs = [pl.BlockSpec((rows, HD), at), pl.BlockSpec((rows, 2 * HD), at), pl.BlockSpec((rows, HD), at)]
        grid = (1,)
        out_specs = [pl.BlockSpec((SHARE, HEADS * HD), lambda i: (0, 0))]
    else:
        out_shape = state_shape
        in_specs = [WHOLE] * 3
        grid = ()
        out_specs = [WHOLE] * 2
    in_specs = in_specs + [ANY] * len(pieces)
    args = [queries, *begin, *pieces]
    scratch.append(pltpu.SemaphoreType.DMA((subs, 2)))
    if table is not None:
        in_specs.append(pl.BlockSpec(memory_space=pltpu.SMEM))
        args.append(table)
        if cache is not None:
            in_specs.append(WHOLE)
            args.append(cache)
        out_shape = out_shape + [jax.ShapeDtypeStruct((SIDE * SIDE * PAIR, BLOCK, 2 * HD), BF)]
        out_specs = out_specs + [WHOLE]
        scratch.append(pltpu.SemaphoreType.DMA)
    return pl.pallas_call(
        functools.partial(attend_kernel, plan, halves, diagonal, final),
        grid=grid,
        in_specs=in_specs,
        out_specs=out_specs,
        out_shape=out_shape,
        scratch_shapes=scratch,
        compiler_params=limit(20),
        cost_estimate=pl.CostEstimate(
            flops=8 * rows * size * HD, bytes_accessed=8 << 20, transcendentals=rows * size
        ),
        name=name,
    )(*args)


def join_kernel(*refs):
    n = (len(refs) - 2) // 2
    for ins, out in ((refs[:n], refs[-2]), (refs[n : 2 * n], refs[-1])):
        for j, piece in enumerate(ins):
            out[j * HALF : (j + 1) * HALF, :] = piece[...]


def join(first, second):
    out = jax.ShapeDtypeStruct((len(first) * HALF, 2 * HD), BF)
    return pl.pallas_call(
        join_kernel,
        in_specs=[WHOLE] * (len(first) + len(second)),
        out_specs=[WHOLE] * 2,
        out_shape=[out] * 2,
        compiler_params=limit(8),
        cost_estimate=pl.CostEstimate(flops=0, bytes_accessed=2 << 20, transcendentals=0),
        name="join",
    )(*first, *second)


def cache_kernel(places, table, *refs):
    pieces, (out, zeros, sem) = refs[:-3], refs[-3:]
    zeros[...] = jnp.zeros_like(zeros)
    section = lax.axis_index("section")
    x, z = section // SIDE, section % SIDE
    for dx in range(SIDE):
        for dz in range(SIDE):
            source = lax.rem(x + dx, SIDE) * SIDE + lax.rem(z + dz, SIDE)
            for rank in range(PAIR):
                slot = source * PAIR + rank
                block = table[slot]

                @pl.when(block < 0)
                def _():
                    pltpu.make_async_copy(zeros, out.at[slot], sem).start()

                for half in range(2):
                    piece, row = places[half][(dx, dz)]
                    inside = block - half * (HALF // BLOCK)

                    @pl.when((inside >= 0) & (inside < HALF // BLOCK))
                    def _():
                        at = pl.ds(pl.multiple_of(row + inside * BLOCK, BLOCK), BLOCK)
                        pltpu.make_async_copy(pieces[piece].at[at, :], out.at[slot], sem).start()

    pltpu.make_async_copy(out, out, sem).wait()


def cache_table(placement, section):
    owners = placement.reshape(SIDE * SIDE, ROWS // BLOCK)
    mine = owners == section
    before = jnp.arange(ROWS // BLOCK)[:, None] < jnp.arange(ROWS // BLOCK)[None, :]
    ranks = jnp.sum((mine[:, :, None] & before[None]).astype(jnp.int32), axis=1)
    hit = mine[:, None, :] & (ranks[:, None, :] == jnp.arange(PAIR)[None, :, None])
    number = jnp.arange(ROWS // BLOCK, dtype=jnp.int32) + 1
    return (jnp.sum(jnp.where(hit, number[None, None, :], 0), axis=-1) - 1).reshape(-1)


def decode(places, table, pieces):
    slots = SIDE * SIDE * PAIR
    return pl.pallas_call(
        functools.partial(cache_kernel, places),
        in_specs=[pl.BlockSpec(memory_space=pltpu.SMEM)] + [ANY] * len(pieces),
        out_specs=WHOLE,
        out_shape=jax.ShapeDtypeStruct((slots, BLOCK, 2 * HD), BF),
        scratch_shapes=[pltpu.VMEM((BLOCK, 2 * HD), BF), pltpu.SemaphoreType.DMA],
        compiler_params=limit(16),
        cost_estimate=pl.CostEstimate(flops=0, bytes_accessed=4 << 20, transcendentals=0),
        name="decode_cache",
    )(table, *pieces)


MID = SHARE // 2
PROJECT_LIMIT = 16


def blocks_of(offsets, w_own, w_other, wv, sems):
    tp = lax.axis_index("tp")
    copies = []
    for n, offset in enumerate(offsets):
        y = lax.rem(tp // 2 + offset, SIDE)
        copies.append(pltpu.make_async_copy(w_own.at[y], wv.at[n, 0], sems.at[n, 0]))
        copies.append(pltpu.make_async_copy(w_other.at[y], wv.at[n, 1], sems.at[n, 1]))
    for copy in copies:
        copy.start()
    return copies


def term(n, copies, own, other, wv):
    copies[2 * n].wait()
    product = jnp.dot(own[...], wv[n, 0], preferred_element_type=F32)
    copies[2 * n + 1].wait()
    return product + jnp.dot(other[...], wv[n, 1], preferred_element_type=F32)


def opposite_kernel(own, other, w_own, w_other, top, bottom, wv, sems):
    copies = blocks_of((2,), w_own, w_other, wv, sems)
    product = term(0, copies, own, other, wv)
    top[...] = product[:MID].astype(BF)
    bottom[...] = product[MID:].astype(BF)


def neighbour_kernel(own, other, w_own, w_other, from_below, from_above, up, down, wv, sems):
    copies = blocks_of((1, 3), w_own, w_other, wv, sems)
    product = term(0, copies, own, other, wv)
    up[:MID] = (product[:MID] + from_below[...].astype(F32)).astype(BF)
    up[MID:] = product[MID:].astype(BF)
    product = term(1, copies, own, other, wv)
    down[:MID] = product[:MID].astype(BF)
    down[MID:] = (product[MID:] + from_above[...].astype(F32)).astype(BF)


def home_kernel(share, own, other, w_own, w_other, residual, out, wv, sems):
    copies = blocks_of((0,), w_own, w_other, wv, sems)
    rows = slice(share * SHARE, (share + 1) * SHARE)
    out[...] = residual[rows, :].astype(F32) + term(0, copies, own, other, wv)


def project(kernel, targets, terms, extra, out, name):
    return pl.pallas_call(
        kernel,
        in_specs=[WHOLE, WHOLE, ANY, ANY] + [WHOLE] * len(extra),
        out_specs=[WHOLE] * len(out),
        out_shape=[jax.ShapeDtypeStruct(shape, dtype) for shape, dtype in out],
        scratch_shapes=[
            pltpu.VMEM((targets, 2, HEADS * HD, COLS), BF),
            pltpu.SemaphoreType.DMA((targets, 2)),
        ],
        compiler_params=limit(PROJECT_LIMIT),
        cost_estimate=pl.CostEstimate(
            flops=4 * SHARE * 512 * COLS * targets, bytes_accessed=4 << 20, transcendentals=0
        ),
        name=name,
    )(*terms, *extra)


def finish_kernel(base, from_below, from_above, *refs):
    refs[-1][...] = (base[...] + from_below[...].astype(F32) + from_above[...].astype(F32)).astype(BF)


def finish(base, from_below, from_above, done, share):
    return pl.pallas_call(
        finish_kernel,
        grid=(1,),
        in_specs=[WHOLE] * 3 + [ANY] * len(done),
        out_specs=pl.BlockSpec((SHARE, COLS), lambda i: (share, 0)),
        out_shape=jax.ShapeDtypeStruct((ROWS, COLS), BF),
        input_output_aliases={3: 0} if done else {},
        compiler_params=limit(8),
        cost_estimate=pl.CostEstimate(flops=4 * SHARE * COLS, bytes_accessed=3 << 20, transcendentals=0),
        name="finish",
    )(base, from_below, from_above, *done)


def from_section(value, dx, dz):
    pairs = []
    for x in range(SIDE):
        for z in range(SIDE):
            pairs.append((((x + dx) % SIDE) * SIDE + (z + dz) % SIDE, x * SIDE + z))
    return lax.ppermute(value, "section", pairs)


def from_tp(value, dy, dc):
    pairs = []
    for y in range(SIDE):
        for c in range(2):
            pairs.append((((y + dy) % SIDE) * 2 + (c ^ dc), y * 2 + c))
    return lax.ppermute(value, "tp", pairs)


RING = (1, 3, 2)
ORDER = (0,) + RING


def per_device(tokens, gain, q_weight, q_bias, kv_weight, kv_bias, out_weight, placement):
    section = lax.axis_index("section")
    small, large = tables()
    factors, first, second, residual, w_send = norm_kv(
        tokens, gain[None, :], kv_weight, kv_bias[None, :], small, large, out_weight
    )
    w_other = from_tp(w_send, 0, 1)
    row_first = [from_section(first, 0, k) for k in RING]
    row_second = [from_section(second, k, 0) for k in RING]
    factors, row_first[0] = lax.optimization_barrier((factors, row_first[0]))
    queries, w_own = query(
        tokens, factors, gain[None, :], q_weight, q_bias[None, :], small, large, out_weight
    )
    row_first[1], w_other, queries = lax.optimization_barrier((row_first[1], w_other, queries))
    all_first, all_second = join([first, *row_first], [second, *row_second])
    far_first = [from_section(all_first, k, 0) for k in RING]
    far_second = [from_section(all_second, 0, k) for k in RING]
    near = [[(0, k)] for k in RING] + [[(k, 0)] for k in RING]
    state = attention(queries, (first, second), row_first + row_second, near, "attention_near", diagonal=True)
    far = [[(k, j) for j in ORDER] for k in RING], [[(j, k) for j in ORDER] for k in RING]
    state = attention(
        queries, state, far_first[:2] + far_second[:2], far[0][:2] + far[1][:2], "attention_far"
    )
    shares = []
    for share in range(ROWS // SHARE):
        shares += attention(
            queries, state, far_first[2:] + far_second[2:], far[0][2:] + far[1][2:], "attention_last", share=share
        )
    mixed = []
    for share, own in enumerate(shares):
        terms = (own, from_tp(own, 0, 1), w_own, w_other)
        top, bottom = project(opposite_kernel, 1, terms, [], [((MID, COLS), BF)] * 2, "project_opposite")
        from_below, from_above = from_tp(top, 3, 0), from_tp(bottom, 1, 0)
        up, down = project(
            neighbour_kernel, 2, terms, [from_below, from_above], [((SHARE, COLS), BF)] * 2, "project_neighbours"
        )
        from_below, from_above = from_tp(up, 3, 0), from_tp(down, 1, 0)
        (base,) = project(
            functools.partial(home_kernel, share), 1, terms, [residual], [((SHARE, COLS), F32)], "project_home"
        )
        mixed = [finish(base, from_below, from_above, mixed, share)]
    pieces = [first, second] + row_first + row_second + far_first + far_second
    places = [{(0, 0): (0, 0)}, {(0, 0): (1, 0)}]
    for i, k in enumerate(RING):
        places[0][(0, k)] = (2 + i, 0)
        places[1][(k, 0)] = (5 + i, 0)
        for n, j in enumerate(ORDER):
            places[0][(k, j)] = (8 + i, n * HALF)
            places[1][(j, k)] = (11 + i, n * HALF)
    placement, base = lax.optimization_barrier((placement, base))
    decode_cache = decode(places, cache_table(placement, section), pieces)
    return mixed[0], decode_cache


def solution(mesh):
    placed = (
        P("section", None),
        P(),
        P(None, "tp"),
        P("tp"),
        P(None, "tp"),
        P("tp"),
        P("tp", None),
        P(),
    )
    return jax.shard_map(
        per_device,
        mesh=mesh,
        in_specs=placed,
        out_specs=(P("section", "tp"), P("section", None, "tp")),
        check_vma=False,
    )
```

```python
import functools
import math

import jax
import jax.numpy as jnp
import numpy as np
from jax import lax
from jax.experimental import pallas as pl
from jax.experimental.pallas import tpu as pltpu
from jax.sharding import PartitionSpec as P

HD = 128
BLOCK = 16
SIDE = 4
HALF = 256
ROWS = 512
D = 8192
HEADS = 4
PAIR = 4
ROPE_BASE = 1000000.0
LOG2_SCALE = math.log2(math.e) / math.sqrt(HD)
SHARE = 256
COLS = 1024
limit = lambda mib: pltpu.CompilerParams(vmem_limit_bytes=mib * 1024 * 1024)
BF = jnp.bfloat16
F32 = jnp.float32
ANY = pl.BlockSpec(memory_space=pl.ANY)
WHOLE = pl.BlockSpec(memory_space=pltpu.VMEM)
FAR = pl.BlockSpec(memory_space=pltpu.HBM)


def tables():
    freq = ROPE_BASE ** (-(np.arange(HD // 2, dtype=np.float64) * 2.0 / HD))
    inner = np.arange(ROWS, dtype=np.float64)[:, None] * freq
    outer = ROWS * np.arange(SIDE * SIDE, dtype=np.float64)[:, None] * freq
    twice = lambda a: np.concatenate([a, a], -1)
    signed = lambda a: np.concatenate([-a, a], -1)
    small = np.concatenate([twice(np.cos(inner)), twice(np.sin(inner))], -1)
    large = np.concatenate(
        [twice(np.cos(outer)), twice(np.sin(outer)), signed(np.cos(outer)), signed(np.sin(outer))], -1
    )
    return small.astype(np.float32), large.astype(np.float32)


def angles(small, large):
    cos_r, sin_r = small[:, :HD], small[:, HD:]
    cos_s, sin_s = large[:, :HD], large[:, HD : 2 * HD]
    cos_g, sin_g = large[:, 2 * HD : 3 * HD], large[:, 3 * HD :]
    return cos_s * cos_r - sin_s * sin_r, sin_g * cos_r + cos_g * sin_r


def turn(value, cosine, sine):
    return value * cosine + pltpu.roll(value, HD // 2, 1) * sine


CHUNK = 64
GROUP = 32
DEPTH = 2048
AHEAD = 4
NORM_LIMIT = 56


def norm_kv_kernel(
    tokens, gain, weight, bias, small, large, w_out, factors, first, second, residual, w_send,
    tv, nv, wv, sv, total, st, sw, s_in, s_out
):
    chunks = ROWS // CHUNK
    rows_at = lambda i: pl.ds(pl.multiple_of(i * CHUNK, CHUNK), CHUNK)
    load = lambda i: pltpu.make_async_copy(tokens.at[rows_at(i), :], tv.at[rows_at(i), :], st.at[i])
    weights = [
        pltpu.make_async_copy(weight.at[k : k + DEPTH, :], wv.at[k : k + DEPTH, :], sw.at[k // DEPTH])
        for k in range(0, D, DEPTH)
    ]
    sibling = 1 - lax.rem(lax.axis_index("tp"), 2)
    fetches, sends = [], []
    for y in range(SIDE):
        here = pl.ds(pl.multiple_of((2 * y + sibling) * COLS, COLS), COLS)
        fetches.append(pltpu.make_async_copy(w_out.at[:, here], sv.at[y], s_in.at[y]))
        sends.append(pltpu.make_async_copy(sv.at[y], w_send.at[y], s_out.at[y]))
    for i in range(AHEAD):
        load(i).start()

    def chunk(i, _):
        load(i).wait()

        @pl.when(i < chunks - AHEAD)
        def _():
            load(i + AHEAD).start()

        for n in range(AHEAD):
            @pl.when(i == chunks - AHEAD + n)
            def _():
                weights[n].start()

        for g in range(0, CHUNK, GROUP):
            rows = pl.ds(pl.multiple_of(i * CHUNK + g, GROUP), GROUP)
            squares = jnp.zeros((GROUP, 128), F32)
            for c in range(0, D, 1024):
                wide = tv[rows, c : c + 1024].astype(F32)
                square = wide * wide
                for k in range(0, 1024, 128):
                    squares = squares + square[:, k : k + 128]
            meansq = jnp.sum(squares, axis=1, keepdims=True) * (1.0 / D)
            factor = lax.rsqrt(meansq + 1e-06)
            factors[rows, :] = jnp.broadcast_to(factor, (GROUP, 128))
            for c in range(0, D, 1024):
                wide = tv[rows, c : c + 1024].astype(F32)
                nv[rows, c : c + 1024] = (wide * factor * gain[:, c : c + 1024]).astype(BF)
        return 0

    lax.fori_loop(0, chunks, chunk, 0)
    for n in range(AHEAD, D // DEPTH):
        weights[n].start()
    for copy in fetches:
        copy.start()
    residual[...] = tv[:, pl.ds(pl.multiple_of(lax.axis_index("tp") * COLS, COLS), COLS)]
    total[...] = jnp.broadcast_to(bias[...], total.shape)
    for n, k in enumerate(range(0, D, DEPTH)):
        weights[n].wait()
        total[...] += jnp.dot(nv[:, k : k + DEPTH], wv[k : k + DEPTH, :], preferred_element_type=F32)
        fetches[n].wait()
        sends[n].start()
    cosine, sine = angles(small[...], large[pl.ds(lax.axis_index("section"), 1), :])
    keys = turn(total[:, :HD], cosine, sine).astype(BF)
    values = total[:, HD:].astype(BF)
    for half, out in enumerate((first, second)):
        rows = slice(half * HALF, (half + 1) * HALF)
        out[:, :HD] = keys[rows]
        out[:, HD:] = values[rows]
    for copy in sends:
        copy.wait()


def norm_kv(tokens, gain, weight, bias, small, large, w_out):
    half = jax.ShapeDtypeStruct((HALF, 2 * HD), BF)
    return pl.pallas_call(
        norm_kv_kernel,
        in_specs=[ANY, WHOLE, ANY, WHOLE, WHOLE, WHOLE, ANY],
        out_specs=[WHOLE] * 4 + [ANY],
        out_shape=[
            jax.ShapeDtypeStruct((ROWS, 128), F32),
            half,
            half,
            jax.ShapeDtypeStruct((ROWS, COLS), BF),
            jax.ShapeDtypeStruct((SIDE, HEADS * HD, COLS), BF),
        ],
        scratch_shapes=[
            pltpu.VMEM((ROWS, D), BF),
            pltpu.VMEM((ROWS, D), BF),
            pltpu.VMEM((D, 2 * HD), BF),
            pltpu.VMEM((SIDE, HEADS * HD, COLS), BF),
            pltpu.VMEM((ROWS, 2 * HD), F32),
            pltpu.SemaphoreType.DMA((ROWS // CHUNK,)),
            pltpu.SemaphoreType.DMA((D // DEPTH,)),
            pltpu.SemaphoreType.DMA((SIDE,)),
            pltpu.SemaphoreType.DMA((SIDE,)),
        ],
        compiler_params=limit(NORM_LIMIT),
        cost_estimate=pl.CostEstimate(flops=2 * ROWS * D * 256, bytes_accessed=20 << 20, transcendentals=0),
        name="norm_kv",
    )(tokens, gain, weight, bias, small, large, w_out)


Q_DEPTH = 1024
Q_AHEAD = 2


def query_kernel(
    tokens, factors, gain, weight, bias, small, large, w_out, out, w_own, tv, nv, wv, sv, total, sems, s_in, s_out
):
    steps = D // Q_DEPTH
    copies = []
    for n in range(steps):
        at = slice(n * Q_DEPTH, (n + 1) * Q_DEPTH)
        copies.append(
            (
                pltpu.make_async_copy(tokens.at[:, at], tv.at[n], sems.at[n, 0]),
                pltpu.make_async_copy(weight.at[at, :], wv.at[n], sems.at[n, 1]),
            )
        )
    core = lax.rem(lax.axis_index("tp"), 2)
    fetches, keeps = [], []
    for y in range(SIDE):
        here = pl.ds(pl.multiple_of((2 * y + core) * COLS, COLS), COLS)
        fetches.append(pltpu.make_async_copy(w_out.at[:, here], sv.at[y], s_in.at[y]))
        keeps.append(pltpu.make_async_copy(sv.at[y], w_own.at[y], s_out.at[y]))
    begin = lambda n: [copy.start() for copy in copies[n]]
    for n in range(Q_AHEAD):
        begin(n)
    total[...] = jnp.broadcast_to(bias[...], total.shape)

    def scale(n):
        for copy in copies[n]:
            copy.wait()
        if n + Q_AHEAD < steps:
            begin(n + Q_AHEAD)
        for r in range(0, ROWS, 128):
            factor = factors[r : r + 128, :1]
            at = slice(n * Q_DEPTH, (n + 1) * Q_DEPTH)
            nv[n, r : r + 128, :] = (tv[n, r : r + 128, :].astype(F32) * factor * gain[:, at]).astype(BF)

    scale(0)
    for n in range(steps):
        if n + 1 < steps:
            scale(n + 1)
        if n < SIDE:
            fetches[n].start()
        else:
            fetches[n - SIDE].wait()
            keeps[n - SIDE].start()
        total[...] += jnp.dot(nv[n], wv[n], preferred_element_type=F32)
    cosine, sine = angles(small[...], large[pl.ds(lax.axis_index("section"), 1), :])
    for h in range(HEADS):
        value = turn(total[:, h * HD : (h + 1) * HD], cosine, sine).astype(BF)
        for n in range(ROWS // SHARE):
            start = (n * HEADS + h) * SHARE
            out[start : start + SHARE, :] = value[n * SHARE : (n + 1) * SHARE]
    for copy in keeps:
        copy.wait()


def query(tokens, factors, gain, weight, bias, small, large, w_out):
    width = HEADS * HD
    steps = D // Q_DEPTH
    columns = (SIDE, HEADS * HD, COLS)
    return pl.pallas_call(
        query_kernel,
        in_specs=[ANY, WHOLE, WHOLE, ANY, WHOLE, WHOLE, WHOLE, ANY],
        out_specs=[WHOLE, ANY],
        out_shape=[jax.ShapeDtypeStruct((HEADS * ROWS, HD), BF), jax.ShapeDtypeStruct(columns, BF)],
        scratch_shapes=[
            pltpu.VMEM((steps, ROWS, Q_DEPTH), BF),
            pltpu.VMEM((steps, ROWS, Q_DEPTH), BF),
            pltpu.VMEM((steps, Q_DEPTH, width), BF),
            pltpu.VMEM(columns, BF),
            pltpu.VMEM((ROWS, width), F32),
            pltpu.SemaphoreType.DMA((steps, 2)),
            pltpu.SemaphoreType.DMA((SIDE,)),
            pltpu.SemaphoreType.DMA((SIDE,)),
        ],
        compiler_params=limit(56),
        cost_estimate=pl.CostEstimate(flops=2 * ROWS * D * 512, bytes_accessed=16 << 20, transcendentals=0),
        name="query",
    )(tokens, factors, gain, weight, bias, small, large, w_out)


TILE = 128
QROWS = HEADS * ROWS


def attend(queries, keys, values, acc, maxima, rows, mask=None, first=False):
    scores = lax.dot_general(queries, keys, (((1,), (1,)), ((), ())), preferred_element_type=F32)
    if mask is not None:
        scores = jnp.where(mask, scores, -1e30)
    highest = jnp.max(scores, axis=1, keepdims=True)
    if first:
        newest = jnp.broadcast_to(highest, (rows.size, HD))
    else:
        old = maxima[rows, :]
        newest = jnp.maximum(old, highest)
        rescale = jnp.exp2((old - newest) * LOG2_SCALE)
    maxima[rows, :] = newest
    weights = jnp.exp2(scores * LOG2_SCALE - newest[:, :1] * LOG2_SCALE).astype(BF)
    added = jnp.dot(weights, values, preferred_element_type=F32)
    if first:
        acc[rows, :] = added
    else:
        acc[rows, :HD] = acc[rows, :HD] * rescale + added[:, :HD]
        acc[rows, HD:] = acc[rows, HD:] * rescale + added[:, HD:]


def attend_kernel(plan, halves, diagonal, final, staged, *refs):
    refs = list(refs)
    take = lambda n: [refs.pop(0) for _ in range(n)]
    (queries,) = take(1)
    begin = take(2)
    pieces = take(len(plan))
    placing = halves is not None
    if placing:
        (table,) = take(1)
        before = [] if diagonal else take(1)
    far_away = take(staged)
    outs = take(1 if final else 2)
    if placing:
        (cache,) = take(1)
    moves = list(zip(far_away, take(staged)))
    if staged:
        stage_sems = refs.pop()
    if placing:
        block_sem = refs.pop()
    moves = [pltpu.make_async_copy(a, b, stage_sems.at[n]) for n, (a, b) in enumerate(moves)]
    for move in moves:
        move.start()
    if final:
        keys, values, acc, maxima, sems = refs
    else:
        keys, values, sems = refs
        acc, maxima = outs
    count_rows = queries.shape[0]
    section = lax.axis_index("section")
    x, z = section // SIDE, section % SIDE
    count = jnp.int32(0)
    jobs = []
    for piece, offsets in zip(pieces, plan):
        for j, (dx, dz) in enumerate(offsets):
            source = lax.rem(x + dx, SIDE) * SIDE + lax.rem(z + dz, SIDE)
            needed = source < section
            here = pl.ds(j * HALF, HALF)
            there = pl.ds(pl.multiple_of(count * HALF, HALF), HALF)
            n = len(jobs)
            copies = (
                pltpu.make_async_copy(piece.at[here, :HD], keys.at[there, :], sems.at[n, 0]),
                pltpu.make_async_copy(piece.at[here, HD:], values.at[there, :HD], sems.at[n, 1]),
            )

            @pl.when(needed)
            def _():
                copies[0].start()
                copies[1].start()

            jobs.append((needed, copies))
            count = count + needed.astype(jnp.int32)
    if placing:
        cache[...] = jnp.zeros_like(cache) if diagonal else before[0][...]
        placed = jnp.int32(0)
        sources = [(piece, j * HALF, dx, dz, half)
                   for piece, offsets, half in zip(pieces, plan, halves)
                   for j, (dx, dz) in enumerate(offsets)]
        if diagonal:
            sources += [(begin[0], 0, 0, 0, 0), (begin[1], 0, 0, 0, 1)]
        for piece, row, dx, dz, half in sources:
            source = lax.rem(x + dx, SIDE) * SIDE + lax.rem(z + dz, SIDE)
            for rank in range(PAIR):
                slot = source * PAIR + rank
                inside = table[slot] - half * (HALF // BLOCK)
                found = (inside >= 0) & (inside < HALF // BLOCK)

                @pl.when(found)
                def _():
                    at = pl.ds(pl.multiple_of(row + inside * BLOCK, BLOCK), BLOCK)
                    pltpu.make_async_copy(piece.at[at, :], cache.at[slot], block_sem).start()

                placed = placed + found.astype(jnp.int32)
    values[:, HD:] = jnp.ones((values.shape[0], HD), BF)
    if diagonal:
        last = len(jobs) * HALF
        for half in range(2):
            rows = slice(last + half * HALF, last + (half + 1) * HALF)
            keys[rows, :] = begin[half][:, :HD]
            values[rows, :HD] = begin[half][:, HD:]
        for start in range(0, ROWS, TILE):
            shape = (TILE, start + TILE)
            mask = lax.broadcasted_iota(jnp.int32, shape, 1) <= start + lax.broadcasted_iota(jnp.int32, shape, 0)
            kd, vd = keys[last : last + start + TILE, :], values[last : last + start + TILE, :]
            for h in range(HEADS):
                rows = pl.ds((start // SHARE * HEADS + h) * SHARE + start % SHARE, TILE)
                attend(queries[rows, :], kd, vd, acc, maxima, rows, mask, True)
    else:
        acc[...] = begin[0][...]
        maxima[...] = begin[1][...]
    for needed, copies in jobs:
        @pl.when(needed)
        def _():
            copies[0].wait()
            copies[1].wait()

    def part(base, size):
        at = pl.ds(pl.multiple_of(base, HALF), size)
        kd, vd = keys[at, :], values[at, :]
        for start in range(0, count_rows, TILE):
            rows = pl.ds(start, TILE)
            attend(queries[rows, :], kd, vd, acc, maxima, rows)

    def whole(i, _):
        part(i * 4 * HALF, 4 * HALF)
        return 0

    lax.fori_loop(0, count // 4, whole, 0)
    left = lax.rem(count, 4)

    @pl.when(left >= 2)
    def _():
        part((count // 4) * 4 * HALF, 2 * HALF)

    @pl.when(lax.rem(left, 2) == 1)
    def _():
        part((count - 1) * HALF, HALF)

    if final:
        for h in range(HEADS):
            rows = slice(h * SHARE, (h + 1) * SHARE)
            outs[0][:, h * HD : (h + 1) * HD] = (acc[rows, :HD] / acc[rows, HD:]).astype(BF)
    if placing:
        def block(i, _):
            pltpu.make_async_copy(cache.at[0], cache.at[0], block_sem).wait()
            return 0

        lax.fori_loop(0, placed, block, 0)
    for move in moves:
        move.wait()


def attention(queries, begin, pieces, plan, name, diagonal=False, share=None, table=None, cache=None, halves=None, staged=()):
    subs = sum(len(p) for p in plan)
    final = share is not None
    rows = HEADS * SHARE if final else QROWS
    size = subs * HALF + (ROWS if diagonal else 0)
    state_shape = [jax.ShapeDtypeStruct((rows, 2 * HD), F32), jax.ShapeDtypeStruct((rows, HD), F32)]
    scratch = [pltpu.VMEM((size, HD), BF), pltpu.VMEM((size, 2 * HD), BF)]
    if final:
        scratch += [pltpu.VMEM(s.shape, s.dtype) for s in state_shape]
        out_shape = [jax.ShapeDtypeStruct((SHARE, HEADS * HD), BF)]
        at = lambda i: (share, 0)
        in_specs = [pl.BlockSpec((rows, HD), at), pl.BlockSpec((rows, 2 * HD), at), pl.BlockSpec((rows, HD), at)]
        grid = (1,)
        out_specs = [pl.BlockSpec((SHARE, HEADS * HD), lambda i: (0, 0))]
    else:
        out_shape = state_shape
        in_specs = [WHOLE] * 3
        grid = ()
        out_specs = [WHOLE] * 2
    in_specs = in_specs + [ANY] * len(pieces)
    args = [queries, *begin, *pieces]
    scratch.append(pltpu.SemaphoreType.DMA((subs, 2)))
    if table is not None:
        in_specs.append(pl.BlockSpec(memory_space=pltpu.SMEM))
        args.append(table)
        if cache is not None:
            in_specs.append(WHOLE)
            args.append(cache)
        out_shape = out_shape + [jax.ShapeDtypeStruct((SIDE * SIDE * PAIR, BLOCK, 2 * HD), BF)]
        out_specs = out_specs + [WHOLE]
        scratch.append(pltpu.SemaphoreType.DMA)
    if staged:
        in_specs += [ANY] * len(staged)
        args += staged
        out_shape = out_shape + [jax.ShapeDtypeStruct(a.shape, a.dtype) for a in staged]
        out_specs = out_specs + [WHOLE] * len(staged)
        scratch.append(pltpu.SemaphoreType.DMA((len(staged),)))
    return pl.pallas_call(
        functools.partial(attend_kernel, plan, halves, diagonal, final, len(staged)),
        grid=grid,
        in_specs=in_specs,
        out_specs=out_specs,
        out_shape=out_shape,
        scratch_shapes=scratch,
        compiler_params=limit(20),
        cost_estimate=pl.CostEstimate(
            flops=8 * rows * size * HD, bytes_accessed=8 << 20, transcendentals=rows * size
        ),
        name=name,
    )(*args)


def join_kernel(*refs):
    n = (len(refs) - 2) // 2
    for ins, out in ((refs[:n], refs[-2]), (refs[n : 2 * n], refs[-1])):
        for j, piece in enumerate(ins):
            out[j * HALF : (j + 1) * HALF, :] = piece[...]


def join(first, second):
    out = jax.ShapeDtypeStruct((len(first) * HALF, 2 * HD), BF)
    return pl.pallas_call(
        join_kernel,
        in_specs=[WHOLE] * (len(first) + len(second)),
        out_specs=[WHOLE] * 2,
        out_shape=[out] * 2,
        compiler_params=limit(8),
        cost_estimate=pl.CostEstimate(flops=0, bytes_accessed=2 << 20, transcendentals=0),
        name="join",
    )(*first, *second)


def cache_table(placement, section):
    owners = placement.reshape(SIDE * SIDE, ROWS // BLOCK)
    mine = owners == section
    before = jnp.arange(ROWS // BLOCK)[:, None] < jnp.arange(ROWS // BLOCK)[None, :]
    ranks = jnp.sum((mine[:, :, None] & before[None]).astype(jnp.int32), axis=1)
    hit = mine[:, None, :] & (ranks[:, None, :] == jnp.arange(PAIR)[None, :, None])
    number = jnp.arange(ROWS // BLOCK, dtype=jnp.int32) + 1
    return (jnp.sum(jnp.where(hit, number[None, None, :], 0), axis=-1) - 1).reshape(-1)


MID = SHARE // 2
PROJECT_LIMIT = 14


def term(offset, own, other, w_own, w_other):
    y = lax.rem(lax.axis_index("tp") // 2 + offset, SIDE)
    product = jnp.dot(own[...], w_own[y], preferred_element_type=F32)
    return product + jnp.dot(other[...], w_other[y], preferred_element_type=F32)


def opposite_kernel(own, other, w_own, w_other, top, bottom):
    product = term(2, own, other, w_own, w_other)
    top[...] = product[:MID].astype(BF)
    bottom[...] = product[MID:].astype(BF)


def neighbour_kernel(own, other, w_own, w_other, from_below, from_above, up, down):
    product = term(1, own, other, w_own, w_other)
    up[:MID] = (product[:MID] + from_below[...].astype(F32)).astype(BF)
    up[MID:] = product[MID:].astype(BF)
    product = term(3, own, other, w_own, w_other)
    down[:MID] = product[:MID].astype(BF)
    down[MID:] = (product[MID:] + from_above[...].astype(F32)).astype(BF)


def home_kernel(share, own, other, w_own, w_other, residual, out):
    rows = slice(share * SHARE, (share + 1) * SHARE)
    out[...] = residual[rows, :].astype(F32) + term(0, own, other, w_own, w_other)


def project(kernel, targets, terms, extra, out, name):
    return pl.pallas_call(
        kernel,
        in_specs=[WHOLE] * (len(terms) + len(extra)),
        out_specs=[WHOLE] * len(out),
        out_shape=[jax.ShapeDtypeStruct(shape, dtype) for shape, dtype in out],
        compiler_params=limit(PROJECT_LIMIT),
        cost_estimate=pl.CostEstimate(
            flops=4 * SHARE * 512 * COLS * targets, bytes_accessed=4 << 20, transcendentals=0
        ),
        name=name,
    )(*terms, *extra)


def finish_kernel(base, from_below, from_above, *refs):
    refs[-1][...] = (base[...] + from_below[...].astype(F32) + from_above[...].astype(F32)).astype(BF)


def finish(base, from_below, from_above, done, share):
    return pl.pallas_call(
        finish_kernel,
        grid=(1,),
        in_specs=[WHOLE] * 3 + [ANY] * len(done),
        out_specs=pl.BlockSpec((SHARE, COLS), lambda i: (share, 0)),
        out_shape=jax.ShapeDtypeStruct((ROWS, COLS), BF),
        input_output_aliases={3: 0} if done else {},
        compiler_params=limit(8),
        cost_estimate=pl.CostEstimate(flops=4 * SHARE * COLS, bytes_accessed=3 << 20, transcendentals=0),
        name="finish",
    )(base, from_below, from_above, *done)


def from_section(value, dx, dz):
    pairs = []
    for x in range(SIDE):
        for z in range(SIDE):
            pairs.append((((x + dx) % SIDE) * SIDE + (z + dz) % SIDE, x * SIDE + z))
    return lax.ppermute(value, "section", pairs)


def from_tp(value, dy, dc):
    pairs = []
    for y in range(SIDE):
        for c in range(2):
            pairs.append((((y + dy) % SIDE) * 2 + (c ^ dc), y * 2 + c))
    return lax.ppermute(value, "tp", pairs)


RING = (1, 3, 2)
ORDER = (0,) + RING


def per_device(tokens, gain, q_weight, q_bias, kv_weight, kv_bias, out_weight, placement):
    section = lax.axis_index("section")
    small, large = tables()
    factors, first, second, residual, w_send = norm_kv(
        tokens, gain[None, :], kv_weight, kv_bias[None, :], small, large, out_weight
    )
    w_other = from_tp(w_send, 0, 1)
    row_first = [from_section(first, 0, k) for k in RING]
    row_second = [from_section(second, k, 0) for k in RING]
    factors, row_first[0] = lax.optimization_barrier((factors, row_first[0]))
    queries, w_own = query(
        tokens, factors, gain[None, :], q_weight, q_bias[None, :], small, large, out_weight
    )
    row_first[1], w_other, queries = lax.optimization_barrier((row_first[1], w_other, queries))
    all_first, all_second = join([first, *row_first], [second, *row_second])
    far_first = [from_section(all_first, k, 0) for k in RING]
    far_second = [from_section(all_second, 0, k) for k in RING]
    near = [[(0, k)] for k in RING] + [[(k, 0)] for k in RING]
    table = cache_table(placement, section)
    *state, cache = attention(
        queries,
        (first, second),
        row_first + row_second,
        near,
        "attention_near",
        diagonal=True,
        table=table,
        halves=[0] * 3 + [1] * 3,
    )
    far = [[(k, j) for j in ORDER] for k in RING], [[(j, k) for j in ORDER] for k in RING]
    *state, cache = attention(
        queries,
        state,
        far_first[:2] + far_second[:2],
        far[0][:2] + far[1][:2],
        "attention_far",
        table=table,
        cache=cache,
        halves=[0] * 2 + [1] * 2,
    )
    pieces, plan = far_first[2:] + far_second[2:], far[0][2:] + far[1][2:]
    (early,) = attention(queries, state, pieces, plan, "attention_last", share=0)
    late, cache, w_own, w_other = attention(
        queries,
        state,
        pieces,
        plan,
        "attention_last",
        share=1,
        table=table,
        cache=cache,
        halves=[0, 1],
        staged=(w_own, w_other),
    )
    mixed = []
    for share, own in enumerate((early, late)):
        terms = (own, from_tp(own, 0, 1), w_own, w_other)
        top, bottom = project(opposite_kernel, 1, terms, [], [((MID, COLS), BF)] * 2, "project_opposite")
        from_below, from_above = from_tp(top, 3, 0), from_tp(bottom, 1, 0)
        up, down = project(
            neighbour_kernel, 2, terms, [from_below, from_above], [((SHARE, COLS), BF)] * 2, "project_neighbours"
        )
        from_below, from_above = from_tp(up, 3, 0), from_tp(down, 1, 0)
        (base,) = project(
            functools.partial(home_kernel, share), 1, terms, [residual], [((SHARE, COLS), F32)], "project_home"
        )
        mixed = [finish(base, from_below, from_above, mixed, share)]
    return mixed[0], cache


def solution(mesh):
    placed = (
        P("section", None),
        P(),
        P(None, "tp"),
        P("tp"),
        P(None, "tp"),
        P("tp"),
        P("tp", None),
        P(),
    )
    return jax.shard_map(
        per_device,
        mesh=mesh,
        in_specs=placed,
        out_specs=(P("section", "tp"), P("section", None, "tp")),
        check_vma=False,
    )
```

```python
import functools
import math

import jax
import jax.numpy as jnp
import numpy as np
from jax import lax
from jax.experimental import pallas as pl
from jax.experimental.pallas import tpu as pltpu
from jax.sharding import PartitionSpec as P

HD = 128
BLOCK = 16
SIDE = 4
HALF = 256
ROWS = 512
D = 8192
HEADS = 4
PAIR = 4
ROPE_BASE = 1000000.0
LOG2_SCALE = math.log2(math.e) / math.sqrt(HD)
SHARE = 256
COLS = 1024
limit = lambda mib: pltpu.CompilerParams(vmem_limit_bytes=mib * 1024 * 1024)
BF = jnp.bfloat16
F32 = jnp.float32
ANY = pl.BlockSpec(memory_space=pl.ANY)
WHOLE = pl.BlockSpec(memory_space=pltpu.VMEM)
FAR = pl.BlockSpec(memory_space=pltpu.HBM)


def tables():
    freq = ROPE_BASE ** (-(np.arange(HD // 2, dtype=np.float64) * 2.0 / HD))
    inner = np.arange(ROWS, dtype=np.float64)[:, None] * freq
    outer = ROWS * np.arange(SIDE * SIDE, dtype=np.float64)[:, None] * freq
    twice = lambda a: np.concatenate([a, a], -1)
    signed = lambda a: np.concatenate([-a, a], -1)
    small = np.concatenate([twice(np.cos(inner)), twice(np.sin(inner))], -1)
    large = np.concatenate(
        [twice(np.cos(outer)), twice(np.sin(outer)), signed(np.cos(outer)), signed(np.sin(outer))], -1
    )
    return small.astype(np.float32), large.astype(np.float32)


def angles(small, large):
    cos_r, sin_r = small[:, :HD], small[:, HD:]
    cos_s, sin_s = large[:, :HD], large[:, HD : 2 * HD]
    cos_g, sin_g = large[:, 2 * HD : 3 * HD], large[:, 3 * HD :]
    return cos_s * cos_r - sin_s * sin_r, sin_g * cos_r + cos_g * sin_r


def turn(value, cosine, sine):
    return value * cosine + pltpu.roll(value, HD // 2, 1) * sine


CHUNK = 64
GROUP = 32
DEPTH = 2048
AHEAD = 4
NORM_LIMIT = 56


def norm_kv_kernel(
    tokens, gain, weight, bias, small, large, w_out, factors, first, second, residual, w_send,
    tv, nv, wv, sv, total, st, sw, s_in, s_out
):
    chunks = ROWS // CHUNK
    rows_at = lambda i: pl.ds(pl.multiple_of(i * CHUNK, CHUNK), CHUNK)
    load = lambda i: pltpu.make_async_copy(tokens.at[rows_at(i), :], tv.at[rows_at(i), :], st.at[i])
    weights = [
        pltpu.make_async_copy(weight.at[k : k + DEPTH, :], wv.at[k : k + DEPTH, :], sw.at[k // DEPTH])
        for k in range(0, D, DEPTH)
    ]
    sibling = 1 - lax.rem(lax.axis_index("tp"), 2)
    fetches, sends = [], []
    for y in range(SIDE):
        here = pl.ds(pl.multiple_of((2 * y + sibling) * COLS, COLS), COLS)
        fetches.append(pltpu.make_async_copy(w_out.at[:, here], sv.at[y], s_in.at[y]))
        sends.append(pltpu.make_async_copy(sv.at[y], w_send.at[y], s_out.at[y]))
    for i in range(AHEAD):
        load(i).start()

    def chunk(i, _):
        load(i).wait()

        @pl.when(i < chunks - AHEAD)
        def _():
            load(i + AHEAD).start()

        for n in range(AHEAD):
            @pl.when(i == chunks - AHEAD + n)
            def _():
                weights[n].start()

        for g in range(0, CHUNK, GROUP):
            rows = pl.ds(pl.multiple_of(i * CHUNK + g, GROUP), GROUP)
            squares = jnp.zeros((GROUP, 128), F32)
            for c in range(0, D, 1024):
                wide = tv[rows, c : c + 1024].astype(F32)
                square = wide * wide
                for k in range(0, 1024, 128):
                    squares = squares + square[:, k : k + 128]
            meansq = jnp.sum(squares, axis=1, keepdims=True) * (1.0 / D)
            factor = lax.rsqrt(meansq + 1e-06)
            factors[rows, :] = jnp.broadcast_to(factor, (GROUP, 128))
            for c in range(0, D, 1024):
                wide = tv[rows, c : c + 1024].astype(F32)
                nv[rows, c : c + 1024] = (wide * factor * gain[:, c : c + 1024]).astype(BF)
        return 0

    lax.fori_loop(0, chunks, chunk, 0)
    for n in range(AHEAD, D // DEPTH):
        weights[n].start()
    for copy in fetches:
        copy.start()
    residual[...] = tv[:, pl.ds(pl.multiple_of(lax.axis_index("tp") * COLS, COLS), COLS)]
    for copy in weights:
        copy.wait()
    total[...] = jnp.dot(nv[...], wv[...], preferred_element_type=F32) + bias[...]
    for n in range(SIDE):
        fetches[n].wait()
        sends[n].start()
    cosine, sine = angles(small[...], large[pl.ds(lax.axis_index("section"), 1), :])
    keys = turn(total[:, :HD], cosine, sine).astype(BF)
    values = total[:, HD:].astype(BF)
    for half, out in enumerate((first, second)):
        rows = slice(half * HALF, (half + 1) * HALF)
        out[:, :HD] = keys[rows]
        out[:, HD:] = values[rows]
    for copy in sends:
        copy.wait()


def norm_kv(tokens, gain, weight, bias, small, large, w_out):
    half = jax.ShapeDtypeStruct((HALF, 2 * HD), BF)
    return pl.pallas_call(
        norm_kv_kernel,
        in_specs=[ANY, WHOLE, ANY, WHOLE, WHOLE, WHOLE, ANY],
        out_specs=[WHOLE] * 4 + [ANY],
        out_shape=[
            jax.ShapeDtypeStruct((ROWS, 128), F32),
            half,
            half,
            jax.ShapeDtypeStruct((ROWS, COLS), BF),
            jax.ShapeDtypeStruct((SIDE, HEADS * HD, COLS), BF),
        ],
        scratch_shapes=[
            pltpu.VMEM((ROWS, D), BF),
            pltpu.VMEM((ROWS, D), BF),
            pltpu.VMEM((D, 2 * HD), BF),
            pltpu.VMEM((SIDE, HEADS * HD, COLS), BF),
            pltpu.VMEM((ROWS, 2 * HD), F32),
            pltpu.SemaphoreType.DMA((ROWS // CHUNK,)),
            pltpu.SemaphoreType.DMA((D // DEPTH,)),
            pltpu.SemaphoreType.DMA((SIDE,)),
            pltpu.SemaphoreType.DMA((SIDE,)),
        ],
        compiler_params=limit(NORM_LIMIT),
        cost_estimate=pl.CostEstimate(flops=2 * ROWS * D * 256, bytes_accessed=20 << 20, transcendentals=0),
        name="norm_kv",
    )(tokens, gain, weight, bias, small, large, w_out)


Q_DEPTH = 1024
Q_AHEAD = 4
Q_ROWS = 256


def query_kernel(tokens, factors, gain, weight, bias, small, large, out, tv, nv, wv, total, sems):
    steps = D // Q_DEPTH
    copies = []
    for n in range(steps):
        at = slice(n * Q_DEPTH, (n + 1) * Q_DEPTH)
        copies.append(
            (
                pltpu.make_async_copy(tokens.at[:, at], tv.at[n], sems.at[n, 0]),
                pltpu.make_async_copy(weight.at[at, :], wv.at[n], sems.at[n, 1]),
            )
        )
    begin = lambda n: [copy.start() for copy in copies[n]]
    for n in range(Q_AHEAD):
        begin(n)
    total[...] = jnp.broadcast_to(bias[...], total.shape)

    def scale(n):
        for copy in copies[n]:
            copy.wait()
        if n + Q_AHEAD < steps:
            begin(n + Q_AHEAD)

    def rows_of(n, r):
        factor = factors[r : r + Q_ROWS, :1]
        at = slice(n * Q_DEPTH, (n + 1) * Q_DEPTH)
        nv[n, r : r + Q_ROWS, :] = (tv[n, r : r + Q_ROWS, :].astype(F32) * factor * gain[:, at]).astype(BF)

    scale(0)
    for r in range(0, ROWS, Q_ROWS):
        rows_of(0, r)
    for n in range(steps):
        if n + 1 < steps:
            scale(n + 1)
        for r in range(0, ROWS, Q_ROWS):
            total[r : r + Q_ROWS, :] += jnp.dot(nv[n, r : r + Q_ROWS, :], wv[n], preferred_element_type=F32)
            if n + 1 < steps:
                rows_of(n + 1, r)
    cosine, sine = angles(small[...], large[pl.ds(lax.axis_index("section"), 1), :])
    for h in range(HEADS):
        value = turn(total[:, h * HD : (h + 1) * HD], cosine, sine).astype(BF)
        for n in range(ROWS // SHARE):
            start = (n * HEADS + h) * SHARE
            out[start : start + SHARE, :] = value[n * SHARE : (n + 1) * SHARE]


def query(tokens, factors, gain, weight, bias, small, large):
    width = HEADS * HD
    steps = D // Q_DEPTH
    return pl.pallas_call(
        query_kernel,
        in_specs=[ANY, WHOLE, WHOLE, ANY, WHOLE, WHOLE, WHOLE],
        out_specs=WHOLE,
        out_shape=jax.ShapeDtypeStruct((HEADS * ROWS, HD), BF),
        scratch_shapes=[
            pltpu.VMEM((steps, ROWS, Q_DEPTH), BF),
            pltpu.VMEM((steps, ROWS, Q_DEPTH), BF),
            pltpu.VMEM((steps, Q_DEPTH, width), BF),
            pltpu.VMEM((ROWS, width), F32),
            pltpu.SemaphoreType.DMA((steps, 2)),
        ],
        compiler_params=limit(56),
        cost_estimate=pl.CostEstimate(flops=2 * ROWS * D * 512, bytes_accessed=16 << 20, transcendentals=0),
        name="query",
    )(tokens, factors, gain, weight, bias, small, large)


TILE = 128
QROWS = HEADS * ROWS


def attend(queries, keys, values, acc, maxima, rows, mask=None, first=False):
    scores = lax.dot_general(queries, keys, (((1,), (1,)), ((), ())), preferred_element_type=F32)
    if mask is not None:
        scores = jnp.where(mask, scores, -1e30)
    highest = jnp.max(scores, axis=1, keepdims=True)
    if first:
        newest = jnp.broadcast_to(highest, (rows.size, HD))
    else:
        old = maxima[rows, :]
        newest = jnp.maximum(old, highest)
        rescale = jnp.exp2((old - newest) * LOG2_SCALE)
    maxima[rows, :] = newest
    weights = jnp.exp2(scores * LOG2_SCALE - newest[:, :1] * LOG2_SCALE).astype(BF)
    added = jnp.dot(weights, values, preferred_element_type=F32)
    if first:
        acc[rows, :] = added
    else:
        acc[rows, :HD] = acc[rows, :HD] * rescale + added[:, :HD]
        acc[rows, HD:] = acc[rows, HD:] * rescale + added[:, HD:]


def attend_kernel(plan, halves, diagonal, final, staged, *refs):
    refs = list(refs)
    take = lambda n: [refs.pop(0) for _ in range(n)]
    (queries,) = take(1)
    begin = take(2)
    pieces = take(len(plan))
    placing = halves is not None
    if placing:
        (table,) = take(1)
        before = [] if diagonal else take(1)
    far_away = take(staged)
    outs = take(1 if final else 2)
    if placing:
        (cache,) = take(1)
    moves = list(zip(far_away, take(staged)))
    if staged:
        stage_sems = refs.pop()
    if placing:
        block_sem = refs.pop()
    if staged:
        (w_out, own), (w_other, other) = moves
        core = lax.rem(lax.axis_index("tp"), 2)
        moves = [pltpu.make_async_copy(w_other, other, stage_sems.at[SIDE])]
        for y in range(SIDE):
            here = pl.ds(pl.multiple_of((2 * y + core) * COLS, COLS), COLS)
            moves.append(pltpu.make_async_copy(w_out.at[:, here], own.at[y], stage_sems.at[y]))
    for move in moves:
        move.start()
    if final:
        keys, values, acc, maxima, sems = refs
    else:
        keys, values, sems = refs
        acc, maxima = outs
    count_rows = queries.shape[0]
    section = lax.axis_index("section")
    x, z = section // SIDE, section % SIDE
    count = jnp.int32(0)
    jobs = []
    for piece, offsets in zip(pieces, plan):
        for j, (dx, dz) in enumerate(offsets):
            source = lax.rem(x + dx, SIDE) * SIDE + lax.rem(z + dz, SIDE)
            needed = source < section
            here = pl.ds(j * HALF, HALF)
            there = pl.ds(pl.multiple_of(count * HALF, HALF), HALF)
            n = len(jobs)
            copies = (
                pltpu.make_async_copy(piece.at[here, :HD], keys.at[there, :], sems.at[n, 0]),
                pltpu.make_async_copy(piece.at[here, HD:], values.at[there, :HD], sems.at[n, 1]),
            )

            @pl.when(needed)
            def _():
                copies[0].start()
                copies[1].start()

            jobs.append((needed, copies))
            count = count + needed.astype(jnp.int32)
    if placing:
        cache[...] = jnp.zeros_like(cache) if diagonal else before[0][...]
        placed = jnp.int32(0)
        sources = [(piece, j * HALF, dx, dz, half)
                   for piece, offsets, half in zip(pieces, plan, halves)
                   for j, (dx, dz) in enumerate(offsets)]
        if diagonal:
            sources += [(begin[0], 0, 0, 0, 0), (begin[1], 0, 0, 0, 1)]
        for piece, row, dx, dz, half in sources:
            source = lax.rem(x + dx, SIDE) * SIDE + lax.rem(z + dz, SIDE)
            for rank in range(PAIR):
                slot = source * PAIR + rank
                inside = table[slot] - half * (HALF // BLOCK)
                found = (inside >= 0) & (inside < HALF // BLOCK)

                @pl.when(found)
                def _():
                    at = pl.ds(pl.multiple_of(row + inside * BLOCK, BLOCK), BLOCK)
                    pltpu.make_async_copy(piece.at[at, :], cache.at[slot], block_sem).start()

                placed = placed + found.astype(jnp.int32)
    values[:, HD:] = jnp.ones((values.shape[0], HD), BF)
    if diagonal:
        last = -(-len(jobs) // 4) * 4 * HALF
        for half in range(2):
            rows = slice(last + half * HALF, last + (half + 1) * HALF)
            keys[rows, :] = begin[half][:, :HD]
            values[rows, :HD] = begin[half][:, HD:]
        for start in range(0, ROWS, TILE):
            shape = (TILE, start + TILE)
            mask = lax.broadcasted_iota(jnp.int32, shape, 1) <= start + lax.broadcasted_iota(jnp.int32, shape, 0)
            kd, vd = keys[last : last + start + TILE, :], values[last : last + start + TILE, :]
            for h in range(HEADS):
                rows = pl.ds((start // SHARE * HEADS + h) * SHARE + start % SHARE, TILE)
                attend(queries[rows, :], kd, vd, acc, maxima, rows, mask, True)
    else:
        acc[...] = begin[0][...]
        maxima[...] = begin[1][...]
    for needed, copies in jobs:
        @pl.when(needed)
        def _():
            copies[0].wait()
            copies[1].wait()

    def part(base, size):
        at = pl.ds(pl.multiple_of(base, HALF), size)
        kd, vd = keys[at, :], values[at, :]
        for start in range(0, count_rows, TILE):
            rows = pl.ds(start, TILE)
            attend(queries[rows, :], kd, vd, acc, maxima, rows)

    def whole(i, _):
        part(i * 4 * HALF, 4 * HALF)
        return 0

    steps = (count + 3) // 4
    for n in range(3):
        @pl.when(count + n < steps * 4)
        def _():
            at = pl.ds(pl.multiple_of((count + n) * HALF, HALF), HALF)
            keys[at, :] = keys[:HALF, :]
            values[at, :] = jnp.zeros((HALF, 2 * HD), BF)

    lax.fori_loop(0, steps, whole, 0)

    if final:
        for h in range(HEADS):
            rows = slice(h * SHARE, (h + 1) * SHARE)
            outs[0][:, h * HD : (h + 1) * HD] = (acc[rows, :HD] / acc[rows, HD:]).astype(BF)
    if placing:
        def block(i, _):
            pltpu.make_async_copy(cache.at[0], cache.at[0], block_sem).wait()
            return 0

        lax.fori_loop(0, placed, block, 0)
    for move in moves:
        move.wait()


def attention(queries, begin, pieces, plan, name, diagonal=False, share=None, table=None, cache=None, halves=None, staged=()):
    subs = sum(len(p) for p in plan)
    final = share is not None
    rows = HEADS * SHARE if final else QROWS
    size = -(-subs // 4) * 4 * HALF + (ROWS if diagonal else 0)
    state_shape = [jax.ShapeDtypeStruct((rows, 2 * HD), F32), jax.ShapeDtypeStruct((rows, HD), F32)]
    scratch = [pltpu.VMEM((size, HD), BF), pltpu.VMEM((size, 2 * HD), BF)]
    if final:
        scratch += [pltpu.VMEM(s.shape, s.dtype) for s in state_shape]
        out_shape = [jax.ShapeDtypeStruct((SHARE, HEADS * HD), BF)]
        at = lambda i: (share, 0)
        in_specs = [pl.BlockSpec((rows, HD), at), pl.BlockSpec((rows, 2 * HD), at), pl.BlockSpec((rows, HD), at)]
        grid = (1,)
        out_specs = [pl.BlockSpec((SHARE, HEADS * HD), lambda i: (0, 0))]
    else:
        out_shape = state_shape
        in_specs = [WHOLE] * 3
        grid = ()
        out_specs = [WHOLE] * 2
    in_specs = in_specs + [ANY] * len(pieces)
    args = [queries, *begin, *pieces]
    scratch.append(pltpu.SemaphoreType.DMA((subs, 2)))
    if table is not None:
        in_specs.append(pl.BlockSpec(memory_space=pltpu.SMEM))
        args.append(table)
        if cache is not None:
            in_specs.append(WHOLE)
            args.append(cache)
        out_shape = out_shape + [jax.ShapeDtypeStruct((SIDE * SIDE * PAIR, BLOCK, 2 * HD), BF)]
        out_specs = out_specs + [WHOLE]
        scratch.append(pltpu.SemaphoreType.DMA)
    if staged:
        in_specs += [ANY] * len(staged)
        args += staged
        out_shape = out_shape + [jax.ShapeDtypeStruct(staged[1].shape, BF)] * 2
        out_specs = out_specs + [WHOLE] * len(staged)
        scratch.append(pltpu.SemaphoreType.DMA((SIDE + 1,)))
    return pl.pallas_call(
        functools.partial(attend_kernel, plan, halves, diagonal, final, len(staged)),
        grid=grid,
        in_specs=in_specs,
        out_specs=out_specs,
        out_shape=out_shape,
        scratch_shapes=scratch,
        compiler_params=limit(20),
        cost_estimate=pl.CostEstimate(
            flops=8 * rows * size * HD, bytes_accessed=8 << 20, transcendentals=rows * size
        ),
        name=name,
    )(*args)


def join_kernel(*refs):
    n = (len(refs) - 2) // 2
    for ins, out in ((refs[:n], refs[-2]), (refs[n : 2 * n], refs[-1])):
        for j, piece in enumerate(ins):
            out[j * HALF : (j + 1) * HALF, :] = piece[...]


def join(first, second):
    out = jax.ShapeDtypeStruct((len(first) * HALF, 2 * HD), BF)
    return pl.pallas_call(
        join_kernel,
        in_specs=[WHOLE] * (len(first) + len(second)),
        out_specs=[WHOLE] * 2,
        out_shape=[out] * 2,
        compiler_params=limit(8),
        cost_estimate=pl.CostEstimate(flops=0, bytes_accessed=2 << 20, transcendentals=0),
        name="join",
    )(*first, *second)


def cache_table(placement, section):
    owners = placement.reshape(SIDE * SIDE, ROWS // BLOCK)
    mine = owners == section
    before = jnp.arange(ROWS // BLOCK)[:, None] < jnp.arange(ROWS // BLOCK)[None, :]
    ranks = jnp.sum((mine[:, :, None] & before[None]).astype(jnp.int32), axis=1)
    hit = mine[:, None, :] & (ranks[:, None, :] == jnp.arange(PAIR)[None, :, None])
    number = jnp.arange(ROWS // BLOCK, dtype=jnp.int32) + 1
    return (jnp.sum(jnp.where(hit, number[None, None, :], 0), axis=-1) - 1).reshape(-1)


MID = SHARE // 2
PROJECT_LIMIT = 14


def term(offset, own, other, w_own, w_other):
    y = lax.rem(lax.axis_index("tp") // 2 + offset, SIDE)
    product = jnp.dot(own[...], w_own[y], preferred_element_type=F32)
    return product + jnp.dot(other[...], w_other[y], preferred_element_type=F32)


def opposite_kernel(own, other, w_own, w_other, top, bottom):
    product = term(2, own, other, w_own, w_other)
    top[...] = product[:MID].astype(BF)
    bottom[...] = product[MID:].astype(BF)


def neighbour_kernel(own, other, w_own, w_other, from_below, from_above, up, down):
    product = term(1, own, other, w_own, w_other)
    up[:MID] = (product[:MID] + from_below[...].astype(F32)).astype(BF)
    up[MID:] = product[MID:].astype(BF)
    product = term(3, own, other, w_own, w_other)
    down[:MID] = product[:MID].astype(BF)
    down[MID:] = (product[MID:] + from_above[...].astype(F32)).astype(BF)


def home_kernel(share, own, other, w_own, w_other, residual, out):
    rows = slice(share * SHARE, (share + 1) * SHARE)
    out[...] = residual[rows, :].astype(F32) + term(0, own, other, w_own, w_other)


def project(kernel, targets, terms, extra, out, name):
    return pl.pallas_call(
        kernel,
        in_specs=[WHOLE] * (len(terms) + len(extra)),
        out_specs=[WHOLE] * len(out),
        out_shape=[jax.ShapeDtypeStruct(shape, dtype) for shape, dtype in out],
        compiler_params=limit(PROJECT_LIMIT),
        cost_estimate=pl.CostEstimate(
            flops=4 * SHARE * 512 * COLS * targets, bytes_accessed=4 << 20, transcendentals=0
        ),
        name=name,
    )(*terms, *extra)


def finish_kernel(base, from_below, from_above, *refs):
    refs[-1][...] = (base[...] + from_below[...].astype(F32) + from_above[...].astype(F32)).astype(BF)


def finish(base, from_below, from_above, done, share):
    return pl.pallas_call(
        finish_kernel,
        grid=(1,),
        in_specs=[WHOLE] * 3 + [ANY] * len(done),
        out_specs=pl.BlockSpec((SHARE, COLS), lambda i: (share, 0)),
        out_shape=jax.ShapeDtypeStruct((ROWS, COLS), BF),
        input_output_aliases={3: 0} if done else {},
        compiler_params=limit(8),
        cost_estimate=pl.CostEstimate(flops=4 * SHARE * COLS, bytes_accessed=3 << 20, transcendentals=0),
        name="finish",
    )(base, from_below, from_above, *done)


def from_section(value, dx, dz):
    pairs = []
    for x in range(SIDE):
        for z in range(SIDE):
            pairs.append((((x + dx) % SIDE) * SIDE + (z + dz) % SIDE, x * SIDE + z))
    return lax.ppermute(value, "section", pairs)


def from_tp(value, dy, dc):
    pairs = []
    for y in range(SIDE):
        for c in range(2):
            pairs.append((((y + dy) % SIDE) * 2 + (c ^ dc), y * 2 + c))
    return lax.ppermute(value, "tp", pairs)


RING = (1, 3, 2)
ORDER = (0,) + RING


def per_device(tokens, gain, q_weight, q_bias, kv_weight, kv_bias, out_weight, placement):
    section = lax.axis_index("section")
    small, large = tables()
    factors, first, second, residual, w_send = norm_kv(
        tokens, gain[None, :], kv_weight, kv_bias[None, :], small, large, out_weight
    )
    w_other = from_tp(w_send, 0, 1)
    row_first = [from_section(first, 0, k) for k in RING]
    row_second = [from_section(second, k, 0) for k in RING]
    factors, row_first[0] = lax.optimization_barrier((factors, row_first[0]))
    queries = query(tokens, factors, gain[None, :], q_weight, q_bias[None, :], small, large)
    row_first[1], w_other, queries = lax.optimization_barrier((row_first[1], w_other, queries))
    all_first, all_second = join([first, *row_first], [second, *row_second])
    far_first = [from_section(all_first, k, 0) for k in RING]
    far_second = [from_section(all_second, 0, k) for k in RING]
    near = [[(0, k)] for k in RING] + [[(k, 0)] for k in RING]
    table = cache_table(placement, section)
    *state, cache = attention(
        queries,
        (first, second),
        row_first + row_second,
        near,
        "attention_near",
        diagonal=True,
        table=table,
        halves=[0] * 3 + [1] * 3,
    )
    far = [[(k, j) for j in ORDER] for k in RING], [[(j, k) for j in ORDER] for k in RING]
    *state, cache = attention(
        queries,
        state,
        far_first[:2] + far_second[:2],
        far[0][:2] + far[1][:2],
        "attention_far",
        table=table,
        cache=cache,
        halves=[0] * 2 + [1] * 2,
    )
    pieces, plan = far_first[2:] + far_second[2:], far[0][2:] + far[1][2:]
    (early,) = attention(queries, state, pieces, plan, "attention_last", share=0)
    late, cache, w_own, w_other = attention(
        queries,
        state,
        pieces,
        plan,
        "attention_last",
        share=1,
        table=table,
        cache=cache,
        halves=[0, 1],
        staged=(out_weight, w_other),
    )
    mixed = []
    for share, own in enumerate((early, late)):
        terms = (own, from_tp(own, 0, 1), w_own, w_other)
        top, bottom = project(opposite_kernel, 1, terms, [], [((MID, COLS), BF)] * 2, "project_opposite")
        from_below, from_above = from_tp(top, 3, 0), from_tp(bottom, 1, 0)
        up, down = project(
            neighbour_kernel, 2, terms, [from_below, from_above], [((SHARE, COLS), BF)] * 2, "project_neighbours"
        )
        from_below, from_above = from_tp(up, 3, 0), from_tp(down, 1, 0)
        (base,) = project(
            functools.partial(home_kernel, share), 1, terms, [residual], [((SHARE, COLS), F32)], "project_home"
        )
        mixed = [finish(base, from_below, from_above, mixed, share)]
    return mixed[0], cache


def solution(mesh):
    placed = (
        P("section", None),
        P(),
        P(None, "tp"),
        P("tp"),
        P(None, "tp"),
        P("tp"),
        P("tp", None),
        P(),
    )
    return jax.shard_map(
        per_device,
        mesh=mesh,
        in_specs=placed,
        out_specs=(P("section", "tp"), P("section", None, "tp")),
        check_vma=False,
    )
```

```python
import functools
import math

import jax
import jax.numpy as jnp
import numpy as np
from jax import lax
from jax.experimental import pallas as pl
from jax.experimental.pallas import tpu as pltpu
from jax.sharding import PartitionSpec as P

HD = 128
BLOCK = 16
SIDE = 4
HALF = 256
ROWS = 512
D = 8192
HEADS = 4
PAIR = 4
ROPE_BASE = 1000000.0
LOG2_SCALE = math.log2(math.e) / math.sqrt(HD)
SHARE = 256
COLS = 1024
limit = lambda mib: pltpu.CompilerParams(vmem_limit_bytes=mib * 1024 * 1024)
BF = jnp.bfloat16
F32 = jnp.float32
ANY = pl.BlockSpec(memory_space=pl.ANY)
WHOLE = pl.BlockSpec(memory_space=pltpu.VMEM)
FAR = pl.BlockSpec(memory_space=pltpu.HBM)


def tables():
    freq = ROPE_BASE ** (-(np.arange(HD // 2, dtype=np.float64) * 2.0 / HD))
    inner = np.arange(ROWS, dtype=np.float64)[:, None] * freq
    outer = ROWS * np.arange(SIDE * SIDE, dtype=np.float64)[:, None] * freq
    twice = lambda a: np.concatenate([a, a], -1)
    signed = lambda a: np.concatenate([-a, a], -1)
    small = np.concatenate([twice(np.cos(inner)), twice(np.sin(inner))], -1)
    large = np.concatenate(
        [twice(np.cos(outer)), twice(np.sin(outer)), signed(np.cos(outer)), signed(np.sin(outer))], -1
    )
    return small.astype(np.float32), large.astype(np.float32)


def angles(small, large):
    cos_r, sin_r = small[:, :HD], small[:, HD:]
    cos_s, sin_s = large[:, :HD], large[:, HD : 2 * HD]
    cos_g, sin_g = large[:, 2 * HD : 3 * HD], large[:, 3 * HD :]
    return cos_s * cos_r - sin_s * sin_r, sin_g * cos_r + cos_g * sin_r


def turn(value, cosine, sine):
    return value * cosine + pltpu.roll(value, HD // 2, 1) * sine


CHUNK = 64
GROUP = 32
DEPTH = 2048
AHEAD = 4
NORM_LIMIT = 56


def norm_kv_kernel(
    tokens, gain, weight, bias, small, large, w_out, factors, first, second, residual, w_send,
    tv, nv, wv, sv, total, st, sw, s_in, s_out
):
    chunks = ROWS // CHUNK
    rows_at = lambda i: pl.ds(pl.multiple_of(i * CHUNK, CHUNK), CHUNK)
    load = lambda i: pltpu.make_async_copy(tokens.at[rows_at(i), :], tv.at[rows_at(i), :], st.at[i])
    weights = [
        pltpu.make_async_copy(weight.at[k : k + DEPTH, :], wv.at[k : k + DEPTH, :], sw.at[k // DEPTH])
        for k in range(0, D, DEPTH)
    ]
    sibling = 1 - lax.rem(lax.axis_index("tp"), 2)
    fetches, sends = [], []
    for y in range(SIDE):
        here = pl.ds(pl.multiple_of((2 * y + sibling) * COLS, COLS), COLS)
        fetches.append(pltpu.make_async_copy(w_out.at[:, here], sv.at[y], s_in.at[y]))
        sends.append(pltpu.make_async_copy(sv.at[y], w_send.at[y], s_out.at[y]))
    for i in range(AHEAD):
        load(i).start()

    def chunk(i, _):
        load(i).wait()

        @pl.when(i < chunks - AHEAD)
        def _():
            load(i + AHEAD).start()

        for n in range(AHEAD):
            @pl.when(i == chunks - AHEAD + n)
            def _():
                weights[n].start()

        for g in range(0, CHUNK, GROUP):
            rows = pl.ds(pl.multiple_of(i * CHUNK + g, GROUP), GROUP)
            squares = jnp.zeros((GROUP, 128), F32)
            for c in range(0, D, 1024):
                wide = tv[rows, c : c + 1024].astype(F32)
                square = wide * wide
                for k in range(0, 1024, 128):
                    squares = squares + square[:, k : k + 128]
            meansq = jnp.sum(squares, axis=1, keepdims=True) * (1.0 / D)
            factor = lax.rsqrt(meansq + 1e-06)
            factors[rows, :] = jnp.broadcast_to(factor, (GROUP, 128))
            for c in range(0, D, 1024):
                wide = tv[rows, c : c + 1024].astype(F32)
                nv[rows, c : c + 1024] = (wide * factor * gain[:, c : c + 1024]).astype(BF)
        return 0

    lax.fori_loop(0, chunks, chunk, 0)
    for n in range(AHEAD, D // DEPTH):
        weights[n].start()
    for copy in fetches:
        copy.start()
    residual[...] = tv[:, pl.ds(pl.multiple_of(lax.axis_index("tp") * COLS, COLS), COLS)]
    for copy in weights:
        copy.wait()
    total[...] = jnp.dot(nv[...], wv[...], preferred_element_type=F32) + bias[...]
    for n in range(SIDE):
        fetches[n].wait()
        sends[n].start()
    cosine, sine = angles(small[...], large[pl.ds(lax.axis_index("section"), 1), :])
    keys = turn(total[:, :HD], cosine, sine).astype(BF)
    values = total[:, HD:].astype(BF)
    for half, out in enumerate((first, second)):
        rows = slice(half * HALF, (half + 1) * HALF)
        out[:, :HD] = keys[rows]
        out[:, HD:] = values[rows]
    for copy in sends:
        copy.wait()


def norm_kv(tokens, gain, weight, bias, small, large, w_out):
    half = jax.ShapeDtypeStruct((HALF, 2 * HD), BF)
    return pl.pallas_call(
        norm_kv_kernel,
        in_specs=[ANY, WHOLE, ANY, WHOLE, WHOLE, WHOLE, ANY],
        out_specs=[WHOLE] * 4 + [ANY],
        out_shape=[
            jax.ShapeDtypeStruct((ROWS, 128), F32),
            half,
            half,
            jax.ShapeDtypeStruct((ROWS, COLS), BF),
            jax.ShapeDtypeStruct((SIDE, HEADS * HD, COLS), BF),
        ],
        scratch_shapes=[
            pltpu.VMEM((ROWS, D), BF),
            pltpu.VMEM((ROWS, D), BF),
            pltpu.VMEM((D, 2 * HD), BF),
            pltpu.VMEM((SIDE, HEADS * HD, COLS), BF),
            pltpu.VMEM((ROWS, 2 * HD), F32),
            pltpu.SemaphoreType.DMA((ROWS // CHUNK,)),
            pltpu.SemaphoreType.DMA((D // DEPTH,)),
            pltpu.SemaphoreType.DMA((SIDE,)),
            pltpu.SemaphoreType.DMA((SIDE,)),
        ],
        compiler_params=limit(NORM_LIMIT),
        cost_estimate=pl.CostEstimate(flops=2 * ROWS * D * 256, bytes_accessed=20 << 20, transcendentals=0),
        name="norm_kv",
    )(tokens, gain, weight, bias, small, large, w_out)


Q_DEPTH = 1024
Q_AHEAD = 4
Q_ROWS = 256


def query_kernel(tokens, factors, gain, weight, bias, small, large, out, tv, nv, wv, total, sems):
    steps = D // Q_DEPTH
    copies = []
    for n in range(steps):
        at = slice(n * Q_DEPTH, (n + 1) * Q_DEPTH)
        copies.append(
            (
                pltpu.make_async_copy(tokens.at[:, at], tv.at[n], sems.at[n, 0]),
                pltpu.make_async_copy(weight.at[at, :], wv.at[n], sems.at[n, 1]),
            )
        )
    begin = lambda n: [copy.start() for copy in copies[n]]
    for n in range(Q_AHEAD):
        begin(n)
    total[...] = jnp.broadcast_to(bias[...], total.shape)

    def scale(n):
        for copy in copies[n]:
            copy.wait()
        if n + Q_AHEAD < steps:
            begin(n + Q_AHEAD)

    def rows_of(n, r):
        factor = factors[r : r + Q_ROWS, :1]
        at = slice(n * Q_DEPTH, (n + 1) * Q_DEPTH)
        nv[n, r : r + Q_ROWS, :] = (tv[n, r : r + Q_ROWS, :].astype(F32) * factor * gain[:, at]).astype(BF)

    scale(0)
    for r in range(0, ROWS, Q_ROWS):
        rows_of(0, r)
    for n in range(steps):
        if n + 1 < steps:
            scale(n + 1)
        for r in range(0, ROWS, Q_ROWS):
            total[r : r + Q_ROWS, :] += jnp.dot(nv[n, r : r + Q_ROWS, :], wv[n], preferred_element_type=F32)
            if n + 1 < steps:
                rows_of(n + 1, r)
    cosine, sine = angles(small[...], large[pl.ds(lax.axis_index("section"), 1), :])
    for h in range(HEADS):
        value = turn(total[:, h * HD : (h + 1) * HD], cosine, sine).astype(BF)
        for n in range(ROWS // SHARE):
            start = (n * HEADS + h) * SHARE
            out[start : start + SHARE, :] = value[n * SHARE : (n + 1) * SHARE]


def query(tokens, factors, gain, weight, bias, small, large):
    width = HEADS * HD
    steps = D // Q_DEPTH
    return pl.pallas_call(
        query_kernel,
        in_specs=[ANY, WHOLE, WHOLE, ANY, WHOLE, WHOLE, WHOLE],
        out_specs=WHOLE,
        out_shape=jax.ShapeDtypeStruct((HEADS * ROWS, HD), BF),
        scratch_shapes=[
            pltpu.VMEM((steps, ROWS, Q_DEPTH), BF),
            pltpu.VMEM((steps, ROWS, Q_DEPTH), BF),
            pltpu.VMEM((steps, Q_DEPTH, width), BF),
            pltpu.VMEM((ROWS, width), F32),
            pltpu.SemaphoreType.DMA((steps, 2)),
        ],
        compiler_params=limit(56),
        cost_estimate=pl.CostEstimate(flops=2 * ROWS * D * 512, bytes_accessed=16 << 20, transcendentals=0),
        name="query",
    )(tokens, factors, gain, weight, bias, small, large)


TILE = 128
QROWS = HEADS * ROWS


def attend(queries, keys, values, acc, maxima, rows, mask=None, first=False):
    scores = lax.dot_general(queries, keys, (((1,), (1,)), ((), ())), preferred_element_type=F32)
    if mask is not None:
        scores = jnp.where(mask, scores, -1e30)
    highest = jnp.max(scores, axis=1, keepdims=True)
    if first:
        newest = jnp.broadcast_to(highest, (rows.size, HD))
    else:
        old = maxima[rows, :]
        newest = jnp.maximum(old, highest)
        rescale = jnp.exp2((old - newest) * LOG2_SCALE)
    maxima[rows, :] = newest
    weights = jnp.exp2(scores * LOG2_SCALE - newest[:, :1] * LOG2_SCALE).astype(BF)
    added = jnp.dot(weights, values, preferred_element_type=F32)
    if first:
        acc[rows, :] = added
    else:
        acc[rows, :HD] = acc[rows, :HD] * rescale + added[:, :HD]
        acc[rows, HD:] = acc[rows, HD:] * rescale + added[:, HD:]


def attend_kernel(plan, halves, diagonal, final, staged, *refs):
    refs = list(refs)
    take = lambda n: [refs.pop(0) for _ in range(n)]
    (queries,) = take(1)
    begin = take(2)
    pieces = take(len(plan))
    placing = halves is not None
    if placing:
        (table,) = take(1)
        before = [] if diagonal else take(1)
    far_away = take(staged)
    outs = take(1 if final else 2)
    if placing:
        (cache,) = take(1)
    moves = list(zip(far_away, take(staged)))
    if staged:
        stage_sems = refs.pop()
    if placing:
        block_sem = refs.pop()
    if staged:
        (w_out, own), (w_other, other) = moves
        core = lax.rem(lax.axis_index("tp"), 2)
        moves = [pltpu.make_async_copy(w_other, other, stage_sems.at[SIDE])]
        for y in range(SIDE):
            here = pl.ds(pl.multiple_of((2 * y + core) * COLS, COLS), COLS)
            moves.append(pltpu.make_async_copy(w_out.at[:, here], own.at[y], stage_sems.at[y]))
    for move in moves:
        move.start()
    if final:
        keys, values, acc, maxima, sems = refs
    else:
        keys, values, sems = refs
        acc, maxima = outs
    count_rows = queries.shape[0]
    section = lax.axis_index("section")
    x, z = section // SIDE, section % SIDE
    count = jnp.int32(0)
    jobs = []
    for piece, offsets in zip(pieces, plan):
        for j, (dx, dz) in enumerate(offsets):
            source = lax.rem(x + dx, SIDE) * SIDE + lax.rem(z + dz, SIDE)
            needed = source < section
            here = pl.ds(j * HALF, HALF)
            there = pl.ds(pl.multiple_of(count * HALF, HALF), HALF)
            n = len(jobs)
            copies = (
                pltpu.make_async_copy(piece.at[here, :HD], keys.at[there, :], sems.at[n, 0]),
                pltpu.make_async_copy(piece.at[here, HD:], values.at[there, :HD], sems.at[n, 1]),
            )

            @pl.when(needed)
            def _():
                copies[0].start()
                copies[1].start()

            jobs.append((needed, copies))
            count = count + needed.astype(jnp.int32)
    if placing:
        cache[...] = jnp.zeros_like(cache) if diagonal else before[0][...]
        placed = jnp.int32(0)
        sources = [(piece, j * HALF, dx, dz, half)
                   for piece, offsets, half in zip(pieces, plan, halves)
                   for j, (dx, dz) in enumerate(offsets)]
        if diagonal:
            sources += [(begin[0], 0, 0, 0, 0), (begin[1], 0, 0, 0, 1)]
        for piece, row, dx, dz, half in sources:
            source = lax.rem(x + dx, SIDE) * SIDE + lax.rem(z + dz, SIDE)
            for rank in range(PAIR):
                slot = source * PAIR + rank
                inside = table[slot] - half * (HALF // BLOCK)
                found = (inside >= 0) & (inside < HALF // BLOCK)

                @pl.when(found)
                def _():
                    at = pl.ds(pl.multiple_of(row + inside * BLOCK, BLOCK), BLOCK)
                    pltpu.make_async_copy(piece.at[at, :], cache.at[slot], block_sem).start()

                placed = placed + found.astype(jnp.int32)
    values[:, HD:] = jnp.ones((values.shape[0], HD), BF)
    if diagonal:
        last = -(-len(jobs) // 4) * 4 * HALF
        for half in range(2):
            rows = slice(last + half * HALF, last + (half + 1) * HALF)
            keys[rows, :] = begin[half][:, :HD]
            values[rows, :HD] = begin[half][:, HD:]
        for start in range(0, ROWS, TILE):
            shape = (TILE, start + TILE)
            mask = lax.broadcasted_iota(jnp.int32, shape, 1) <= start + lax.broadcasted_iota(jnp.int32, shape, 0)
            kd, vd = keys[last : last + start + TILE, :], values[last : last + start + TILE, :]
            for h in range(HEADS):
                rows = pl.ds((start // SHARE * HEADS + h) * SHARE + start % SHARE, TILE)
                attend(queries[rows, :], kd, vd, acc, maxima, rows, mask, True)
    else:
        acc[...] = begin[0][...]
        maxima[...] = begin[1][...]
    for needed, copies in jobs:
        @pl.when(needed)
        def _():
            copies[0].wait()
            copies[1].wait()

    def part(base, size):
        at = pl.ds(pl.multiple_of(base, HALF), size)
        kd, vd = keys[at, :], values[at, :]
        for start in range(0, count_rows, TILE):
            rows = pl.ds(start, TILE)
            attend(queries[rows, :], kd, vd, acc, maxima, rows)

    def whole(i, _):
        part(i * 4 * HALF, 4 * HALF)
        return 0

    steps = (count + 3) // 4
    for n in range(3):
        @pl.when(count + n < steps * 4)
        def _():
            at = pl.ds(pl.multiple_of((count + n) * HALF, HALF), HALF)
            keys[at, :] = keys[:HALF, :]
            values[at, :] = jnp.zeros((HALF, 2 * HD), BF)

    lax.fori_loop(0, steps, whole, 0)

    if final:
        for h in range(HEADS):
            rows = slice(h * SHARE, (h + 1) * SHARE)
            outs[0][:, h * HD : (h + 1) * HD] = (acc[rows, :HD] / acc[rows, HD:]).astype(BF)
    if placing:
        def block(i, _):
            pltpu.make_async_copy(cache.at[0], cache.at[0], block_sem).wait()
            return 0

        lax.fori_loop(0, placed, block, 0)
    for move in moves:
        move.wait()


def attention(queries, begin, pieces, plan, name, diagonal=False, share=None, table=None, cache=None, halves=None, staged=()):
    subs = sum(len(p) for p in plan)
    final = share is not None
    rows = HEADS * SHARE if final else QROWS
    size = -(-subs // 4) * 4 * HALF + (ROWS if diagonal else 0)
    state_shape = [jax.ShapeDtypeStruct((rows, 2 * HD), F32), jax.ShapeDtypeStruct((rows, HD), F32)]
    scratch = [pltpu.VMEM((size, HD), BF), pltpu.VMEM((size, 2 * HD), BF)]
    if final:
        scratch += [pltpu.VMEM(s.shape, s.dtype) for s in state_shape]
        out_shape = [jax.ShapeDtypeStruct((SHARE, HEADS * HD), BF)]
        at = lambda i: (share, 0)
        in_specs = [pl.BlockSpec((rows, HD), at), pl.BlockSpec((rows, 2 * HD), at), pl.BlockSpec((rows, HD), at)]
        grid = (1,)
        out_specs = [pl.BlockSpec((SHARE, HEADS * HD), lambda i: (0, 0))]
    else:
        out_shape = state_shape
        in_specs = [WHOLE] * 3
        grid = ()
        out_specs = [WHOLE] * 2
    in_specs = in_specs + [ANY] * len(pieces)
    args = [queries, *begin, *pieces]
    scratch.append(pltpu.SemaphoreType.DMA((subs, 2)))
    if table is not None:
        in_specs.append(pl.BlockSpec(memory_space=pltpu.SMEM))
        args.append(table)
        if cache is not None:
            in_specs.append(WHOLE)
            args.append(cache)
        out_shape = out_shape + [jax.ShapeDtypeStruct((SIDE * SIDE * PAIR, BLOCK, 2 * HD), BF)]
        out_specs = out_specs + [WHOLE]
        scratch.append(pltpu.SemaphoreType.DMA)
    if staged:
        in_specs += [ANY] * len(staged)
        args += staged
        out_shape = out_shape + [jax.ShapeDtypeStruct(staged[1].shape, BF)] * 2
        out_specs = out_specs + [WHOLE] * len(staged)
        scratch.append(pltpu.SemaphoreType.DMA((SIDE + 1,)))
    return pl.pallas_call(
        functools.partial(attend_kernel, plan, halves, diagonal, final, len(staged)),
        grid=grid,
        in_specs=in_specs,
        out_specs=out_specs,
        out_shape=out_shape,
        scratch_shapes=scratch,
        compiler_params=limit(20),
        cost_estimate=pl.CostEstimate(
            flops=8 * rows * size * HD, bytes_accessed=8 << 20, transcendentals=rows * size
        ),
        name=name,
    )(*args)


def join_kernel(*refs):
    n = (len(refs) - 2) // 2
    for ins, out in ((refs[:n], refs[-2]), (refs[n : 2 * n], refs[-1])):
        for j, piece in enumerate(ins):
            out[j * HALF : (j + 1) * HALF, :] = piece[...]


def join(first, second):
    out = jax.ShapeDtypeStruct((len(first) * HALF, 2 * HD), BF)
    return pl.pallas_call(
        join_kernel,
        in_specs=[WHOLE] * (len(first) + len(second)),
        out_specs=[WHOLE] * 2,
        out_shape=[out] * 2,
        compiler_params=limit(8),
        cost_estimate=pl.CostEstimate(flops=0, bytes_accessed=2 << 20, transcendentals=0),
        name="join",
    )(*first, *second)


def cache_table(placement, section):
    owners = placement.reshape(SIDE * SIDE, ROWS // BLOCK)
    mine = owners == section
    before = jnp.arange(ROWS // BLOCK)[:, None] < jnp.arange(ROWS // BLOCK)[None, :]
    ranks = jnp.sum((mine[:, :, None] & before[None]).astype(jnp.int32), axis=1)
    hit = mine[:, None, :] & (ranks[:, None, :] == jnp.arange(PAIR)[None, :, None])
    number = jnp.arange(ROWS // BLOCK, dtype=jnp.int32) + 1
    return (jnp.sum(jnp.where(hit, number[None, None, :], 0), axis=-1) - 1).reshape(-1)


MID = SHARE // 2
PROJECT_LIMIT = 14


def term(offset, own, other, w_own, w_other):
    y = lax.rem(lax.axis_index("tp") // 2 + offset, SIDE)
    product = jnp.dot(own[...], w_own[y], preferred_element_type=F32)
    return product + jnp.dot(other[...], w_other[y], preferred_element_type=F32)


def opposite_kernel(own, other, w_own, w_other, top, bottom):
    product = term(2, own, other, w_own, w_other)
    top[...] = product[:MID].astype(BF)
    bottom[...] = product[MID:].astype(BF)


def neighbour_kernel(own, other, w_own, w_other, from_below, from_above, up, down):
    product = term(1, own, other, w_own, w_other)
    up[:MID] = (product[:MID] + from_below[...].astype(F32)).astype(BF)
    up[MID:] = product[MID:].astype(BF)
    product = term(3, own, other, w_own, w_other)
    down[:MID] = product[:MID].astype(BF)
    down[MID:] = (product[MID:] + from_above[...].astype(F32)).astype(BF)


def home_kernel(share, own, other, w_own, w_other, residual, out):
    rows = slice(share * SHARE, (share + 1) * SHARE)
    out[...] = residual[rows, :].astype(F32) + term(0, own, other, w_own, w_other)


def project(kernel, targets, terms, extra, out, name):
    return pl.pallas_call(
        kernel,
        in_specs=[WHOLE] * (len(terms) + len(extra)),
        out_specs=[WHOLE] * len(out),
        out_shape=[jax.ShapeDtypeStruct(shape, dtype) for shape, dtype in out],
        compiler_params=limit(PROJECT_LIMIT),
        cost_estimate=pl.CostEstimate(
            flops=4 * SHARE * 512 * COLS * targets, bytes_accessed=4 << 20, transcendentals=0
        ),
        name=name,
    )(*terms, *extra)


def finish_kernel(base, from_below, from_above, *refs):
    refs[-1][...] = (base[...] + from_below[...].astype(F32) + from_above[...].astype(F32)).astype(BF)


def finish(base, from_below, from_above, done, share):
    return pl.pallas_call(
        finish_kernel,
        grid=(1,),
        in_specs=[WHOLE] * 3 + [ANY] * len(done),
        out_specs=pl.BlockSpec((SHARE, COLS), lambda i: (share, 0)),
        out_shape=jax.ShapeDtypeStruct((ROWS, COLS), BF),
        input_output_aliases={3: 0} if done else {},
        compiler_params=limit(8),
        cost_estimate=pl.CostEstimate(flops=4 * SHARE * COLS, bytes_accessed=3 << 20, transcendentals=0),
        name="finish",
    )(base, from_below, from_above, *done)


def from_section(value, dx, dz):
    pairs = []
    for x in range(SIDE):
        for z in range(SIDE):
            pairs.append((((x + dx) % SIDE) * SIDE + (z + dz) % SIDE, x * SIDE + z))
    return lax.ppermute(value, "section", pairs)


def from_tp(value, dy, dc):
    pairs = []
    for y in range(SIDE):
        for c in range(2):
            pairs.append((((y + dy) % SIDE) * 2 + (c ^ dc), y * 2 + c))
    return lax.ppermute(value, "tp", pairs)


RING = (1, 3, 2)
ORDER = (0,) + RING


def per_device(tokens, gain, q_weight, q_bias, kv_weight, kv_bias, out_weight, placement):
    section = lax.axis_index("section")
    small, large = tables()
    factors, first, second, residual, w_send = norm_kv(
        tokens, gain[None, :], kv_weight, kv_bias[None, :], small, large, out_weight
    )
    w_other = from_tp(w_send, 0, 1)
    row_first = [from_section(first, 0, k) for k in RING]
    row_second = [from_section(second, k, 0) for k in RING]
    factors, row_first[0] = lax.optimization_barrier((factors, row_first[0]))
    queries = query(tokens, factors, gain[None, :], q_weight, q_bias[None, :], small, large)
    row_first[1], w_other, queries = lax.optimization_barrier((row_first[1], w_other, queries))
    all_first, all_second = join([first, *row_first], [second, *row_second])
    far_first = [from_section(all_first, k, 0) for k in RING[:2]]
    far_second = [from_section(all_second, 0, k) for k in RING[:2]]
    near = [[(0, k)] for k in RING] + [[(k, 0)] for k in RING]
    table = cache_table(placement, section)
    *state, cache = attention(
        queries,
        (first, second),
        row_first + row_second,
        near,
        "attention_near",
        diagonal=True,
        table=table,
        halves=[0] * 3 + [1] * 3,
    )
    all_first, all_second, *state = lax.optimization_barrier((all_first, all_second, *state))
    far_first.append(from_section(all_first, RING[2], 0))
    far_second.append(from_section(all_second, 0, RING[2]))
    far = [[(k, j) for j in ORDER] for k in RING], [[(j, k) for j in ORDER] for k in RING]
    *state, cache, w_own, w_other = attention(
        queries,
        state,
        far_first[:2] + far_second[:2],
        far[0][:2] + far[1][:2],
        "attention_far",
        table=table,
        cache=cache,
        halves=[0] * 2 + [1] * 2,
        staged=(out_weight, w_other),
    )
    pieces, plan = far_first[2:] + far_second[2:], far[0][2:] + far[1][2:]
    (early,) = attention(queries, state, pieces, plan, "attention_last", share=0)
    late, cache = attention(
        queries,
        state,
        pieces,
        plan,
        "attention_last",
        share=1,
        table=table,
        cache=cache,
        halves=[0, 1],
    )
    mixed = []
    for share, own in enumerate((early, late)):
        terms = (own, from_tp(own, 0, 1), w_own, w_other)
        top, bottom = project(opposite_kernel, 1, terms, [], [((MID, COLS), BF)] * 2, "project_opposite")
        from_below, from_above = from_tp(top, 3, 0), from_tp(bottom, 1, 0)
        up, down = project(
            neighbour_kernel, 2, terms, [from_below, from_above], [((SHARE, COLS), BF)] * 2, "project_neighbours"
        )
        from_below, from_above = from_tp(up, 3, 0), from_tp(down, 1, 0)
        (base,) = project(
            functools.partial(home_kernel, share), 1, terms, [residual], [((SHARE, COLS), F32)], "project_home"
        )
        mixed = [finish(base, from_below, from_above, mixed, share)]
    return mixed[0], cache


def solution(mesh):
    placed = (
        P("section", None),
        P(),
        P(None, "tp"),
        P("tp"),
        P(None, "tp"),
        P("tp"),
        P("tp", None),
        P(),
    )
    return jax.shard_map(
        per_device,
        mesh=mesh,
        in_specs=placed,
        out_specs=(P("section", "tp"), P("section", None, "tp")),
        check_vma=False,
    )
```

```python
import functools
import math

import jax
import jax.numpy as jnp
import numpy as np
from jax import lax
from jax.experimental import pallas as pl
from jax.experimental.pallas import tpu as pltpu
from jax.sharding import PartitionSpec as P

HD = 128
BLOCK = 16
SIDE = 4
HALF = 256
ROWS = 512
D = 8192
HEADS = 4
PAIR = 4
ROPE_BASE = 1000000.0
LOG2_SCALE = math.log2(math.e) / math.sqrt(HD)
SHARE = 256
COLS = 1024
limit = lambda mib: pltpu.CompilerParams(vmem_limit_bytes=mib * 1024 * 1024)
BF = jnp.bfloat16
F32 = jnp.float32
ANY = pl.BlockSpec(memory_space=pl.ANY)
WHOLE = pl.BlockSpec(memory_space=pltpu.VMEM)
FAR = pl.BlockSpec(memory_space=pltpu.HBM)


def tables():
    freq = ROPE_BASE ** (-(np.arange(HD // 2, dtype=np.float64) * 2.0 / HD))
    inner = np.arange(ROWS, dtype=np.float64)[:, None] * freq
    outer = ROWS * np.arange(SIDE * SIDE, dtype=np.float64)[:, None] * freq
    twice = lambda a: np.concatenate([a, a], -1)
    signed = lambda a: np.concatenate([-a, a], -1)
    small = np.concatenate([twice(np.cos(inner)), twice(np.sin(inner))], -1)
    large = np.concatenate(
        [twice(np.cos(outer)), twice(np.sin(outer)), signed(np.cos(outer)), signed(np.sin(outer))], -1
    )
    return small.astype(np.float32), large.astype(np.float32)


def angles(small, large):
    cos_r, sin_r = small[:, :HD], small[:, HD:]
    cos_s, sin_s = large[:, :HD], large[:, HD : 2 * HD]
    cos_g, sin_g = large[:, 2 * HD : 3 * HD], large[:, 3 * HD :]
    return cos_s * cos_r - sin_s * sin_r, sin_g * cos_r + cos_g * sin_r


def turn(value, cosine, sine):
    return value * cosine + pltpu.roll(value, HD // 2, 1) * sine


CHUNK = 64
GROUP = 32
DEPTH = 2048
AHEAD = 4
NORM_LIMIT = 56


def norm_kv_kernel(
    tokens, gain, weight, bias, small, large, w_out, factors, first, second, residual, w_send,
    tv, nv, wv, sv, total, st, sw, s_in, s_out
):
    chunks = ROWS // CHUNK
    rows_at = lambda i: pl.ds(pl.multiple_of(i * CHUNK, CHUNK), CHUNK)
    load = lambda i: pltpu.make_async_copy(tokens.at[rows_at(i), :], tv.at[rows_at(i), :], st.at[i])
    weights = [
        pltpu.make_async_copy(weight.at[k : k + DEPTH, :], wv.at[k : k + DEPTH, :], sw.at[k // DEPTH])
        for k in range(0, D, DEPTH)
    ]
    sibling = 1 - lax.rem(lax.axis_index("tp"), 2)
    fetches, sends = [], []
    for y in range(SIDE):
        here = pl.ds(pl.multiple_of((2 * y + sibling) * COLS, COLS), COLS)
        fetches.append(pltpu.make_async_copy(w_out.at[:, here], sv.at[y], s_in.at[y]))
        sends.append(pltpu.make_async_copy(sv.at[y], w_send.at[y], s_out.at[y]))
    for i in range(AHEAD):
        load(i).start()

    def chunk(i, _):
        load(i).wait()

        @pl.when(i < chunks - AHEAD)
        def _():
            load(i + AHEAD).start()

        for n in range(AHEAD):
            @pl.when(i == chunks - AHEAD + n)
            def _():
                weights[n].start()

        for g in range(0, CHUNK, GROUP):
            rows = pl.ds(pl.multiple_of(i * CHUNK + g, GROUP), GROUP)
            squares = jnp.zeros((GROUP, 128), F32)
            for c in range(0, D, 1024):
                wide = tv[rows, c : c + 1024].astype(F32)
                square = wide * wide
                for k in range(0, 1024, 128):
                    squares = squares + square[:, k : k + 128]
            meansq = jnp.sum(squares, axis=1, keepdims=True) * (1.0 / D)
            factor = lax.rsqrt(meansq + 1e-06)
            factors[rows, :] = jnp.broadcast_to(factor, (GROUP, 128))
            for c in range(0, D, 1024):
                wide = tv[rows, c : c + 1024].astype(F32)
                nv[rows, c : c + 1024] = (wide * factor * gain[:, c : c + 1024]).astype(BF)
        return 0

    lax.fori_loop(0, chunks, chunk, 0)
    for n in range(AHEAD, D // DEPTH):
        weights[n].start()
    for copy in fetches:
        copy.start()
    residual[...] = tv[:, pl.ds(pl.multiple_of(lax.axis_index("tp") * COLS, COLS), COLS)]
    for copy in weights:
        copy.wait()
    total[...] = jnp.dot(nv[...], wv[...], preferred_element_type=F32) + bias[...]
    for n in range(SIDE):
        fetches[n].wait()
        sends[n].start()
    cosine, sine = angles(small[...], large[pl.ds(lax.axis_index("section"), 1), :])
    keys = turn(total[:, :HD], cosine, sine).astype(BF)
    values = total[:, HD:].astype(BF)
    for half, out in enumerate((first, second)):
        rows = slice(half * HALF, (half + 1) * HALF)
        out[:, :HD] = keys[rows]
        out[:, HD:] = values[rows]
    for copy in sends:
        copy.wait()


def norm_kv(tokens, gain, weight, bias, small, large, w_out):
    half = jax.ShapeDtypeStruct((HALF, 2 * HD), BF)
    return pl.pallas_call(
        norm_kv_kernel,
        in_specs=[ANY, WHOLE, ANY, WHOLE, WHOLE, WHOLE, ANY],
        out_specs=[WHOLE] * 4 + [ANY],
        out_shape=[
            jax.ShapeDtypeStruct((ROWS, 128), F32),
            half,
            half,
            jax.ShapeDtypeStruct((ROWS, COLS), BF),
            jax.ShapeDtypeStruct((SIDE, HEADS * HD, COLS), BF),
        ],
        scratch_shapes=[
            pltpu.VMEM((ROWS, D), BF),
            pltpu.VMEM((ROWS, D), BF),
            pltpu.VMEM((D, 2 * HD), BF),
            pltpu.VMEM((SIDE, HEADS * HD, COLS), BF),
            pltpu.VMEM((ROWS, 2 * HD), F32),
            pltpu.SemaphoreType.DMA((ROWS // CHUNK,)),
            pltpu.SemaphoreType.DMA((D // DEPTH,)),
            pltpu.SemaphoreType.DMA((SIDE,)),
            pltpu.SemaphoreType.DMA((SIDE,)),
        ],
        compiler_params=limit(NORM_LIMIT),
        cost_estimate=pl.CostEstimate(flops=2 * ROWS * D * 256, bytes_accessed=20 << 20, transcendentals=0),
        name="norm_kv",
    )(tokens, gain, weight, bias, small, large, w_out)


Q_DEPTH = 1024
Q_AHEAD = 4
Q_ROWS = 256


def query_kernel(tokens, factors, gain, weight, bias, small, large, out, tv, nv, wv, total, sems):
    steps = D // Q_DEPTH
    copies = []
    for n in range(steps):
        at = slice(n * Q_DEPTH, (n + 1) * Q_DEPTH)
        copies.append(
            (
                pltpu.make_async_copy(tokens.at[:, at], tv.at[n], sems.at[n, 0]),
                pltpu.make_async_copy(weight.at[at, :], wv.at[n], sems.at[n, 1]),
            )
        )
    begin = lambda n: [copy.start() for copy in copies[n]]
    for n in range(Q_AHEAD):
        begin(n)
    total[...] = jnp.broadcast_to(bias[...], total.shape)

    def scale(n):
        for copy in copies[n]:
            copy.wait()
        if n + Q_AHEAD < steps:
            begin(n + Q_AHEAD)

    def rows_of(n, r):
        factor = factors[r : r + Q_ROWS, :1]
        at = slice(n * Q_DEPTH, (n + 1) * Q_DEPTH)
        nv[n, r : r + Q_ROWS, :] = (tv[n, r : r + Q_ROWS, :].astype(F32) * factor * gain[:, at]).astype(BF)

    scale(0)
    for r in range(0, ROWS, Q_ROWS):
        rows_of(0, r)
    for n in range(steps):
        if n + 1 < steps:
            scale(n + 1)
        for r in range(0, ROWS, Q_ROWS):
            total[r : r + Q_ROWS, :] += jnp.dot(nv[n, r : r + Q_ROWS, :], wv[n], preferred_element_type=F32)
            if n + 1 < steps:
                rows_of(n + 1, r)
    cosine, sine = angles(small[...], large[pl.ds(lax.axis_index("section"), 1), :])
    for h in range(HEADS):
        value = turn(total[:, h * HD : (h + 1) * HD], cosine, sine).astype(BF)
        for n in range(ROWS // SHARE):
            start = (n * HEADS + h) * SHARE
            out[start : start + SHARE, :] = value[n * SHARE : (n + 1) * SHARE]


def query(tokens, factors, gain, weight, bias, small, large):
    width = HEADS * HD
    steps = D // Q_DEPTH
    return pl.pallas_call(
        query_kernel,
        in_specs=[ANY, WHOLE, WHOLE, ANY, WHOLE, WHOLE, WHOLE],
        out_specs=WHOLE,
        out_shape=jax.ShapeDtypeStruct((HEADS * ROWS, HD), BF),
        scratch_shapes=[
            pltpu.VMEM((steps, ROWS, Q_DEPTH), BF),
            pltpu.VMEM((steps, ROWS, Q_DEPTH), BF),
            pltpu.VMEM((steps, Q_DEPTH, width), BF),
            pltpu.VMEM((ROWS, width), F32),
            pltpu.SemaphoreType.DMA((steps, 2)),
        ],
        compiler_params=limit(56),
        cost_estimate=pl.CostEstimate(flops=2 * ROWS * D * 512, bytes_accessed=16 << 20, transcendentals=0),
        name="query",
    )(tokens, factors, gain, weight, bias, small, large)


TILE = 128
QROWS = HEADS * ROWS


def attend(queries, keys, values, acc, maxima, rows, mask=None, first=False):
    scores = lax.dot_general(queries, keys, (((1,), (1,)), ((), ())), preferred_element_type=F32)
    if mask is not None:
        scores = jnp.where(mask, scores, -1e30)
    highest = jnp.max(scores, axis=1, keepdims=True)
    if first:
        newest = jnp.broadcast_to(highest, (rows.size, HD))
    else:
        old = maxima[rows, :]
        newest = jnp.maximum(old, highest)
        rescale = jnp.exp2((old - newest) * LOG2_SCALE)
    maxima[rows, :] = newest
    weights = jnp.exp2(scores * LOG2_SCALE - newest[:, :1] * LOG2_SCALE).astype(BF)
    added = jnp.dot(weights, values, preferred_element_type=F32)
    if first:
        acc[rows, :] = added
    else:
        acc[rows, :HD] = acc[rows, :HD] * rescale + added[:, :HD]
        acc[rows, HD:] = acc[rows, HD:] * rescale + added[:, HD:]


def attend_kernel(plan, halves, diagonal, final, staged, *refs):
    refs = list(refs)
    take = lambda n: [refs.pop(0) for _ in range(n)]
    (queries,) = take(1)
    begin = take(2)
    pieces = take(len(plan))
    placing = halves is not None
    if placing:
        (table,) = take(1)
        before = [] if diagonal else take(1)
    far_away = take(staged)
    outs = take(1 if final else 2)
    if placing:
        (cache,) = take(1)
    moves = list(zip(far_away, take(staged)))
    if staged:
        stage_sems = refs.pop()
    if placing:
        block_sem = refs.pop()
    if staged:
        (w_out, own), (w_other, other) = moves
        core = lax.rem(lax.axis_index("tp"), 2)
        moves = [pltpu.make_async_copy(w_other, other, stage_sems.at[SIDE])]
        for y in range(SIDE):
            here = pl.ds(pl.multiple_of((2 * y + core) * COLS, COLS), COLS)
            moves.append(pltpu.make_async_copy(w_out.at[:, here], own.at[y], stage_sems.at[y]))
    for move in moves:
        move.start()
    if final:
        keys, values, acc, maxima, sems = refs
    else:
        keys, values, sems = refs
        acc, maxima = outs
    count_rows = queries.shape[0]
    section = lax.axis_index("section")
    x, z = section // SIDE, section % SIDE
    count = jnp.int32(0)
    jobs = []
    for piece, offsets in zip(pieces, plan):
        for j, (dx, dz) in enumerate(offsets):
            source = lax.rem(x + dx, SIDE) * SIDE + lax.rem(z + dz, SIDE)
            needed = source < section
            here = pl.ds(j * HALF, HALF)
            there = pl.ds(pl.multiple_of(count * HALF, HALF), HALF)
            n = len(jobs)
            copies = (
                pltpu.make_async_copy(piece.at[here, :HD], keys.at[there, :], sems.at[n, 0]),
                pltpu.make_async_copy(piece.at[here, HD:], values.at[there, :HD], sems.at[n, 1]),
            )

            @pl.when(needed)
            def _():
                copies[0].start()
                copies[1].start()

            jobs.append((needed, copies))
            count = count + needed.astype(jnp.int32)
    if placing:
        cache[...] = jnp.zeros_like(cache) if diagonal else before[0][...]
        placed = jnp.int32(0)
        sources = [(piece, j * HALF, dx, dz, half)
                   for piece, offsets, half in zip(pieces, plan, halves)
                   for j, (dx, dz) in enumerate(offsets)]
        if diagonal:
            sources += [(begin[0], 0, 0, 0, 0), (begin[1], 0, 0, 0, 1)]
        for piece, row, dx, dz, half in sources:
            source = lax.rem(x + dx, SIDE) * SIDE + lax.rem(z + dz, SIDE)
            for rank in range(PAIR):
                slot = source * PAIR + rank
                inside = table[slot] - half * (HALF // BLOCK)
                found = (inside >= 0) & (inside < HALF // BLOCK)

                @pl.when(found)
                def _():
                    at = pl.ds(pl.multiple_of(row + inside * BLOCK, BLOCK), BLOCK)
                    pltpu.make_async_copy(piece.at[at, :], cache.at[slot], block_sem).start()

                placed = placed + found.astype(jnp.int32)
    values[:, HD:] = jnp.ones((values.shape[0], HD), BF)
    if diagonal:
        last = -(-len(jobs) // 4) * 4 * HALF
        for half in range(2):
            rows = slice(last + half * HALF, last + (half + 1) * HALF)
            keys[rows, :] = begin[half][:, :HD]
            values[rows, :HD] = begin[half][:, HD:]
        for start in range(0, ROWS, TILE):
            shape = (TILE, start + TILE)
            mask = lax.broadcasted_iota(jnp.int32, shape, 1) <= start + lax.broadcasted_iota(jnp.int32, shape, 0)
            kd, vd = keys[last : last + start + TILE, :], values[last : last + start + TILE, :]
            for h in range(HEADS):
                rows = pl.ds((start // SHARE * HEADS + h) * SHARE + start % SHARE, TILE)
                attend(queries[rows, :], kd, vd, acc, maxima, rows, mask, True)
    else:
        acc[...] = begin[0][...]
        maxima[...] = begin[1][...]
    for needed, copies in jobs:
        @pl.when(needed)
        def _():
            copies[0].wait()
            copies[1].wait()

    def part(base, size):
        at = pl.ds(pl.multiple_of(base, HALF), size)
        kd, vd = keys[at, :], values[at, :]
        for start in range(0, count_rows, TILE):
            rows = pl.ds(start, TILE)
            attend(queries[rows, :], kd, vd, acc, maxima, rows)

    def whole(i, _):
        part(i * 4 * HALF, 4 * HALF)
        return 0

    steps = (count + 3) // 4
    for n in range(3):
        @pl.when(count + n < steps * 4)
        def _():
            at = pl.ds(pl.multiple_of((count + n) * HALF, HALF), HALF)
            keys[at, :] = keys[:HALF, :]
            values[at, :] = jnp.zeros((HALF, 2 * HD), BF)

    lax.fori_loop(0, steps, whole, 0)

    if final:
        for h in range(HEADS):
            rows = slice(h * SHARE, (h + 1) * SHARE)
            outs[0][:, h * HD : (h + 1) * HD] = (acc[rows, :HD] / acc[rows, HD:]).astype(BF)
    if placing:
        def block(i, _):
            pltpu.make_async_copy(cache.at[0], cache.at[0], block_sem).wait()
            return 0

        lax.fori_loop(0, placed, block, 0)
    for move in moves:
        move.wait()


def attention(queries, begin, pieces, plan, name, diagonal=False, share=None, table=None, cache=None, halves=None, staged=()):
    subs = sum(len(p) for p in plan)
    final = share is not None
    rows = HEADS * SHARE if final else QROWS
    size = -(-subs // 4) * 4 * HALF + (ROWS if diagonal else 0)
    state_shape = [jax.ShapeDtypeStruct((rows, 2 * HD), F32), jax.ShapeDtypeStruct((rows, HD), F32)]
    scratch = [pltpu.VMEM((size, HD), BF), pltpu.VMEM((size, 2 * HD), BF)]
    if final:
        scratch += [pltpu.VMEM(s.shape, s.dtype) for s in state_shape]
        out_shape = [jax.ShapeDtypeStruct((SHARE, HEADS * HD), BF)]
        at = lambda i: (share, 0)
        in_specs = [pl.BlockSpec((rows, HD), at), pl.BlockSpec((rows, 2 * HD), at), pl.BlockSpec((rows, HD), at)]
        grid = (1,)
        out_specs = [pl.BlockSpec((SHARE, HEADS * HD), lambda i: (0, 0))]
    else:
        out_shape = state_shape
        in_specs = [WHOLE] * 3
        grid = ()
        out_specs = [WHOLE] * 2
    in_specs = in_specs + [ANY] * len(pieces)
    args = [queries, *begin, *pieces]
    scratch.append(pltpu.SemaphoreType.DMA((subs, 2)))
    if table is not None:
        in_specs.append(pl.BlockSpec(memory_space=pltpu.SMEM))
        args.append(table)
        if cache is not None:
            in_specs.append(WHOLE)
            args.append(cache)
        out_shape = out_shape + [jax.ShapeDtypeStruct((SIDE * SIDE * PAIR, BLOCK, 2 * HD), BF)]
        out_specs = out_specs + [WHOLE]
        scratch.append(pltpu.SemaphoreType.DMA)
    if staged:
        in_specs += [ANY] * len(staged)
        args += staged
        out_shape = out_shape + [jax.ShapeDtypeStruct(staged[1].shape, BF)] * 2
        out_specs = out_specs + [WHOLE] * len(staged)
        scratch.append(pltpu.SemaphoreType.DMA((SIDE + 1,)))
    return pl.pallas_call(
        functools.partial(attend_kernel, plan, halves, diagonal, final, len(staged)),
        grid=grid,
        in_specs=in_specs,
        out_specs=out_specs,
        out_shape=out_shape,
        scratch_shapes=scratch,
        compiler_params=limit(20),
        cost_estimate=pl.CostEstimate(
            flops=8 * rows * size * HD, bytes_accessed=8 << 20, transcendentals=rows * size
        ),
        name=name,
    )(*args)


def join_kernel(*refs):
    n = (len(refs) - 2) // 2
    for ins, out in ((refs[:n], refs[-2]), (refs[n : 2 * n], refs[-1])):
        for j, piece in enumerate(ins):
            out[j * HALF : (j + 1) * HALF, :] = piece[...]


def join(first, second):
    out = jax.ShapeDtypeStruct((len(first) * HALF, 2 * HD), BF)
    return pl.pallas_call(
        join_kernel,
        in_specs=[WHOLE] * (len(first) + len(second)),
        out_specs=[WHOLE] * 2,
        out_shape=[out] * 2,
        compiler_params=limit(8),
        cost_estimate=pl.CostEstimate(flops=0, bytes_accessed=2 << 20, transcendentals=0),
        name="join",
    )(*first, *second)


def cache_table(placement, section):
    owners = placement.reshape(SIDE * SIDE, ROWS // BLOCK)
    mine = owners == section
    before = jnp.arange(ROWS // BLOCK)[:, None] < jnp.arange(ROWS // BLOCK)[None, :]
    ranks = jnp.sum((mine[:, :, None] & before[None]).astype(jnp.int32), axis=1)
    hit = mine[:, None, :] & (ranks[:, None, :] == jnp.arange(PAIR)[None, :, None])
    number = jnp.arange(ROWS // BLOCK, dtype=jnp.int32) + 1
    return (jnp.sum(jnp.where(hit, number[None, None, :], 0), axis=-1) - 1).reshape(-1)


MID = SHARE // 2
PROJECT_LIMIT = 14


def term(offset, own, other, w_own, w_other):
    y = lax.rem(lax.axis_index("tp") // 2 + offset, SIDE)
    product = jnp.dot(own[...], w_own[y], preferred_element_type=F32)
    return product + jnp.dot(other[...], w_other[y], preferred_element_type=F32)


def opposite_kernel(own, other, w_own, w_other, top, bottom):
    product = term(2, own, other, w_own, w_other)
    top[...] = product[:MID].astype(BF)
    bottom[...] = product[MID:].astype(BF)


def neighbour_kernel(own, other, w_own, w_other, from_below, from_above, up, down):
    product = term(1, own, other, w_own, w_other)
    up[:MID] = (product[:MID] + from_below[...].astype(F32)).astype(BF)
    up[MID:] = product[MID:].astype(BF)
    product = term(3, own, other, w_own, w_other)
    down[:MID] = product[:MID].astype(BF)
    down[MID:] = (product[MID:] + from_above[...].astype(F32)).astype(BF)


def home_kernel(share, own, other, w_own, w_other, residual, out):
    rows = slice(share * SHARE, (share + 1) * SHARE)
    out[...] = residual[rows, :].astype(F32) + term(0, own, other, w_own, w_other)


def project(kernel, targets, terms, extra, out, name):
    return pl.pallas_call(
        kernel,
        in_specs=[WHOLE] * (len(terms) + len(extra)),
        out_specs=[WHOLE] * len(out),
        out_shape=[jax.ShapeDtypeStruct(shape, dtype) for shape, dtype in out],
        compiler_params=limit(PROJECT_LIMIT),
        cost_estimate=pl.CostEstimate(
            flops=4 * SHARE * 512 * COLS * targets, bytes_accessed=4 << 20, transcendentals=0
        ),
        name=name,
    )(*terms, *extra)


def finish_kernel(base, from_below, from_above, *refs):
    refs[-1][...] = (base[...] + from_below[...].astype(F32) + from_above[...].astype(F32)).astype(BF)


def finish(base, from_below, from_above, done, share):
    return pl.pallas_call(
        finish_kernel,
        grid=(1,),
        in_specs=[WHOLE] * 3 + [ANY] * len(done),
        out_specs=pl.BlockSpec((SHARE, COLS), lambda i: (share, 0)),
        out_shape=jax.ShapeDtypeStruct((ROWS, COLS), BF),
        input_output_aliases={3: 0} if done else {},
        compiler_params=limit(8),
        cost_estimate=pl.CostEstimate(flops=4 * SHARE * COLS, bytes_accessed=3 << 20, transcendentals=0),
        name="finish",
    )(base, from_below, from_above, *done)


def from_section(value, dx, dz):
    pairs = []
    for x in range(SIDE):
        for z in range(SIDE):
            pairs.append((((x + dx) % SIDE) * SIDE + (z + dz) % SIDE, x * SIDE + z))
    return lax.ppermute(value, "section", pairs)


def from_tp(value, dy, dc):
    pairs = []
    for y in range(SIDE):
        for c in range(2):
            pairs.append((((y + dy) % SIDE) * 2 + (c ^ dc), y * 2 + c))
    return lax.ppermute(value, "tp", pairs)


RING = (1, 3, 2)
ORDER = (0,) + RING


def per_device(tokens, gain, q_weight, q_bias, kv_weight, kv_bias, out_weight, placement):
    section = lax.axis_index("section")
    small, large = tables()
    factors, first, second, residual, w_send = norm_kv(
        tokens, gain[None, :], kv_weight, kv_bias[None, :], small, large, out_weight
    )
    w_other = from_tp(w_send, 0, 1)
    row_first = [from_section(first, 0, k) for k in RING]
    row_second = [from_section(second, k, 0) for k in RING]
    factors, row_first[0] = lax.optimization_barrier((factors, row_first[0]))
    queries = query(tokens, factors, gain[None, :], q_weight, q_bias[None, :], small, large)
    row_first[1], w_other, queries = lax.optimization_barrier((row_first[1], w_other, queries))
    all_first, all_second = join([first, *row_first], [second, *row_second])
    far_first = [from_section(all_first, k, 0) for k in RING[:2]]
    far_second = [from_section(all_second, 0, k) for k in RING[:2]]
    near = [[(0, k)] for k in RING] + [[(k, 0)] for k in RING]
    table = cache_table(placement, section)
    *state, cache = attention(
        queries,
        (first, second),
        row_first + row_second,
        near,
        "attention_near",
        diagonal=True,
        table=table,
        halves=[0] * 3 + [1] * 3,
    )
    all_first, all_second, *state = lax.optimization_barrier((all_first, all_second, *state))
    far_first.append(from_section(all_first, RING[2], 0))
    far_second.append(from_section(all_second, 0, RING[2]))
    far = [[(k, j) for j in ORDER] for k in RING], [[(j, k) for j in ORDER] for k in RING]
    *state, cache = attention(
        queries,
        state,
        far_first[:2] + far_second[:2],
        far[0][:2] + far[1][:2],
        "attention_far",
        table=table,
        cache=cache,
        halves=[0] * 2 + [1] * 2,
    )
    pieces, plan = far_first[2:] + far_second[2:], far[0][2:] + far[1][2:]
    (early,) = attention(queries, state, pieces, plan, "attention_last", share=0)
    late, cache, w_own, w_other = attention(
        queries,
        state,
        pieces,
        plan,
        "attention_last",
        share=1,
        table=table,
        cache=cache,
        halves=[0, 1],
        staged=(out_weight, w_other),
    )
    mixed = []
    for share, own in enumerate((early, late)):
        terms = (own, from_tp(own, 0, 1), w_own, w_other)
        top, bottom = project(opposite_kernel, 1, terms, [], [((MID, COLS), BF)] * 2, "project_opposite")
        from_below, from_above = from_tp(top, 3, 0), from_tp(bottom, 1, 0)
        up, down = project(
            neighbour_kernel, 2, terms, [from_below, from_above], [((SHARE, COLS), BF)] * 2, "project_neighbours"
        )
        from_below, from_above = from_tp(up, 3, 0), from_tp(down, 1, 0)
        (base,) = project(
            functools.partial(home_kernel, share), 1, terms, [residual], [((SHARE, COLS), F32)], "project_home"
        )
        mixed = [finish(base, from_below, from_above, mixed, share)]
    return mixed[0], cache


def solution(mesh):
    placed = (
        P("section", None),
        P(),
        P(None, "tp"),
        P("tp"),
        P(None, "tp"),
        P("tp"),
        P("tp", None),
        P(),
    )
    return jax.shard_map(
        per_device,
        mesh=mesh,
        in_specs=placed,
        out_specs=(P("section", "tp"), P("section", None, "tp")),
        check_vma=False,
    )
```

```python
import functools
import math

import jax
import jax.numpy as jnp
import numpy as np
from jax import lax
from jax.experimental import pallas as pl
from jax.experimental.pallas import tpu as pltpu
from jax.sharding import PartitionSpec as P

HD = 128
BLOCK = 16
SIDE = 4
HALF = 256
ROWS = 512
D = 8192
HEADS = 4
PAIR = 4
ROPE_BASE = 1000000.0
LOG2_SCALE = math.log2(math.e) / math.sqrt(HD)
SHARE = 256
COLS = 1024
limit = lambda mib: pltpu.CompilerParams(vmem_limit_bytes=mib * 1024 * 1024)
BF = jnp.bfloat16
F32 = jnp.float32
ANY = pl.BlockSpec(memory_space=pl.ANY)
WHOLE = pl.BlockSpec(memory_space=pltpu.VMEM)
FAR = pl.BlockSpec(memory_space=pltpu.HBM)


def tables():
    freq = ROPE_BASE ** (-(np.arange(HD // 2, dtype=np.float64) * 2.0 / HD))
    inner = np.arange(ROWS, dtype=np.float64)[:, None] * freq
    outer = ROWS * np.arange(SIDE * SIDE, dtype=np.float64)[:, None] * freq
    twice = lambda a: np.concatenate([a, a], -1)
    signed = lambda a: np.concatenate([-a, a], -1)
    small = np.concatenate([twice(np.cos(inner)), twice(np.sin(inner))], -1)
    large = np.concatenate(
        [twice(np.cos(outer)), twice(np.sin(outer)), signed(np.cos(outer)), signed(np.sin(outer))], -1
    )
    return small.astype(np.float32), large.astype(np.float32)


def angles(small, large):
    cos_r, sin_r = small[:, :HD], small[:, HD:]
    cos_s, sin_s = large[:, :HD], large[:, HD : 2 * HD]
    cos_g, sin_g = large[:, 2 * HD : 3 * HD], large[:, 3 * HD :]
    return cos_s * cos_r - sin_s * sin_r, sin_g * cos_r + cos_g * sin_r


def turn(value, cosine, sine):
    return value * cosine + pltpu.roll(value, HD // 2, 1) * sine


CHUNK = 64
GROUP = 32
DEPTH = 2048
AHEAD = 4
NORM_LIMIT = 56


def norm_kv_kernel(
    tokens, gain, weight, bias, small, large, w_out, factors, first, second, residual, w_send,
    tv, nv, wv, sv, total, st, sw, s_in, s_out
):
    chunks = ROWS // CHUNK
    rows_at = lambda i: pl.ds(pl.multiple_of(i * CHUNK, CHUNK), CHUNK)
    load = lambda i: pltpu.make_async_copy(tokens.at[rows_at(i), :], tv.at[rows_at(i), :], st.at[i])
    weights = [
        pltpu.make_async_copy(weight.at[k : k + DEPTH, :], wv.at[k : k + DEPTH, :], sw.at[k // DEPTH])
        for k in range(0, D, DEPTH)
    ]
    sibling = 1 - lax.rem(lax.axis_index("tp"), 2)
    fetches, sends = [], []
    for y in range(SIDE):
        here = pl.ds(pl.multiple_of((2 * y + sibling) * COLS, COLS), COLS)
        fetches.append(pltpu.make_async_copy(w_out.at[:, here], sv.at[y], s_in.at[y]))
        sends.append(pltpu.make_async_copy(sv.at[y], w_send.at[y], s_out.at[y]))
    for i in range(AHEAD):
        load(i).start()

    def chunk(i, _):
        load(i).wait()

        @pl.when(i < chunks - AHEAD)
        def _():
            load(i + AHEAD).start()

        for n in range(AHEAD):
            @pl.when(i == chunks - AHEAD + n)
            def _():
                weights[n].start()

        for g in range(0, CHUNK, GROUP):
            rows = pl.ds(pl.multiple_of(i * CHUNK + g, GROUP), GROUP)
            squares = jnp.zeros((GROUP, 128), F32)
            for c in range(0, D, 1024):
                wide = tv[rows, c : c + 1024].astype(F32)
                square = wide * wide
                for k in range(0, 1024, 128):
                    squares = squares + square[:, k : k + 128]
            meansq = jnp.sum(squares, axis=1, keepdims=True) * (1.0 / D)
            factor = lax.rsqrt(meansq + 1e-06)
            factors[rows, :] = jnp.broadcast_to(factor, (GROUP, 128))
            for c in range(0, D, 1024):
                wide = tv[rows, c : c + 1024].astype(F32)
                nv[rows, c : c + 1024] = (wide * factor * gain[:, c : c + 1024]).astype(BF)
        return 0

    lax.fori_loop(0, chunks, chunk, 0)
    for n in range(AHEAD, D // DEPTH):
        weights[n].start()
    for copy in fetches:
        copy.start()
    residual[...] = tv[:, pl.ds(pl.multiple_of(lax.axis_index("tp") * COLS, COLS), COLS)]
    for copy in weights:
        copy.wait()
    total[...] = jnp.dot(nv[...], wv[...], preferred_element_type=F32) + bias[...]
    for n in range(SIDE):
        fetches[n].wait()
        sends[n].start()
    cosine, sine = angles(small[...], large[pl.ds(lax.axis_index("section"), 1), :])
    keys = turn(total[:, :HD], cosine, sine).astype(BF)
    values = total[:, HD:].astype(BF)
    for half, out in enumerate((first, second)):
        rows = slice(half * HALF, (half + 1) * HALF)
        out[:, :HD] = keys[rows]
        out[:, HD:] = values[rows]
    for copy in sends:
        copy.wait()


def norm_kv(tokens, gain, weight, bias, small, large, w_out):
    half = jax.ShapeDtypeStruct((HALF, 2 * HD), BF)
    return pl.pallas_call(
        norm_kv_kernel,
        in_specs=[ANY, WHOLE, ANY, WHOLE, WHOLE, WHOLE, ANY],
        out_specs=[WHOLE] * 4 + [ANY],
        out_shape=[
            jax.ShapeDtypeStruct((ROWS, 128), F32),
            half,
            half,
            jax.ShapeDtypeStruct((ROWS, COLS), BF),
            jax.ShapeDtypeStruct((SIDE, HEADS * HD, COLS), BF),
        ],
        scratch_shapes=[
            pltpu.VMEM((ROWS, D), BF),
            pltpu.VMEM((ROWS, D), BF),
            pltpu.VMEM((D, 2 * HD), BF),
            pltpu.VMEM((SIDE, HEADS * HD, COLS), BF),
            pltpu.VMEM((ROWS, 2 * HD), F32),
            pltpu.SemaphoreType.DMA((ROWS // CHUNK,)),
            pltpu.SemaphoreType.DMA((D // DEPTH,)),
            pltpu.SemaphoreType.DMA((SIDE,)),
            pltpu.SemaphoreType.DMA((SIDE,)),
        ],
        compiler_params=limit(NORM_LIMIT),
        cost_estimate=pl.CostEstimate(flops=2 * ROWS * D * 256, bytes_accessed=20 << 20, transcendentals=0),
        name="norm_kv",
    )(tokens, gain, weight, bias, small, large, w_out)


Q_DEPTH = 1024
Q_AHEAD = 4
Q_ROWS = 256


def query_kernel(tokens, factors, gain, weight, bias, small, large, out, tv, nv, wv, total, sems):
    steps = D // Q_DEPTH
    copies = []
    for n in range(steps):
        at = slice(n * Q_DEPTH, (n + 1) * Q_DEPTH)
        copies.append(
            (
                pltpu.make_async_copy(tokens.at[:, at], tv.at[n], sems.at[n, 0]),
                pltpu.make_async_copy(weight.at[at, :], wv.at[n], sems.at[n, 1]),
            )
        )
    begin = lambda n: [copy.start() for copy in copies[n]]
    for n in range(Q_AHEAD):
        begin(n)
    total[...] = jnp.broadcast_to(bias[...], total.shape)

    def scale(n):
        for copy in copies[n]:
            copy.wait()
        if n + Q_AHEAD < steps:
            begin(n + Q_AHEAD)

    def rows_of(n, r):
        factor = factors[r : r + Q_ROWS, :1]
        at = slice(n * Q_DEPTH, (n + 1) * Q_DEPTH)
        nv[n, r : r + Q_ROWS, :] = (tv[n, r : r + Q_ROWS, :].astype(F32) * factor * gain[:, at]).astype(BF)

    scale(0)
    for r in range(0, ROWS, Q_ROWS):
        rows_of(0, r)
    for n in range(steps):
        if n + 1 < steps:
            scale(n + 1)
        for r in range(0, ROWS, Q_ROWS):
            total[r : r + Q_ROWS, :] += jnp.dot(nv[n, r : r + Q_ROWS, :], wv[n], preferred_element_type=F32)
            if n + 1 < steps:
                rows_of(n + 1, r)
    cosine, sine = angles(small[...], large[pl.ds(lax.axis_index("section"), 1), :])
    for h in range(HEADS):
        value = turn(total[:, h * HD : (h + 1) * HD], cosine, sine).astype(BF)
        for n in range(ROWS // SHARE):
            start = (n * HEADS + h) * SHARE
            out[start : start + SHARE, :] = value[n * SHARE : (n + 1) * SHARE]


def query(tokens, factors, gain, weight, bias, small, large):
    width = HEADS * HD
    steps = D // Q_DEPTH
    return pl.pallas_call(
        query_kernel,
        in_specs=[ANY, WHOLE, WHOLE, ANY, WHOLE, WHOLE, WHOLE],
        out_specs=WHOLE,
        out_shape=jax.ShapeDtypeStruct((HEADS * ROWS, HD), BF),
        scratch_shapes=[
            pltpu.VMEM((steps, ROWS, Q_DEPTH), BF),
            pltpu.VMEM((steps, ROWS, Q_DEPTH), BF),
            pltpu.VMEM((steps, Q_DEPTH, width), BF),
            pltpu.VMEM((ROWS, width), F32),
            pltpu.SemaphoreType.DMA((steps, 2)),
        ],
        compiler_params=limit(56),
        cost_estimate=pl.CostEstimate(flops=2 * ROWS * D * 512, bytes_accessed=16 << 20, transcendentals=0),
        name="query",
    )(tokens, factors, gain, weight, bias, small, large)


TILE = 128
QROWS = HEADS * ROWS


def attend(queries, keys, values, acc, maxima, rows, mask=None, first=False):
    scores = lax.dot_general(queries, keys, (((1,), (1,)), ((), ())), preferred_element_type=F32)
    if mask is not None:
        scores = jnp.where(mask, scores, -1e30)
    highest = jnp.max(scores, axis=1, keepdims=True)
    if first:
        newest = jnp.broadcast_to(highest, (rows.size, HD))
    else:
        old = maxima[rows, :]
        newest = jnp.maximum(old, highest)
        rescale = jnp.exp2((old - newest) * LOG2_SCALE)
    maxima[rows, :] = newest
    weights = jnp.exp2(scores * LOG2_SCALE - newest[:, :1] * LOG2_SCALE).astype(BF)
    added = jnp.dot(weights, values, preferred_element_type=F32)
    if first:
        acc[rows, :] = added
    else:
        acc[rows, :HD] = acc[rows, :HD] * rescale + added[:, :HD]
        acc[rows, HD:] = acc[rows, HD:] * rescale + added[:, HD:]


def attend_kernel(plan, halves, diagonal, final, staged, *refs):
    refs = list(refs)
    take = lambda n: [refs.pop(0) for _ in range(n)]
    (queries,) = take(1)
    begin = take(2)
    pieces = take(len(plan))
    placing = halves is not None
    if placing:
        (table,) = take(1)
        before = [] if diagonal else take(1)
    far_away = take(staged)
    outs = take(1 if final else 2)
    if placing:
        (cache,) = take(1)
    moves = list(zip(far_away, take(staged)))
    if staged:
        stage_sems = refs.pop()
    if placing:
        block_sem = refs.pop()
    if staged:
        (w_out, own), (w_other, other) = moves
        core = lax.rem(lax.axis_index("tp"), 2)
        moves = [pltpu.make_async_copy(w_other, other, stage_sems.at[SIDE])]
        for y in range(SIDE):
            here = pl.ds(pl.multiple_of((2 * y + core) * COLS, COLS), COLS)
            moves.append(pltpu.make_async_copy(w_out.at[:, here], own.at[y], stage_sems.at[y]))
    for move in moves:
        move.start()
    if final:
        keys, values, acc, maxima, sems = refs
    else:
        keys, values, sems = refs
        acc, maxima = outs
    count_rows = queries.shape[0]
    section = lax.axis_index("section")
    x, z = section // SIDE, section % SIDE
    count = jnp.int32(0)
    jobs = []
    for piece, offsets in zip(pieces, plan):
        for j, (dx, dz) in enumerate(offsets):
            source = lax.rem(x + dx, SIDE) * SIDE + lax.rem(z + dz, SIDE)
            needed = source < section
            here = pl.ds(j * HALF, HALF)
            there = pl.ds(pl.multiple_of(count * HALF, HALF), HALF)
            n = len(jobs)
            copies = (
                pltpu.make_async_copy(piece.at[here, :HD], keys.at[there, :], sems.at[n, 0]),
                pltpu.make_async_copy(piece.at[here, HD:], values.at[there, :HD], sems.at[n, 1]),
            )

            @pl.when(needed)
            def _():
                copies[0].start()
                copies[1].start()

            jobs.append((needed, copies))
            count = count + needed.astype(jnp.int32)
    if placing:
        cache[...] = jnp.zeros_like(cache) if diagonal else before[0][...]
        placed = jnp.int32(0)
        sources = [(piece, j * HALF, dx, dz, half)
                   for piece, offsets, half in zip(pieces, plan, halves)
                   for j, (dx, dz) in enumerate(offsets)]
        if diagonal:
            sources += [(begin[0], 0, 0, 0, 0), (begin[1], 0, 0, 0, 1)]
        for piece, row, dx, dz, half in sources:
            source = lax.rem(x + dx, SIDE) * SIDE + lax.rem(z + dz, SIDE)
            for rank in range(PAIR):
                slot = source * PAIR + rank
                inside = table[slot] - half * (HALF // BLOCK)
                found = (inside >= 0) & (inside < HALF // BLOCK)

                @pl.when(found)
                def _():
                    at = pl.ds(pl.multiple_of(row + inside * BLOCK, BLOCK), BLOCK)
                    pltpu.make_async_copy(piece.at[at, :], cache.at[slot], block_sem).start()

                placed = placed + found.astype(jnp.int32)
    values[:, HD:] = jnp.ones((values.shape[0], HD), BF)
    if diagonal:
        last = -(-len(jobs) // 4) * 4 * HALF
        for half in range(2):
            rows = slice(last + half * HALF, last + (half + 1) * HALF)
            keys[rows, :] = begin[half][:, :HD]
            values[rows, :HD] = begin[half][:, HD:]
        for start in range(0, ROWS, TILE):
            shape = (TILE, start + TILE)
            mask = lax.broadcasted_iota(jnp.int32, shape, 1) <= start + lax.broadcasted_iota(jnp.int32, shape, 0)
            kd, vd = keys[last : last + start + TILE, :], values[last : last + start + TILE, :]
            for h in range(HEADS):
                rows = pl.ds((start // SHARE * HEADS + h) * SHARE + start % SHARE, TILE)
                attend(queries[rows, :], kd, vd, acc, maxima, rows, mask, True)
    else:
        acc[...] = begin[0][...]
        maxima[...] = begin[1][...]
    for needed, copies in jobs:
        @pl.when(needed)
        def _():
            copies[0].wait()
            copies[1].wait()

    def part(base, size):
        at = pl.ds(pl.multiple_of(base, HALF), size)
        kd, vd = keys[at, :], values[at, :]
        for start in range(0, count_rows, TILE):
            rows = pl.ds(start, TILE)
            attend(queries[rows, :], kd, vd, acc, maxima, rows)

    def whole(i, _):
        part(i * 4 * HALF, 4 * HALF)
        return 0

    steps = (count + 3) // 4
    for n in range(3):
        @pl.when(count + n < steps * 4)
        def _():
            at = pl.ds(pl.multiple_of((count + n) * HALF, HALF), HALF)
            keys[at, :] = keys[:HALF, :]
            values[at, :] = jnp.zeros((HALF, 2 * HD), BF)

    lax.fori_loop(0, steps, whole, 0)

    if final:
        for h in range(HEADS):
            rows = slice(h * SHARE, (h + 1) * SHARE)
            outs[0][:, h * HD : (h + 1) * HD] = (acc[rows, :HD] / acc[rows, HD:]).astype(BF)
    if placing:
        def block(i, _):
            pltpu.make_async_copy(cache.at[0], cache.at[0], block_sem).wait()
            return 0

        lax.fori_loop(0, placed, block, 0)
    for move in moves:
        move.wait()


def attention(queries, begin, pieces, plan, name, diagonal=False, share=None, table=None, cache=None, halves=None, staged=()):
    subs = sum(len(p) for p in plan)
    final = share is not None
    rows = HEADS * SHARE if final else QROWS
    size = -(-subs // 4) * 4 * HALF + (ROWS if diagonal else 0)
    state_shape = [jax.ShapeDtypeStruct((rows, 2 * HD), F32), jax.ShapeDtypeStruct((rows, HD), F32)]
    scratch = [pltpu.VMEM((size, HD), BF), pltpu.VMEM((size, 2 * HD), BF)]
    if final:
        scratch += [pltpu.VMEM(s.shape, s.dtype) for s in state_shape]
        out_shape = [jax.ShapeDtypeStruct((SHARE, HEADS * HD), BF)]
        at = lambda i: (share, 0)
        in_specs = [pl.BlockSpec((rows, HD), at), pl.BlockSpec((rows, 2 * HD), at), pl.BlockSpec((rows, HD), at)]
        grid = (1,)
        out_specs = [pl.BlockSpec((SHARE, HEADS * HD), lambda i: (0, 0))]
    else:
        out_shape = state_shape
        in_specs = [WHOLE] * 3
        grid = ()
        out_specs = [WHOLE] * 2
    in_specs = in_specs + [ANY] * len(pieces)
    args = [queries, *begin, *pieces]
    scratch.append(pltpu.SemaphoreType.DMA((subs, 2)))
    if table is not None:
        in_specs.append(pl.BlockSpec(memory_space=pltpu.SMEM))
        args.append(table)
        if cache is not None:
            in_specs.append(WHOLE)
            args.append(cache)
        out_shape = out_shape + [jax.ShapeDtypeStruct((SIDE * SIDE * PAIR, BLOCK, 2 * HD), BF)]
        out_specs = out_specs + [WHOLE]
        scratch.append(pltpu.SemaphoreType.DMA)
    if staged:
        in_specs += [ANY] * len(staged)
        args += staged
        out_shape = out_shape + [jax.ShapeDtypeStruct(staged[1].shape, BF)] * 2
        out_specs = out_specs + [WHOLE] * len(staged)
        scratch.append(pltpu.SemaphoreType.DMA((SIDE + 1,)))
    return pl.pallas_call(
        functools.partial(attend_kernel, plan, halves, diagonal, final, len(staged)),
        grid=grid,
        in_specs=in_specs,
        out_specs=out_specs,
        out_shape=out_shape,
        scratch_shapes=scratch,
        compiler_params=limit(20),
        cost_estimate=pl.CostEstimate(
            flops=8 * rows * size * HD, bytes_accessed=8 << 20, transcendentals=rows * size
        ),
        name=name,
    )(*args)


def join_kernel(*refs):
    n = (len(refs) - 2) // 2
    for ins, out in ((refs[:n], refs[-2]), (refs[n : 2 * n], refs[-1])):
        for j, piece in enumerate(ins):
            out[j * HALF : (j + 1) * HALF, :] = piece[...]


def join(first, second):
    out = jax.ShapeDtypeStruct((len(first) * HALF, 2 * HD), BF)
    return pl.pallas_call(
        join_kernel,
        in_specs=[WHOLE] * (len(first) + len(second)),
        out_specs=[WHOLE] * 2,
        out_shape=[out] * 2,
        compiler_params=limit(8),
        cost_estimate=pl.CostEstimate(flops=0, bytes_accessed=2 << 20, transcendentals=0),
        name="join",
    )(*first, *second)


def cache_table(placement, section):
    owners = placement.reshape(SIDE * SIDE, ROWS // BLOCK)
    mine = owners == section
    before = jnp.arange(ROWS // BLOCK)[:, None] < jnp.arange(ROWS // BLOCK)[None, :]
    ranks = jnp.sum((mine[:, :, None] & before[None]).astype(jnp.int32), axis=1)
    hit = mine[:, None, :] & (ranks[:, None, :] == jnp.arange(PAIR)[None, :, None])
    number = jnp.arange(ROWS // BLOCK, dtype=jnp.int32) + 1
    return (jnp.sum(jnp.where(hit, number[None, None, :], 0), axis=-1) - 1).reshape(-1)


MID = SHARE // 2
PROJECT_LIMIT = 14


def term(offset, own, other, w_own, w_other):
    y = lax.rem(lax.axis_index("tp") // 2 + offset, SIDE)
    product = jnp.dot(own[...], w_own[y], preferred_element_type=F32)
    return product + jnp.dot(other[...], w_other[y], preferred_element_type=F32)


def opposite_kernel(own, other, w_own, w_other, top, bottom):
    product = term(2, own, other, w_own, w_other)
    top[...] = product[:MID].astype(BF)
    bottom[...] = product[MID:].astype(BF)


def neighbour_kernel(own, other, w_own, w_other, from_below, from_above, up, down):
    product = term(1, own, other, w_own, w_other)
    up[:MID] = (product[:MID] + from_below[...].astype(F32)).astype(BF)
    up[MID:] = product[MID:].astype(BF)
    product = term(3, own, other, w_own, w_other)
    down[:MID] = product[:MID].astype(BF)
    down[MID:] = (product[MID:] + from_above[...].astype(F32)).astype(BF)


def home_kernel(share, own, other, w_own, w_other, residual, out):
    rows = slice(share * SHARE, (share + 1) * SHARE)
    out[...] = residual[rows, :].astype(F32) + term(0, own, other, w_own, w_other)


def project(kernel, targets, terms, extra, out, name):
    return pl.pallas_call(
        kernel,
        in_specs=[WHOLE] * (len(terms) + len(extra)),
        out_specs=[WHOLE] * len(out),
        out_shape=[jax.ShapeDtypeStruct(shape, dtype) for shape, dtype in out],
        compiler_params=limit(PROJECT_LIMIT),
        cost_estimate=pl.CostEstimate(
            flops=4 * SHARE * 512 * COLS * targets, bytes_accessed=4 << 20, transcendentals=0
        ),
        name=name,
    )(*terms, *extra)


def finish_kernel(base, from_below, from_above, *refs):
    refs[-1][...] = (base[...] + from_below[...].astype(F32) + from_above[...].astype(F32)).astype(BF)


def finish(base, from_below, from_above, done, share):
    return pl.pallas_call(
        finish_kernel,
        grid=(1,),
        in_specs=[WHOLE] * 3 + [ANY] * len(done),
        out_specs=pl.BlockSpec((SHARE, COLS), lambda i: (share, 0)),
        out_shape=jax.ShapeDtypeStruct((ROWS, COLS), BF),
        input_output_aliases={3: 0} if done else {},
        compiler_params=limit(8),
        cost_estimate=pl.CostEstimate(flops=4 * SHARE * COLS, bytes_accessed=3 << 20, transcendentals=0),
        name="finish",
    )(base, from_below, from_above, *done)


def from_section(value, dx, dz):
    pairs = []
    for x in range(SIDE):
        for z in range(SIDE):
            pairs.append((((x + dx) % SIDE) * SIDE + (z + dz) % SIDE, x * SIDE + z))
    return lax.ppermute(value, "section", pairs)


def from_tp(value, dy, dc):
    pairs = []
    for y in range(SIDE):
        for c in range(2):
            pairs.append((((y + dy) % SIDE) * 2 + (c ^ dc), y * 2 + c))
    return lax.ppermute(value, "tp", pairs)


RING = (1, 3, 2)
ORDER = (0,) + RING


def per_device(tokens, gain, q_weight, q_bias, kv_weight, kv_bias, out_weight, placement):
    section = lax.axis_index("section")
    small, large = tables()
    factors, first, second, residual, w_send = norm_kv(
        tokens, gain[None, :], kv_weight, kv_bias[None, :], small, large, out_weight
    )
    w_other = from_tp(w_send, 0, 1)
    row_first = [from_section(first, 0, k) for k in RING]
    row_second = [from_section(second, k, 0) for k in RING]
    factors, row_first[0] = lax.optimization_barrier((factors, row_first[0]))
    queries = query(tokens, factors, gain[None, :], q_weight, q_bias[None, :], small, large)
    row_first[1], w_other, queries = lax.optimization_barrier((row_first[1], w_other, queries))
    all_first, all_second = join([first, *row_first], [second, *row_second])
    far_first = [from_section(all_first, k, 0) for k in RING[:2]]
    far_second = [from_section(all_second, 0, k) for k in RING[:2]]
    near = [[(0, k)] for k in RING] + [[(k, 0)] for k in RING]
    table = cache_table(placement, section)
    *state, cache, w_own, w_other = attention(
        queries,
        (first, second),
        row_first + row_second,
        near,
        "attention_near",
        diagonal=True,
        table=table,
        halves=[0] * 3 + [1] * 3,
        staged=(out_weight, w_other),
    )
    all_first, all_second, *state = lax.optimization_barrier((all_first, all_second, *state))
    far_first.append(from_section(all_first, RING[2], 0))
    far_second.append(from_section(all_second, 0, RING[2]))
    far = [[(k, j) for j in ORDER] for k in RING], [[(j, k) for j in ORDER] for k in RING]
    *state, cache = attention(
        queries,
        state,
        far_first[:2] + far_second[:2],
        far[0][:2] + far[1][:2],
        "attention_far",
        table=table,
        cache=cache,
        halves=[0] * 2 + [1] * 2,
    )
    pieces, plan = far_first[2:] + far_second[2:], far[0][2:] + far[1][2:]
    (early,) = attention(queries, state, pieces, plan, "attention_last", share=0)
    late, cache = attention(
        queries,
        state,
        pieces,
        plan,
        "attention_last",
        share=1,
        table=table,
        cache=cache,
        halves=[0, 1],
    )
    mixed = []
    for share, own in enumerate((early, late)):
        terms = (own, from_tp(own, 0, 1), w_own, w_other)
        top, bottom = project(opposite_kernel, 1, terms, [], [((MID, COLS), BF)] * 2, "project_opposite")
        from_below, from_above = from_tp(top, 3, 0), from_tp(bottom, 1, 0)
        up, down = project(
            neighbour_kernel, 2, terms, [from_below, from_above], [((SHARE, COLS), BF)] * 2, "project_neighbours"
        )
        from_below, from_above = from_tp(up, 3, 0), from_tp(down, 1, 0)
        (base,) = project(
            functools.partial(home_kernel, share), 1, terms, [residual], [((SHARE, COLS), F32)], "project_home"
        )
        mixed = [finish(base, from_below, from_above, mixed, share)]
    return mixed[0], cache


def solution(mesh):
    placed = (
        P("section", None),
        P(),
        P(None, "tp"),
        P("tp"),
        P(None, "tp"),
        P("tp"),
        P("tp", None),
        P(),
    )
    return jax.shard_map(
        per_device,
        mesh=mesh,
        in_specs=placed,
        out_specs=(P("section", "tp"), P("section", None, "tp")),
        check_vma=False,
    )
```
